32 devices in a mesh: blk: 8 (over y, x, core), head: 4 (over z).
Axes of the slice: x: 2, y: 2, z: 4, core: 2. Of those that a mesh axis runs over, the one named last changes fastest.
Arguments:
- tokens: bfloat16 [2, 2048, 2048], P(None, ('blk', 'head')), may hold values from -6 to 6
- cotangent: bfloat16 [2, 2048, 2048], P(None, ('blk', 'head')), may hold values from -6 to 6
- segments: int32 [2, 2048], P(None, ('blk', 'head')), may hold values from 0 to 127, as said below
- padding: int32 [2, 2048], P(None, ('blk', 'head')), may hold values from 0 to 1, as said below
- query_weight: bfloat16 [2048, 2048], P('blk', 'head'), may hold values from -0.125 to 0.125
- key_weight: bfloat16 [2048, 2048], P('blk', 'head'), may hold values from -0.125 to 0.125
- value_weight: bfloat16 [2048, 2048], P('blk', 'head'), may hold values from -0.125 to 0.125
- output_weight: bfloat16 [2048, 2048], P('head', 'blk'), may hold values from -0.125 to 0.125
- query_gain: float32 [2048], P('head'), may hold values from 0.1 to 1.9
- key_gain: float32 [2048], P('head'), may hold values from 0.1 to 1.9
- attn_gain: float32 [2048], replicated, may hold values from 0.1 to 1.9
- gate_weight: bfloat16 [2048, 8192], P('blk', 'head'), may hold values from -0.125 to 0.125
- up_weight: bfloat16 [2048, 8192], P('blk', 'head'), may hold values from -0.125 to 0.125
- down_weight: bfloat16 [8192, 2048], P('head', 'blk'), may hold values from -0.0625 to 0.0625
- ffn_gain: float32 [2048], replicated, may hold values from 0.1 to 1.9
Outputs:
- output: bfloat16 [2, 2048, 2048], P(None, ('blk', 'head'))
- input_grad: float32 [2, 2048, 2048], P(None, ('blk', 'head'))
- query_weight_grad: float32 [2048, 2048], P('blk', 'head')
- key_weight_grad: float32 [2048, 2048], P('blk', 'head')
- value_weight_grad: float32 [2048, 2048], P('blk', 'head')
- output_weight_grad: float32 [2048, 2048], P('head', 'blk')
- query_gain_grad: float32 [2048], P('head')
- key_gain_grad: float32 [2048], P('head')
- attn_gain_grad: float32 [2048], replicated
- gate_weight_grad: float32 [2048, 8192], P('blk', 'head')
- up_weight_grad: float32 [2048, 8192], P('blk', 'head')
- down_weight_grad: float32 [8192, 2048], P('head', 'blk')
- ffn_gain_grad: float32 [2048], replicated
The draws below stay inside these ranges and needn't reach their ends.
Inputs may be any that keep to these rules, and one draw needn't show every extreme that they name: `segments`: along each sequence the ids never fall; a document is a run of equal ids. `padding`: in each sequence a trailing run of 1 to fewer than 512 positions is 0, all others 1.
All inputs are finite; a program needn't handle non-finite values.
Results may differ from the reference program's by a relative error of at most 0.025.
Values may be sent and summed in bfloat16 or wider, within the bound.
No kernel may reach another device: no remote copies, remote signals or barrier semaphores. Data moves between devices by JAX's collectives and lax.ppermute only.
A program may use at most 192 MiB of HBM per device.

```python
import math
import jax
import jax.numpy as jnp
from jax import lax

D = 2048
HEADS = 16
HD = 128
FF = 8192
TOK_SEQ_DEV = 64
MICRO = 2
SEQ = 2048
N_BLK = 8


def draw_segments(key, part):
    key = jax.random.fold_in(key, 7)
    piece_size = max(TOK_SEQ_DEV // 4, 1)
    doc_count = SEQ // piece_size
    pick_key, base_key = jax.random.split(key)
    chosen = jax.random.randint(pick_key, (), 0, MICRO)
    positions = jnp.arange(SEQ, dtype=jnp.int32)

    def one_sequence(batch_index):
        seq_key = jax.random.fold_in(base_key, batch_index)
        power_key, size_key, start_key = jax.random.split(seq_key, 3)
        powers = jax.random.randint(power_key, (doc_count,), 0, 10)
        span_caps = jnp.left_shift(jnp.ones((doc_count,), jnp.int32), powers)
        doc_sizes = piece_size * (1 + jax.random.randint(size_key, (doc_count,), 0, span_caps))
        doc_ends = jnp.cumsum(doc_sizes).astype(jnp.int32)
        doc_ids = jnp.sum((doc_ends[None, :] <= positions[:, None]).astype(jnp.int32), axis=1)
        long_start = jax.random.randint(start_key, (), 1, SEQ // N_BLK)
        long_id = jnp.sum((doc_ends <= long_start - 1).astype(jnp.int32)) + 1
        joined = jnp.where(positions >= long_start, long_id, doc_ids)
        picked = jnp.where(batch_index == chosen, joined, doc_ids).astype(jnp.int32)
        last_id = picked[SEQ - 1]
        return jnp.where(picked == last_id, doc_count - 1, picked).astype(jnp.int32)
    return jax.vmap(one_sequence)(jnp.arange(MICRO, dtype=jnp.int32))


def draw_padding(key, part):
    key = jax.random.fold_in(key, 13)
    trailing = jax.random.randint(key, (MICRO, 1), 1, max(SEQ // 4, 2))
    positions = jnp.arange(SEQ, dtype=jnp.int32)[None, :]
    return (positions < SEQ - trailing).astype(jnp.int32)


def steps_of(key, dims, shards, least, high):
    level = 1.0
    for position, shards_of in shards:
        steps = jax.random.uniform(jax.random.fold_in(jax.random.fold_in(key, 6), position), (shards_of,), jnp.float32, least / len(shards), high / len(shards))
        level = level * jnp.repeat(jnp.exp(steps), dims[position] // shards_of).reshape((-1,) + (1,) * (len(dims) - 1 - position))
    return level


def noise(rng, shape, scale, most, cuts=(), kind=jnp.bfloat16):
    values = jax.random.normal(rng, shape, jnp.float32) * scale
    if len(cuts) > 0:
        values = steps_of(rng, shape, cuts, -0.22, 0.18) * values
    return jnp.clip(values, min=-most, max=most).astype(kind)


def setup_inputs(seed: int = 0) -> dict:
    seeds = jax.random.split(jax.random.key(seed), 16)
    return {
        "tokens": noise(seeds[0], (MICRO, SEQ, D), 1.0, 6.0, ((1, 32),)),
        "cotangent": noise(seeds[1], (MICRO, SEQ, D), 1.0, 6.0, ((1, 32),)),
        "segments": draw_segments(jax.random.fold_in(seeds[15], 71), 0),
        "padding": draw_padding(jax.random.fold_in(seeds[15], 71), 0),
        "query_weight": noise(seeds[4], (D, D), D ** -0.5, 0.125, ((0, 8), (1, 4))),
        "key_weight": noise(seeds[5], (D, D), D ** -0.5, 0.125, ((0, 8), (1, 4))),
        "value_weight": noise(seeds[6], (D, D), D ** -0.5, 0.125, ((0, 8), (1, 4))),
        "output_weight": noise(seeds[7], (D, D), D ** -0.5, 0.125, ((0, 4), (1, 8))),
        "query_gain": jnp.clip(1.0 + 0.18 * jax.random.normal(seeds[8], (D,), jnp.float32), 0.1, 1.9),
        "key_gain": jnp.clip(1.0 + 0.18 * jax.random.normal(seeds[9], (D,), jnp.float32), 0.1, 1.9),
        "attn_gain": jnp.clip(1.0 + 0.18 * jax.random.normal(seeds[10], (D,), jnp.float32), 0.1, 1.9),
        "gate_weight": noise(seeds[11], (D, FF), D ** -0.5, 0.125, ((0, 8), (1, 4))),
        "up_weight": noise(seeds[12], (D, FF), D ** -0.5, 0.125, ((0, 8), (1, 4))),
        "down_weight": noise(seeds[13], (FF, D), FF ** -0.5, 0.0625, ((0, 4), (1, 8))),
        "ffn_gain": jnp.clip(1.0 + 0.18 * jax.random.normal(seeds[14], (D,), jnp.float32), 0.1, 1.9),
    }


@jax.custom_vjp
def low(v):
    return lax.optimization_barrier(v.astype(jnp.bfloat16)).astype(jnp.float32)

@jax.custom_vjp
def low_back(v):
    return v

def low_keep(v):
    return (low(v), None)

def low_pass(kept, grad):
    return (grad,)

def back_keep(v):
    return (v, None)

def back_low(kept, grad):
    return (low(grad),)
low.defvjp(low_keep, low_pass)
low_back.defvjp(back_keep, back_low)
epsilon = 1e-06
theta = 500000.0
highest = lax.Precision.HIGHEST

def matmul(left_side, right_side):
    return jnp.dot(left_side, right_side, precision=highest)

def rms_scale(values):
    return lax.rsqrt(lax.optimization_barrier(jnp.mean(values * values, axis=-1, keepdims=True)) + epsilon)

def rotary_tables():
    half_size = HD // 2
    positions = jnp.arange(SEQ, dtype=jnp.int32).astype(jnp.float32)
    inverse = theta ** (-2.0 * jnp.arange(half_size, dtype=jnp.int32).astype(jnp.float32) / HD)
    angles = positions[:, None] * inverse[None, :]
    angles = jnp.concatenate([angles, angles], axis=1)
    return (jnp.cos(angles)[:, None, :], jnp.sin(angles)[:, None, :])

def rotate(head_rows, cosine, sine_table):
    half_size = head_rows.shape[-1] // 2
    turned = jnp.concatenate([-head_rows[..., half_size:], head_rows[..., :half_size]], axis=-1)
    return head_rows * cosine + turned * sine_table

def attend(queries, key_rows, value_rows, segment_ids, pad_mask):
    score_scale = HD ** (-0.5)
    positions = jnp.arange(SEQ, dtype=jnp.int32)
    block_size = math.gcd(SEQ, 512)
    block_count = SEQ // block_size

    def one_block(block_index):
        offset = (block_index * block_size).astype(jnp.int32)
        query_rows = lax.dynamic_slice_in_dim(queries, offset, block_size, 0)
        query_seg = lax.dynamic_slice_in_dim(segment_ids, offset, block_size, 0)
        query_pos = offset + jnp.arange(block_size, dtype=jnp.int32)
        scores = jnp.einsum('qhd,khd->hqk', query_rows, key_rows, precision=highest) * score_scale
        scores = low_back(scores)
        allowed = (query_seg[:, None] == segment_ids[None, :]) & (positions[None, :] <= query_pos[:, None])
        allowed = allowed & ((pad_mask[None, :] == 1) | (positions[None, :] == query_pos[:, None]))
        scores = jnp.where(allowed[None], scores, -jnp.inf)
        top_score = lax.optimization_barrier(jnp.max(scores, axis=-1, keepdims=True))
        expanded = jnp.exp(scores - top_score)
        prob_rows = low(expanded / lax.optimization_barrier(jnp.sum(expanded, axis=-1, keepdims=True)))
        return jnp.einsum('hqk,khd->qhd', prob_rows, value_rows, precision=highest)
    blocks = lax.map(jax.checkpoint(one_block), jnp.arange(block_count, dtype=jnp.int32))
    return blocks.reshape(SEQ, HEADS, HD)

def block_forward(inputs, query_weight, key_weight, value_weight, output_weight, query_gain, key_gain, attn_gain, gate_weight, up_weight, down_weight, ffn_gain, segment_ids, pad_mask, cosine, sine_table):
    raw_query = low_back(matmul(inputs, query_weight))
    raw_key = low_back(matmul(inputs, key_weight))
    value_rows = low(low_back(matmul(inputs, value_weight)))
    query_norm = raw_query * rms_scale(raw_query) * query_gain
    key_norm = raw_key * rms_scale(raw_key) * key_gain
    query_heads = low(rotate(query_norm.reshape(SEQ, HEADS, HD), cosine, sine_table))
    key_heads = low(rotate(key_norm.reshape(SEQ, HEADS, HD), cosine, sine_table))
    mixed_heads = attend(query_heads, key_heads, value_rows.reshape(SEQ, HEADS, HD), segment_ids, pad_mask)
    mixed_heads = low(low_back(mixed_heads.reshape(SEQ, D)))
    attn_rows = low_back(matmul(mixed_heads, output_weight))
    hidden = inputs + attn_rows * rms_scale(attn_rows) * attn_gain
    hidden_low = low(hidden)
    gate_values = low_back(matmul(hidden_low, gate_weight))
    up_values = low_back(matmul(hidden_low, up_weight))
    middle = low(jax.nn.silu(gate_values) * up_values)
    down_rows = low_back(matmul(middle, down_weight))
    return hidden + down_rows * rms_scale(down_rows) * ffn_gain

def reference(tokens, cotangent, segments, padding, query_weight, key_weight, value_weight, output_weight, query_gain, key_gain, attn_gain, gate_weight, up_weight, down_weight, ffn_gain):
    weights = tuple((weight_item.astype(jnp.float32) for weight_item in (query_weight, key_weight, value_weight, output_weight, query_gain, key_gain, attn_gain, gate_weight, up_weight, down_weight, ffn_gain)))
    cosine, sine_table = rotary_tables()
    outputs = []
    input_grads = []
    totals = [jnp.zeros_like(weight_item) for weight_item in weights]
    for batch_index in range(MICRO):
        segment_ids = segments[batch_index]
        pad_mask = padding[batch_index]

        def forward(inputs, *params):
            return block_forward(inputs, *params, segment_ids, pad_mask, cosine, sine_table)
        result, pullback = jax.vjp(forward, tokens[batch_index].astype(jnp.float32), *weights)
        pieces = pullback(cotangent[batch_index].astype(jnp.float32))
        outputs.append(result.astype(jnp.bfloat16))
        input_grads.append(pieces[0])
        totals = [running + added for running, added in zip(totals, pieces[1:])]
    return (jnp.stack(outputs), jnp.stack(input_grads), totals[0], totals[1], totals[2], totals[3], totals[4], totals[5], totals[6], totals[7], totals[8], totals[9], totals[10])
```

```python
import functools

import jax
import jax.numpy as jnp
from jax import lax
from jax.experimental import pallas as pl
from jax.experimental.pallas import tpu as pltpu
from jax.sharding import PartitionSpec as P

HD = 128

epsilon = 1e-06
theta = 500000.0
score_scale = HD ** (-0.5)
hidden_score = -1e30
low = jnp.bfloat16
full = jnp.float32
vmem_grant = 56 * 1024 * 1024


def dot_plain(left_side, right_side):
    return jnp.dot(left_side, right_side, preferred_element_type=full)


def dot_right_t(left_side, right_side):
    return lax.dot_general(
        left_side, right_side, (((1,), (1,)), ((), ())), preferred_element_type=full
    )


def dot_left_t(left_side, right_side):
    return lax.dot_general(
        left_side, right_side, (((0,), (0,)), ((), ())), preferred_element_type=full
    )


def rms_scale(values):
    return lax.rsqrt(jnp.mean(values * values, axis=-1, keepdims=True) + epsilon)


def xor_pairs(size, mask):
    return [(i, i ^ mask) for i in range(size)]


def gather_slots(values, axis):
    size = lax.axis_size(axis)
    return [values] + [lax.ppermute(values, axis, xor_pairs(size, s)) for s in range(1, size)]


def exchange_slots(slots, axis):
    size = lax.axis_size(axis)
    return [slots[0]] + [
        lax.ppermute(slots[s], axis, xor_pairs(size, s)) for s in range(1, size)
    ]


def gather_rows(values):
    return jnp.concatenate(gather_slots(values, "head"), axis=0)


def reduce_rows(partial_rows):
    size = lax.axis_size("head")
    rows = partial_rows.shape[0] // size
    slots = [partial_rows[s * rows : (s + 1) * rows] for s in range(size)]
    arrived = exchange_slots([slot.astype(low) for slot in slots], "head")
    return sum(slot.astype(full) for slot in arrived)


def sum_heads(values):
    size = lax.axis_size("head")
    total = None
    for s, arrived in enumerate(gather_slots(values, "head")):
        slots = jnp.split(arrived, size, axis=1)
        ordered = jnp.concatenate([slots[t ^ s] for t in range(size)], axis=1)
        total = ordered if total is None else total + ordered
    return total


def rotary_tables(positions):
    half_size = HD // 2
    inverse = theta ** (-2.0 * jnp.arange(half_size, dtype=jnp.int32).astype(full) / HD)
    angles = positions.astype(full)[:, None] * inverse[None, :]
    cosine, sine = jnp.cos(angles), jnp.sin(angles)
    return (
        jnp.concatenate([cosine, cosine], axis=1),
        jnp.concatenate([-sine, sine], axis=1),
    )


def whole(shape):
    return pl.BlockSpec(shape, lambda: (0,) * len(shape))


def call_whole(body, outs, *args, scalars=1, scratch=(), flops=0):
    moved = sum(a.size * a.dtype.itemsize for a in args) + sum(
        o.size * o.dtype.itemsize for o in outs
    )
    return pl.pallas_call(
        body,
        out_shape=outs,
        in_specs=[pl.BlockSpec(memory_space=pltpu.SMEM)] * scalars
        + [pl.BlockSpec(memory_space=pltpu.VMEM)] * (len(args) - scalars),
        out_specs=[pl.BlockSpec(memory_space=pltpu.VMEM)] * len(outs),
        scratch_shapes=list(scratch),
        compiler_params=pltpu.CompilerParams(vmem_limit_bytes=vmem_grant),
        cost_estimate=pl.CostEstimate(flops=flops, bytes_accessed=moved, transcendentals=0),
    )(*args)


def shape_of(shape, dtype):
    return jax.ShapeDtypeStruct(shape, dtype)


def send_views(me, raw, scale, gains, tables, blocks, rows, heads_local):
    micro_count = blocks // heads_local
    width = heads_local * HD

    def body(me_ref, *refs):
        raw_refs = refs[:micro_count]
        scale_ref, gain_ref, cos_ref, sin_ref = refs[micro_count : micro_count + 4]
        out_refs = refs[micro_count + 4 :]
        cosine, sine = cos_ref[...], sin_ref[...]
        for s in range(blocks):
            target = me_ref[0] ^ s
            column = pl.multiple_of((target % heads_local) * HD, HD)

            def piece(micro):
                for part in range(2):
                    values = raw_refs[micro][:, pl.ds(part * width + column, HD)]
                    factor = scale_ref[:, 2 * micro + part : 2 * micro + part + 1]
                    values = values * factor * gain_ref[part : part + 1, pl.ds(column, HD)]
                    turned = values * cosine + pltpu.roll(values, HD // 2, 1) * sine
                    out_refs[s][:, part * HD : (part + 1) * HD] = turned.astype(low)
                out_refs[s][:, 2 * HD :] = raw_refs[micro][
                    :, pl.ds(2 * width + column, HD)
                ].astype(low)

            for micro in range(micro_count):
                pl.when(target // heads_local == micro)(functools.partial(piece, micro))

    return call_whole(
        body,
        [shape_of((rows, 3 * HD), low)] * blocks,
        me,
        *raw,
        scale,
        gains,
        *tables,
    )


def masked_scores(k_rows, q_rows, key_seg, query_seg, key_pos=None, query_pos=None):
    scores = dot_right_t(k_rows, q_rows) * score_scale
    allowed = key_seg == query_seg
    if key_pos is not None:
        allowed = (allowed & (key_pos <= query_pos)) | (key_pos == query_pos)
    return jnp.where(allowed, scores, hidden_score)


def attention_forward(me, slots, key_seg, key_pos, query_seg, query_pos):
    blocks = len(slots)
    rows = slots[0].shape[0]
    length = blocks * rows

    def body(me_ref, *refs):
        slot_refs = refs[:blocks]
        ks_ref, kp_ref, qs_ref, qp_ref = refs[blocks : blocks + 4]
        out_refs = refs[blocks + 4 : 2 * blocks + 4]
        mixed_ref, norm_ref, q_all, k_all, v_all = refs[2 * blocks + 4 :]
        for s in range(blocks):
            place = pl.ds(pl.multiple_of((me_ref[0] ^ s) * rows, rows), rows)
            q_all[place, :] = slot_refs[s][:, :HD]
            k_all[place, :] = slot_refs[s][:, HD : 2 * HD]
            v_all[place, :] = slot_refs[s][:, 2 * HD :]
        for i in range(blocks):
            here = slice(i * rows, (i + 1) * rows)
            q_rows = q_all[here, :]
            query_seg_row = qs_ref[:, here]
            parts = [
                masked_scores(
                    k_all[here, :], q_rows, ks_ref[here, :], query_seg_row, kp_ref[here, :], qp_ref[:, here]
                )
            ]
            spans = [here]
            if i > 0:
                past = slice(0, i * rows)
                parts.append(masked_scores(k_all[past, :], q_rows, ks_ref[past, :], query_seg_row))
                spans.append(past)
            top = functools.reduce(
                jnp.maximum, [jnp.max(part, axis=0, keepdims=True) for part in parts]
            )
            total = jnp.zeros((1, rows), full)
            summed = jnp.zeros((HD, rows), full)
            for part, span in zip(parts, spans):
                expanded = jnp.exp(part - top)
                total = total + jnp.sum(expanded, axis=0, keepdims=True)
                summed = summed + dot_left_t(v_all[span, :], expanded.astype(low))
            mixed_ref[here, :] = jnp.transpose(summed / total)
            norm_ref[:, here] = top + jnp.log(total)
        for s in range(blocks):
            place = pl.ds(pl.multiple_of((me_ref[0] ^ s) * rows, rows), rows)
            out_refs[s][...] = mixed_ref[place, :].astype(low)

    return call_whole(
        body,
        [shape_of((rows, HD), low)] * blocks
        + [shape_of((length, HD), full), shape_of((1, length), full)],
        me,
        *slots,
        key_seg,
        key_pos,
        query_seg,
        query_pos,
        scratch=[pltpu.VMEM((length, HD), low)] * 3,
        flops=2 * length * length * HD,
    )


def attention_backward(me, slots, grad_slots, mixed, norm, key_seg, key_pos, query_seg, query_pos):
    blocks = len(slots)
    rows = slots[0].shape[0]
    length = blocks * rows

    def body(me_ref, *refs):
        slot_refs = refs[:blocks]
        grad_refs = refs[blocks : 2 * blocks]
        mixed_ref, norm_ref, ks_ref, kp_ref, qs_ref, qp_ref = refs[2 * blocks : 2 * blocks + 6]
        out_refs = refs[2 * blocks + 6 : 3 * blocks + 6]
        q_all, k_all, v_all, g_all, dq_all, dk_all, dv_all = refs[3 * blocks + 6 :]
        for s in range(blocks):
            place = pl.ds(pl.multiple_of((me_ref[0] ^ s) * rows, rows), rows)
            q_all[place, :] = slot_refs[s][:, :HD]
            k_all[place, :] = slot_refs[s][:, HD : 2 * HD]
            v_all[place, :] = slot_refs[s][:, 2 * HD :]
            g_all[place, :] = grad_refs[s][...]
        for i in range(blocks):
            here = slice(i * rows, (i + 1) * rows)
            q_rows = q_all[here, :]
            g_rows = g_all[here, :]
            query_seg_row = qs_ref[:, here]
            norm_row = norm_ref[:, here]
            delta = jnp.sum(
                jnp.transpose(g_rows.astype(full) * mixed_ref[here, :]), axis=0, keepdims=True
            )
            spans = [here] + ([slice(0, i * rows)] if i > 0 else [])
            grad_query = jnp.zeros((HD, rows), full)
            for n, span in enumerate(spans):
                k_rows = k_all[span, :]
                if n == 0:
                    scores = masked_scores(
                        k_rows, q_rows, ks_ref[span, :], query_seg_row, kp_ref[span, :], qp_ref[:, here]
                    )
                else:
                    scores = masked_scores(k_rows, q_rows, ks_ref[span, :], query_seg_row)
                weights = jnp.exp(scores - norm_row)
                grad_probs = dot_right_t(v_all[span, :], g_rows)
                grad_scores = (weights * (grad_probs - delta)).astype(low)
                key_term = dot_plain(grad_scores, q_rows)
                value_term = dot_plain(weights.astype(low), g_rows)
                if n == 0:
                    dk_all[span, :] = key_term
                    dv_all[span, :] = value_term
                else:
                    dk_all[span, :] += key_term
                    dv_all[span, :] += value_term
                grad_query = grad_query + dot_left_t(k_rows, grad_scores)
            dq_all[here, :] = jnp.transpose(grad_query)
        for s in range(blocks):
            place = pl.ds(pl.multiple_of((me_ref[0] ^ s) * rows, rows), rows)
            out_refs[s][:, :HD] = (dq_all[place, :] * score_scale).astype(low)
            out_refs[s][:, HD : 2 * HD] = (dk_all[place, :] * score_scale).astype(low)
            out_refs[s][:, 2 * HD :] = dv_all[place, :].astype(low)

    return call_whole(
        body,
        [shape_of((rows, 3 * HD), low)] * blocks,
        me,
        *slots,
        *grad_slots,
        mixed,
        norm,
        key_seg,
        key_pos,
        query_seg,
        query_pos,
        scratch=[pltpu.VMEM((length, HD), low)] * 4 + [pltpu.VMEM((length, HD), full)] * 3,
        flops=5 * length * length * HD,
    )


def assemble_mixed(me, slots, micro_count, heads_local):
    rows = slots[0].shape[0]
    blocks = len(slots)

    def body(me_ref, *refs):
        out_ref = refs[blocks]
        for s in range(blocks):
            source = me_ref[0] ^ s
            column = pl.multiple_of((source % heads_local) * HD, HD)
            out_ref[source // heads_local, :, pl.ds(column, HD)] = refs[s][...]

    return call_whole(
        body, [shape_of((micro_count, rows, heads_local * HD), low)], me, *slots
    )[0]


def split_mixed(me, mixed, blocks, heads_local):
    micro_count, rows = mixed.shape[:2]

    def body(me_ref, mixed_ref, *out_refs):
        for s in range(blocks):
            target = me_ref[0] ^ s
            column = pl.multiple_of((target % heads_local) * HD, HD)
            out_refs[s][...] = mixed_ref[target // heads_local, :, pl.ds(column, HD)]

    return call_whole(body, [shape_of((rows, HD), low)] * blocks, me, mixed)


def receive_grads(me, slots, tables, micro_count, heads_local):
    rows = slots[0].shape[0]
    blocks = len(slots)
    width = heads_local * HD

    def body(me_ref, *refs):
        cos_ref, sin_ref, norm_ref, value_ref = refs[blocks:]
        cosine, sine = cos_ref[...], sin_ref[...]
        for s in range(blocks):
            source = me_ref[0] ^ s
            micro = source // heads_local
            column = pl.multiple_of((source % heads_local) * HD, HD)
            for part in range(2):
                grads = refs[s][:, part * HD : (part + 1) * HD].astype(full)
                turned = grads * cosine - pltpu.roll(grads, HD // 2, 1) * sine
                norm_ref[micro, :, pl.ds(part * width + column, HD)] = turned
            value_ref[micro, :, pl.ds(column, HD)] = refs[s][:, 2 * HD :]

    return call_whole(
        body,
        [
            shape_of((micro_count, rows, 2 * width), full),
            shape_of((micro_count, rows, width), low),
        ],
        me,
        *slots,
        *tables,
    )


def turn(values, tables):
    return values * tables[0][:, None, :] + jnp.roll(values, HD // 2, axis=-1) * tables[1][:, None, :]


def turn_back(grads, tables):
    return grads * tables[0][:, None, :] - jnp.roll(grads, HD // 2, axis=-1) * tables[1][:, None, :]


def block_scores(query_view, key_rows, query_mark, key_mark):
    scores = score_scale * jnp.einsum(
        "qhd,khd->hqk", query_view, key_rows, preferred_element_type=full
    )
    query_seg, query_pos = query_mark
    key_seg, key_pos = key_mark
    allowed = (query_seg[:, None] == key_seg[None, :]) & (key_pos[None, :] <= query_pos[:, None])
    allowed = allowed | (key_pos[None, :] == query_pos[:, None])
    return jnp.where(allowed[None], scores, hidden_score)


def gathered_forward(query_view, query_mark, stacked):
    rows, heads = query_view.shape[:2]

    def step(running, block):
        key_rows, value_rows, key_seg, key_pos = block
        top, total, summed = running
        scores = block_scores(query_view, key_rows, query_mark, (key_seg, key_pos))
        new_top = jnp.maximum(top, jnp.max(scores, axis=-1))
        shrink = jnp.exp(top - new_top)
        expanded = jnp.where(scores > hidden_score, jnp.exp(scores - new_top[..., None]), 0.0)
        new_total = total * shrink + jnp.sum(expanded, axis=-1)
        new_summed = summed * shrink[..., None] + jnp.einsum(
            "hqk,khd->hqd", expanded.astype(low), value_rows, preferred_element_type=full
        )
        return ((new_top, new_total, new_summed), None)

    start = (
        jnp.full((heads, rows), hidden_score, full),
        jnp.zeros((heads, rows), full),
        jnp.zeros((heads, rows, HD), full),
    )
    top, total, summed = lax.scan(step, start, stacked)[0]
    return jnp.swapaxes(summed / total[..., None], 0, 1), top + jnp.log(total)


def gathered_backward(query_view, grad_view, mixed, norm, query_mark, stacked):
    delta = jnp.sum(grad_view.astype(full) * mixed, axis=2).T

    def step(running, block):
        key_rows, value_rows, key_seg, key_pos = block
        scores = block_scores(query_view, key_rows, query_mark, (key_seg, key_pos))
        weights = jnp.exp(scores - norm[..., None])
        grad_probs = jnp.einsum("qhd,khd->hqk", grad_view, value_rows, preferred_element_type=full)
        grad_scores = (weights * (grad_probs - delta[..., None])).astype(low)
        grad_query = running + jnp.einsum(
            "hqk,khd->qhd", grad_scores, key_rows, preferred_element_type=full
        )
        grad_keys = jnp.einsum("hqk,qhd->khd", grad_scores, query_view, preferred_element_type=full)
        grad_values = jnp.einsum(
            "hqk,qhd->khd", weights.astype(low), grad_view, preferred_element_type=full
        )
        return (
            grad_query,
            jnp.concatenate([grad_keys * score_scale, grad_values], axis=1).astype(low),
        )

    grad_query, key_terms = lax.scan(step, jnp.zeros(query_view.shape, full), stacked)
    return grad_query * score_scale, key_terms


class GatheredAttention:
    def __init__(self, raw, scales, gains, tables, codes, blocks, rows, positions):
        self.tables, self.rows = tables, rows
        width = gains.shape[1]
        shape = (rows, width // HD, HD)
        self.sets = []
        for m, values in enumerate(raw):
            views = []
            for part in range(2):
                cut = values[:, part * width : (part + 1) * width]
                normed = cut * scales[:, 2 * m + part : 2 * m + part + 1] * gains[part]
                views.append(turn(normed.reshape(shape), tables).astype(low))
            value_view = values[:, 2 * width :].astype(low).reshape(shape)
            seg_all = (codes[m] // 2).reshape(blocks, rows)
            key_seg = jnp.where(codes[m] % 2 == 1, codes[m] // 2, -1).reshape(blocks, rows)
            place = lax.axis_index("blk")
            mark = tuple(
                lax.dynamic_index_in_dim(mark, place, 0, keepdims=False)
                for mark in (seg_all, positions)
            )
            stacked = (
                lax.all_gather(views[1], "blk"),
                lax.all_gather(value_view, "blk"),
                key_seg,
                positions,
            )
            self.sets.append((views[0], mark, stacked))

    def forward(self):
        results = [gathered_forward(*one) for one in self.sets]
        self.kept = results
        return jnp.stack(
            [mixed.reshape(self.rows, -1).astype(low) for mixed, norm in results]
        )

    def backward(self, grad_mixed):
        norms, values = [], []
        for m, (view, mark, stacked) in enumerate(self.sets):
            grad_query, terms = gathered_backward(
                view, grad_mixed[m].reshape(view.shape), *self.kept[m], mark, stacked
            )
            own = lax.psum_scatter(terms, "blk", scatter_dimension=0, tiled=False)
            heads = view.shape[1]
            both = [turn_back(grad_query, self.tables)]
            both.append(turn_back(own[:, :heads].astype(full), self.tables))
            norms.append(jnp.concatenate([g.reshape(self.rows, -1) for g in both], axis=1))
            values.append(own[:, heads:].reshape(self.rows, -1))
        return jnp.stack(norms), jnp.stack(values)


class ExchangedAttention:
    def __init__(self, raw, scales, gains, tables, codes, blocks, rows, positions):
        self.blocks, self.tables = blocks, tables
        self.heads = gains.shape[1] // HD
        self.micro_count = len(raw)
        place = lax.axis_index("blk")
        self.me = place.astype(jnp.int32).reshape(1)
        self.slots = exchange_slots(
            send_views(self.me, raw, scales, gains, tables, blocks, rows, self.heads), "blk"
        )
        codes = lax.dynamic_index_in_dim(codes, place // self.heads, 0, keepdims=False)
        seg_all = codes // 2
        seg_key = jnp.where(codes % 2 == 1, seg_all, -1)
        pos_all = positions.reshape(-1)
        self.marks = (seg_key[:, None], pos_all[:, None], seg_all[None, :], pos_all[None, :])

    def forward(self):
        results = attention_forward(self.me, self.slots, *self.marks)
        self.kept = results[self.blocks :]
        return assemble_mixed(
            self.me,
            exchange_slots(results[: self.blocks], "blk"),
            self.micro_count,
            self.heads,
        )

    def backward(self, grad_mixed):
        grad_slots = exchange_slots(
            split_mixed(self.me, grad_mixed, self.blocks, self.heads), "blk"
        )
        back_slots = exchange_slots(
            attention_backward(self.me, self.slots, grad_slots, *self.kept, *self.marks), "blk"
        )
        return receive_grads(self.me, back_slots, self.tables, self.micro_count, self.heads)


def on_device(
    tokens,
    cotangent,
    segments,
    padding,
    query_weight,
    key_weight,
    value_weight,
    output_weight,
    query_gain,
    key_gain,
    attn_gain,
    gate_weight,
    up_weight,
    down_weight,
    ffn_gain,
):
    micro_count, local_rows, model_width = tokens.shape
    blocks = lax.axis_size("blk")
    head_size = lax.axis_size("head")
    group_rows = local_rows * head_size
    width = query_weight.shape[1]
    heads_local = width // HD
    hidden_width = gate_weight.shape[1]
    micros = range(micro_count)
    block_index = lax.axis_index("blk")
    head_index = lax.axis_index("head")
    slot_owner = head_index ^ jnp.arange(head_size, dtype=jnp.int32)
    group_order = (
        slot_owner[:, None] * local_rows + jnp.arange(local_rows, dtype=jnp.int32)[None, :]
    ).reshape(group_rows)
    tables = rotary_tables(block_index * group_rows + group_order)

    qkv_full = lax.all_gather(
        jnp.concatenate([query_weight, key_weight, value_weight], axis=1), "blk", axis=0, tiled=True
    )
    output_full_t = lax.all_gather(output_weight.T, "blk", axis=0, tiled=True)
    gate_up_full = lax.all_gather(
        jnp.concatenate([gate_weight, up_weight], axis=1), "blk", axis=0, tiled=True
    )
    down_full_t = lax.all_gather(down_weight.T, "blk", axis=0, tiled=True)

    codes = lax.all_gather(segments * 2 + padding, ("blk", "head"), axis=1, tiled=True)
    token_rows = [gather_rows(tokens[m]) for m in micros]
    raw = [dot_plain(token_rows[m], qkv_full) for m in micros]
    squares = jnp.stack(
        [
            jnp.sum(jnp.square(raw[m][:, part * width : (part + 1) * width]), axis=1)
            for m in micros
            for part in range(2)
        ]
    )
    scale_rows = lax.rsqrt(sum_heads(squares) / model_width + epsilon)
    scales = scale_rows.T
    gains_qk = jnp.stack([query_gain, key_gain])

    codes = codes.reshape(micro_count, blocks, head_size, local_rows)[:, :, slot_owner, :]
    positions = jnp.arange(blocks, dtype=jnp.int32)[:, None] * group_rows + group_order[None, :]
    exchanged = blocks == micro_count * heads_local and blocks & (blocks - 1) == 0
    attention = (ExchangedAttention if exchanged else GatheredAttention)(
        raw,
        scales,
        gains_qk,
        tables,
        codes.reshape(micro_count, -1),
        blocks,
        group_rows,
        positions,
    )
    mixed = attention.forward()

    outputs, hidden_rows_all, middle_all, grad_down_all, grad_gu_all = [], [], [], [], []
    grad_hidden_all, grad_attn_all = [], []
    attn_gain_grad = jnp.zeros((model_width,), full)
    ffn_gain_grad = jnp.zeros((model_width,), full)
    for m in micros:
        attn_rows = reduce_rows(dot_right_t(mixed[m], output_full_t))
        attn_scale = rms_scale(attn_rows)
        attn_hat = attn_rows * attn_scale
        hidden = tokens[m].astype(full) + attn_hat * attn_gain
        hidden_rows = gather_rows(hidden.astype(low))
        gate_up = dot_plain(hidden_rows, gate_up_full)
        gate_values, up_values = gate_up[:, :hidden_width], gate_up[:, hidden_width:]
        sigmoid_gate = jax.nn.sigmoid(gate_values)
        silu_gate = gate_values * sigmoid_gate
        middle = (silu_gate * up_values).astype(low)
        down_rows = reduce_rows(dot_right_t(middle, down_full_t))
        down_scale = rms_scale(down_rows)
        down_hat = down_rows * down_scale
        outputs.append((hidden + down_hat * ffn_gain).astype(low))
        grad_out = cotangent[m].astype(full)
        ffn_gain_grad = ffn_gain_grad + jnp.sum(grad_out * down_hat, axis=0)
        grad_norm = grad_out * ffn_gain
        grad_down = (
            down_scale
            * (grad_norm - down_hat * jnp.mean(grad_norm * down_hat, axis=1, keepdims=True))
        ).astype(low)
        grad_down_rows = gather_rows(grad_down)
        grad_middle = dot_plain(grad_down_rows, down_full_t)
        grad_gu = jnp.concatenate(
            [
                (
                    grad_middle * up_values * sigmoid_gate * (1.0 + gate_values * (1.0 - sigmoid_gate))
                ).astype(low),
                (grad_middle * silu_gate).astype(low),
            ],
            axis=1,
        )
        grad_hidden = reduce_rows(dot_right_t(grad_gu, gate_up_full)) + grad_out
        attn_gain_grad = attn_gain_grad + jnp.sum(grad_hidden * attn_hat, axis=0)
        grad_norm = grad_hidden * attn_gain
        grad_attn = (
            attn_scale
            * (grad_norm - attn_hat * jnp.mean(grad_norm * attn_hat, axis=1, keepdims=True))
        ).astype(low)
        hidden_rows_all.append(hidden_rows)
        middle_all.append(middle)
        grad_down_all.append(grad_down_rows)
        grad_gu_all.append(grad_gu)
        grad_hidden_all.append(grad_hidden)
        grad_attn_all.append(gather_rows(grad_attn))

    def joined(pieces):
        return jnp.concatenate(pieces, axis=0)

    def to_owner(values):
        return lax.psum_scatter(
            values.astype(low), "blk", scatter_dimension=0, tiled=True
        ).astype(full)

    grad_down_both = joined(grad_down_all)
    grad_attn_both = joined(grad_attn_all)
    down_grad = to_owner(dot_left_t(grad_down_both, joined(middle_all))).T
    gate_up_grad = to_owner(dot_left_t(joined(hidden_rows_all), joined(grad_gu_all)))

    grad_mixed = dot_plain(grad_attn_both, output_full_t).astype(low)
    output_grad = to_owner(
        dot_left_t(grad_attn_both, mixed.reshape(micro_count * group_rows, width))
    ).T
    grad_qk_norm, grad_value = attention.backward(
        grad_mixed.reshape(micro_count, group_rows, width)
    )

    gain_row = jnp.concatenate([query_gain, key_gain])
    hats, grad_hats, dots = [], [], []
    qk_gain_grad = jnp.zeros((2 * width,), full)
    for m in micros:
        scale_cols = jnp.concatenate(
            [
                jnp.broadcast_to(scales[:, 2 * m + part : 2 * m + part + 1], (group_rows, width))
                for part in range(2)
            ],
            axis=1,
        )
        hat = raw[m][:, : 2 * width] * scale_cols
        grad_hat = grad_qk_norm[m] * gain_row
        qk_gain_grad = qk_gain_grad + jnp.sum(grad_qk_norm[m] * hat, axis=0)
        for part in range(2):
            cut = slice(part * width, (part + 1) * width)
            dots.append(jnp.sum(grad_hat[:, cut] * hat[:, cut], axis=1))
        hats.append((hat, scale_cols))
        grad_hats.append(grad_hat)
    mean_dots = (sum_heads(jnp.stack(dots)) / model_width).T
    input_grads, grad_qkv_all = [], []
    for m in micros:
        hat, scale_cols = hats[m]
        dot_cols = jnp.concatenate(
            [
                jnp.broadcast_to(mean_dots[:, 2 * m + part : 2 * m + part + 1], (group_rows, width))
                for part in range(2)
            ],
            axis=1,
        )
        grad_raw = (scale_cols * (grad_hats[m] - hat * dot_cols)).astype(low)
        grad_qkv = jnp.concatenate([grad_raw, grad_value[m]], axis=1)
        grad_qkv_all.append(grad_qkv)
        input_grads.append(reduce_rows(dot_right_t(grad_qkv, qkv_full)) + grad_hidden_all[m])
    qkv_grad = to_owner(dot_left_t(joined(token_rows), joined(grad_qkv_all)))

    ffn_gain_grad, attn_gain_grad = lax.psum((ffn_gain_grad, attn_gain_grad), ("blk", "head"))
    qk_gain_grad = lax.psum(qk_gain_grad, "blk")
    return (
        jnp.stack(outputs),
        jnp.stack(input_grads),
        qkv_grad[:, :width],
        qkv_grad[:, width : 2 * width],
        qkv_grad[:, 2 * width :],
        output_grad,
        qk_gain_grad[:width],
        qk_gain_grad[width:],
        attn_gain_grad,
        gate_up_grad[:, :hidden_width],
        gate_up_grad[:, hidden_width:],
        down_grad,
        ffn_gain_grad,
    )


def solution(mesh):
    return jax.shard_map(
        on_device,
        mesh=mesh,
        in_specs=(
            P(None, ("blk", "head"), None),
            P(None, ("blk", "head"), None),
            P(None, ("blk", "head")),
            P(None, ("blk", "head")),
            P("blk", "head"),
            P("blk", "head"),
            P("blk", "head"),
            P("head", "blk"),
            P("head"),
            P("head"),
            P(),
            P("blk", "head"),
            P("blk", "head"),
            P("head", "blk"),
            P(),
        ),
        out_specs=(
            P(None, ("blk", "head"), None),
            P(None, ("blk", "head"), None),
            P("blk", "head"),
            P("blk", "head"),
            P("blk", "head"),
            P("head", "blk"),
            P("head"),
            P("head"),
            P(),
            P("blk", "head"),
            P("blk", "head"),
            P("head", "blk"),
            P(),
        ),
        check_vma=False,
    )
```

```python
import functools

import jax
import jax.numpy as jnp
from jax import lax
from jax.experimental import pallas as pl
from jax.experimental.pallas import tpu as pltpu
from jax.sharding import PartitionSpec as P

HD = 128

epsilon = 1e-06
theta = 500000.0
tile = 256
score_scale = HD ** (-0.5)
hidden_score = -1e30
low = jnp.bfloat16
full = jnp.float32
vmem_grant = 56 * 1024 * 1024


def dot_plain(left_side, right_side):
    return jnp.dot(left_side, right_side, preferred_element_type=full)


def dot_right_t(left_side, right_side):
    return lax.dot_general(
        left_side, right_side, (((1,), (1,)), ((), ())), preferred_element_type=full
    )


def dot_left_t(left_side, right_side):
    return lax.dot_general(
        left_side, right_side, (((0,), (0,)), ((), ())), preferred_element_type=full
    )


def rms_scale(values):
    return lax.rsqrt(jnp.mean(values * values, axis=-1, keepdims=True) + epsilon)


def xor_pairs(size, mask):
    return [(i, i ^ mask) for i in range(size)]


def gather_slots(values, axis):
    size = lax.axis_size(axis)
    return [values] + [lax.ppermute(values, axis, xor_pairs(size, s)) for s in range(1, size)]


def exchange_slots(slots, axis):
    size = lax.axis_size(axis)
    return [slots[0]] + [
        lax.ppermute(slots[s], axis, xor_pairs(size, s)) for s in range(1, size)
    ]


def gather_doubling(values, axis):
    held = values[None]
    step = 1
    while step < lax.axis_size(axis):
        arrived = lax.ppermute(held, axis, xor_pairs(lax.axis_size(axis), step))
        held = jnp.concatenate([held, arrived], axis=0)
        step *= 2
    return held


def sum_doubling(values, axis):
    step = 1
    while step < lax.axis_size(axis):
        values = values + lax.ppermute(values, axis, xor_pairs(lax.axis_size(axis), step))
        step *= 2
    return values


def sum_heads(values):
    size = lax.axis_size("head")
    total = None
    for s, arrived in enumerate(gather_slots(values, "head")):
        slots = jnp.split(arrived, size, axis=1)
        ordered = jnp.concatenate([slots[t ^ s] for t in range(size)], axis=1)
        total = ordered if total is None else total + ordered
    return total


def rotary_tables(positions):
    half_size = HD // 2
    inverse = theta ** (-2.0 * jnp.arange(half_size, dtype=jnp.int32).astype(full) / HD)
    angles = positions.astype(full)[:, None] * inverse[None, :]
    cosine, sine = jnp.cos(angles), jnp.sin(angles)
    return (
        jnp.concatenate([cosine, cosine], axis=1),
        jnp.concatenate([-sine, sine], axis=1),
    )


def shape_of(shape, dtype):
    return jax.ShapeDtypeStruct(shape, dtype)


def sizes_of(arrays):
    return sum(a.size * a.dtype.itemsize for a in arrays)


def call_whole(body, outs, *args, scalars=1, scratch=(), flops=0):
    return pl.pallas_call(
        body,
        out_shape=outs,
        in_specs=[pl.BlockSpec(memory_space=pltpu.SMEM)] * scalars
        + [pl.BlockSpec(memory_space=pltpu.VMEM)] * (len(args) - scalars),
        out_specs=[pl.BlockSpec(memory_space=pltpu.VMEM)] * len(outs),
        scratch_shapes=list(scratch),
        compiler_params=pltpu.CompilerParams(vmem_limit_bytes=vmem_grant),
        cost_estimate=pl.CostEstimate(
            flops=flops, bytes_accessed=sizes_of(args) + sizes_of(outs), transcendentals=0
        ),
    )(*args)


def call_grid(body, steps, outs, in_specs, out_specs, *args, scratch=(), flops=0):
    return pl.pallas_call(
        body,
        grid=(steps,),
        out_shape=outs,
        in_specs=in_specs,
        out_specs=out_specs,
        scratch_shapes=list(scratch),
        compiler_params=pltpu.CompilerParams(vmem_limit_bytes=vmem_grant),
        cost_estimate=pl.CostEstimate(
            flops=flops, bytes_accessed=sizes_of(args) + sizes_of(outs), transcendentals=0
        ),
    )(*args)


def fixed(shape):
    return pl.BlockSpec(shape, lambda i: (0,) * len(shape))


scalar_spec = pl.BlockSpec(memory_space=pltpu.SMEM)


def column_tile(rows, first=0):
    return pl.BlockSpec((rows, tile), lambda i: (0, first + i))


def put_slots(out_refs, values):
    rows = out_refs[0].shape[0]
    for s, ref in enumerate(out_refs):
        ref[...] = values[s * rows : (s + 1) * rows].astype(ref.dtype)


def sum_slots(refs):
    return sum(ref[...].astype(full) for ref in refs)


def ffn_forward(slots, weights):
    n = len(slots)
    local_rows, width = slots[0].shape
    rows, hidden = n * local_rows, weights.shape[1] // 3
    steps = hidden // tile

    def body(*refs):
        wg_ref, wu_ref, wd_ref = refs[n : n + 3]
        rows_ref, gate_ref, up_ref, middle_ref = refs[n + 3 : n + 7]
        out_refs, total = refs[n + 7 : 2 * n + 7], refs[2 * n + 7]
        step = pl.program_id(0)

        @pl.when(step == 0)
        def _():
            for s in range(n):
                rows_ref[s * local_rows : (s + 1) * local_rows, :] = refs[s][...]

        values = rows_ref[...]
        gate = dot_plain(values, wg_ref[...])
        up = dot_plain(values, wu_ref[...])
        gate_ref[...] = gate.astype(low)
        up_ref[...] = up.astype(low)
        middle = (gate * jax.nn.sigmoid(gate) * up).astype(low)
        middle_ref[...] = middle
        term = dot_right_t(middle, wd_ref[...])

        @pl.when(step == 0)
        def _():
            total[...] = term

        @pl.when(step > 0)
        def _():
            total[...] += term

        @pl.when(step == steps - 1)
        def _():
            put_slots(out_refs, total)

    results = call_grid(
        body,
        steps,
        [shape_of((rows, width), low)]
        + [shape_of((rows, hidden), low)] * 3
        + [shape_of((local_rows, width), low)] * n,
        [fixed((local_rows, width))] * n + [column_tile(width, k * steps) for k in range(3)],
        [fixed((rows, width))] + [column_tile(rows)] * 3 + [fixed((local_rows, width))] * n,
        *slots,
        weights,
        weights,
        weights,
        scratch=[pltpu.VMEM((rows, width), full)],
        flops=6 * rows * width * hidden,
    )
    return results[:4], results[4:]


def ffn_backward(slots, gate, up, weights):
    n = len(slots)
    local_rows, width = slots[0].shape
    rows, hidden = gate.shape
    steps = hidden // tile

    def body(*refs):
        gate_ref, up_ref, wg_ref, wu_ref, wd_ref = refs[n : n + 5]
        rows_ref, gg_ref, gu_ref = refs[n + 5 : n + 8]
        out_refs, total = refs[n + 8 : 2 * n + 8], refs[2 * n + 8]
        step = pl.program_id(0)

        @pl.when(step == 0)
        def _():
            for s in range(n):
                rows_ref[s * local_rows : (s + 1) * local_rows, :] = refs[s][...]

        grad_middle = dot_plain(rows_ref[...], wd_ref[...])
        gate_values = gate_ref[...].astype(full)
        sigmoid = jax.nn.sigmoid(gate_values)
        silu = gate_values * sigmoid
        grad_up = (grad_middle * silu).astype(low)
        grad_gate = (
            grad_middle * up_ref[...].astype(full) * (sigmoid + silu * (1.0 - sigmoid))
        ).astype(low)
        gg_ref[...] = grad_gate
        gu_ref[...] = grad_up
        term = dot_right_t(grad_gate, wg_ref[...]) + dot_right_t(grad_up, wu_ref[...])

        @pl.when(step == 0)
        def _():
            total[...] = term

        @pl.when(step > 0)
        def _():
            total[...] += term

        @pl.when(step == steps - 1)
        def _():
            put_slots(out_refs, total)

    results = call_grid(
        body,
        steps,
        [shape_of((rows, width), low)]
        + [shape_of((rows, hidden), low)] * 2
        + [shape_of((local_rows, width), low)] * n,
        [fixed((local_rows, width))] * n
        + [column_tile(rows)] * 2
        + [column_tile(width, k * steps) for k in range(3)],
        [fixed((rows, width))] + [column_tile(rows)] * 2 + [fixed((local_rows, width))] * n,
        *slots,
        gate,
        up,
        weights,
        weights,
        weights,
        scratch=[pltpu.VMEM((rows, width), full)],
        flops=6 * rows * width * hidden,
    )
    return results[:3], results[3:]


def ffn_weight_terms(hidden_rows, grad_rows, grad_gates, grad_ups, middles):
    n = len(hidden_rows)
    rows, width = hidden_rows[0].shape
    hidden = middles[0].shape[1]
    steps = hidden // tile

    def body(*refs):
        hidden_refs, grad_refs = refs[:n], refs[n : 2 * n]
        groups = [refs[(2 + k) * n : (3 + k) * n] for k in range(3)]
        out_ref, hidden_t, grad_t = refs[5 * n :]
        step = pl.program_id(0)

        @pl.when(step == 0)
        def _():
            for m in range(n):
                cut = slice(m * rows, (m + 1) * rows)
                hidden_t[:, cut] = jnp.transpose(hidden_refs[m][...])
                grad_t[:, cut] = jnp.transpose(grad_refs[m][...])

        for k, left in enumerate((hidden_t, hidden_t, grad_t)):

            @pl.when(step // steps == k)
            def _():
                right = jnp.concatenate([ref[...] for ref in groups[k]], axis=0)
                out_ref[...] = dot_plain(left[...], right).astype(low)

    def spec(k):
        return pl.BlockSpec((rows, tile), lambda i: (0, jnp.clip(i - k * steps, 0, steps - 1)))

    return call_grid(
        body,
        3 * steps,
        [shape_of((width, 3 * hidden), low)],
        [fixed((rows, width))] * (2 * n) + [spec(k) for k in range(3) for _ in range(n)],
        [column_tile(width)],
        *hidden_rows,
        *grad_rows,
        *grad_gates,
        *grad_ups,
        *middles,
        scratch=[pltpu.VMEM((width, n * rows), low)] * 2,
        flops=6 * n * rows * width * hidden,
    )[0]


def after_attention(arrived, tokens, gain):
    n = len(arrived)

    def body(*refs):
        token_ref, gain_ref, hidden_ref, low_ref, hat_ref, scale_ref = refs[n:]
        attn = sum_slots(refs[:n])
        scale = rms_scale(attn)
        hat = attn * scale
        hidden = token_ref[...].astype(full) + hat * gain_ref[...]
        hidden_ref[...] = hidden
        low_ref[...] = hidden.astype(low)
        hat_ref[...] = hat
        scale_ref[...] = scale

    shape = tokens.shape
    return call_whole(
        body,
        [shape_of(shape, full), shape_of(shape, low), shape_of(shape, full), shape_of((shape[0], 1), full)],
        *arrived,
        tokens,
        gain,
        scalars=0,
    )


def after_ffn(arrived, hidden, cotangent, gain):
    n = len(arrived)

    def body(*refs):
        hidden_ref, grad_ref, gain_ref, out_ref, low_ref, gain_grad_ref = refs[n:]
        down = sum_slots(refs[:n])
        scale = rms_scale(down)
        hat = down * scale
        out_ref[...] = (hidden_ref[...] + hat * gain_ref[...]).astype(low)
        grad_out = grad_ref[...].astype(full)
        gain_grad_ref[...] = jnp.sum(grad_out * hat, axis=0, keepdims=True)
        grad = grad_out * gain_ref[...]
        low_ref[...] = (scale * (grad - hat * jnp.mean(grad * hat, axis=1, keepdims=True))).astype(low)

    shape = hidden.shape
    return call_whole(
        body,
        [shape_of(shape, low), shape_of(shape, low), shape_of((1, shape[1]), full)],
        *arrived,
        hidden,
        cotangent,
        gain,
        scalars=0,
    )


def before_attention(arrived, cotangent, hat, scale, gain):
    n = len(arrived)

    def body(*refs):
        grad_ref, hat_ref, scale_ref, gain_ref, hidden_ref, low_ref, gain_grad_ref = refs[n:]
        grad_hidden = sum_slots(refs[:n]) + grad_ref[...].astype(full)
        hidden_ref[...] = grad_hidden
        hat = hat_ref[...]
        gain_grad_ref[...] = jnp.sum(grad_hidden * hat, axis=0, keepdims=True)
        grad = grad_hidden * gain_ref[...]
        low_ref[...] = (
            scale_ref[...] * (grad - hat * jnp.mean(grad * hat, axis=1, keepdims=True))
        ).astype(low)

    shape = hat.shape
    return call_whole(
        body,
        [shape_of(shape, full), shape_of(shape, low), shape_of((1, shape[1]), full)],
        *arrived,
        cotangent,
        hat,
        scale,
        gain,
        scalars=0,
    )


def project_qkv(token_slots, weights):
    count = len(token_slots)
    local_rows, width = token_slots[0].shape
    rows, features = count * local_rows, weights.shape[1]
    part = features // 3
    steps = features // tile
    part_steps = part // tile

    def body(*refs):
        weight_ref, rows_ref, raw_ref, square_ref, totals = refs[count:]
        step = pl.program_id(0)

        @pl.when(step == 0)
        def _():
            for s in range(count):
                rows_ref[s * local_rows : (s + 1) * local_rows, :] = refs[s][...]
            totals[...] = jnp.zeros_like(totals)

        raw = dot_plain(rows_ref[...], weight_ref[...])
        raw_ref[...] = raw
        sums = jnp.sum(raw * raw, axis=1, keepdims=True)
        for k in range(2):

            @pl.when(step // part_steps == k)
            def _():
                totals[:, k : k + 1] += sums

        @pl.when(step == steps - 1)
        def _():
            square_ref[...] = jnp.transpose(totals[...])[:2, :]

    return call_grid(
        body,
        steps,
        [shape_of((rows, width), low), shape_of((rows, features), full), shape_of((2, rows), full)],
        [fixed((local_rows, width))] * count + [column_tile(width)],
        [fixed((rows, width)), column_tile(rows), fixed((2, rows))],
        *token_slots,
        weights,
        scratch=[pltpu.VMEM((rows, 128), full)],
        flops=2 * rows * width * features,
    )


def project_output(mixed, weights_t, micro_count, head_size):
    rows = mixed.shape[1]
    width = weights_t.shape[0]
    local_rows = rows // head_size

    def body(mixed_ref, weight_ref, *out_refs):
        for m in range(micro_count):
            values = dot_right_t(mixed_ref[m], weight_ref[...])
            put_slots(out_refs[m * head_size : (m + 1) * head_size], values)

    return call_whole(
        body,
        [shape_of((local_rows, width), low)] * (micro_count * head_size),
        mixed,
        weights_t,
        scalars=0,
        flops=2 * micro_count * rows * width * weights_t.shape[1],
    )


def project_mixed_grad(grad_slots, weights_t):
    count = len(grad_slots)
    local_rows, width = grad_slots[0].shape
    rows, features = count * local_rows, weights_t.shape[1]

    def body(*refs):
        weight_ref, rows_ref, out_ref = refs[count:]
        for s in range(count):
            rows_ref[s * local_rows : (s + 1) * local_rows, :] = refs[s][...]
        out_ref[...] = dot_plain(rows_ref[...], weight_ref[...]).astype(low)

    return call_whole(
        body,
        [shape_of((rows, width), low), shape_of((rows, features), low)],
        *grad_slots,
        weights_t,
        scalars=0,
        flops=2 * rows * width * features,
    )


def norm_gradients(raw, scales, gains, grads):
    rows, features = grads.shape
    width = features // 2

    def body(raw_ref, scale_ref, gain_ref, grad_ref, dot_ref, gain_grad_ref, totals):
        totals[...] = jnp.zeros_like(totals)
        for k in range(2):
            cut = slice(k * width, (k + 1) * width)
            terms = grad_ref[:, cut] * (raw_ref[:, cut] * scale_ref[:, k : k + 1])
            gain_grad_ref[:, cut] = jnp.sum(terms, axis=0, keepdims=True)
            totals[:, k : k + 1] = jnp.sum(terms * gain_ref[:, cut], axis=1, keepdims=True)
        dot_ref[...] = jnp.transpose(totals[...])[:2, :]

    return call_whole(
        body,
        [shape_of((2, rows), full), shape_of((1, features), full)],
        raw,
        scales,
        gains,
        grads,
        scalars=0,
        scratch=[pltpu.VMEM((rows, 128), full)],
    )


def project_input_grad(raw, scales, dots, gains, grads, grad_value, weights, slot_count):
    rows, features = grad_value.shape[0], weights.shape[1]
    width = features // 3
    out_width = weights.shape[0]
    local_rows = rows // slot_count
    steps = out_width // tile

    def body(raw_ref, scale_ref, dot_ref, gain_ref, grad_ref, value_ref, weight_ref, low_ref, *out_refs):
        @pl.when(pl.program_id(0) == 0)
        def _():
            for k in range(2):
                cut = slice(k * width, (k + 1) * width)
                scale = scale_ref[:, k : k + 1]
                hat = raw_ref[:, cut] * scale
                grad_hat = grad_ref[:, cut] * gain_ref[:, cut]
                low_ref[:, cut] = (scale * (grad_hat - hat * dot_ref[:, k : k + 1])).astype(low)
            low_ref[:, 2 * width :] = value_ref[...]

        put_slots(out_refs, dot_right_t(low_ref[...], weight_ref[...]))

    return call_grid(
        body,
        steps,
        [shape_of((rows, features), low)] + [shape_of((local_rows, out_width), low)] * slot_count,
        [
            fixed((rows, 2 * width)),
            fixed((rows, 2)),
            fixed((rows, 2)),
            fixed((1, 2 * width)),
            fixed((rows, 2 * width)),
            fixed((rows, width)),
            pl.BlockSpec((tile, features), lambda i: (i, 0)),
        ],
        [fixed((rows, features))]
        + [pl.BlockSpec((local_rows, tile), lambda i: (0, i))] * slot_count,
        raw,
        scales,
        dots,
        gains,
        grads,
        grad_value,
        weights,
        flops=2 * rows * features * out_width,
    )


def weight_term_slots(me, left, right, blocks):
    rows, width = left.shape
    features = right.shape[1]
    part = width // blocks
    half = blocks // 2

    def body(me_ref, left_ref, right_ref, odd_ref, even_ref, left_t):
        step = pl.program_id(0)

        @pl.when(step == 0)
        def _():
            left_t[...] = jnp.transpose(left_ref[...])

        slot = jnp.where(step < half, 2 * step + 1, 2 * step - blocks)
        place = pl.multiple_of((me_ref[0] ^ slot) * part, part)
        term = dot_plain(left_t[pl.ds(place, part), :], right_ref[...]).astype(low)

        @pl.when(step < half)
        def _():
            odd_ref[0] = term

        @pl.when(step >= half)
        def _():
            even_ref[0] = term

    return call_grid(
        body,
        blocks,
        [shape_of((half, part, features), low)] * 2,
        [scalar_spec, fixed((rows, width)), fixed((rows, features))],
        [
            pl.BlockSpec((1, part, features), lambda i: (jnp.minimum(i, half - 1), 0, 0)),
            pl.BlockSpec((1, part, features), lambda i: (jnp.maximum(i - half, 0), 0, 0)),
        ],
        me,
        left,
        right,
        scratch=[pltpu.VMEM((width, rows), low)],
        flops=2 * rows * width * features,
    )


def to_owner(me, left, right):
    blocks = lax.axis_size("blk")
    odd, even = weight_term_slots(me, left, right, blocks)
    arrived = lax.ppermute(odd, "blk", xor_pairs(blocks, 1))
    pairs = [
        (even[k].astype(full) + arrived[k].astype(full)) for k in range(blocks // 2)
    ]
    return sum(
        [pairs[0]]
        + [
            lax.ppermute(pairs[k].astype(low), "blk", xor_pairs(blocks, 2 * k)).astype(full)
            for k in range(1, blocks // 2)
        ]
    )


def send_views(me, raw, scales, gains, tables, heads_local):
    micro_count, rows = raw.shape[:2]
    blocks = micro_count * heads_local
    width = heads_local * HD

    def body(me_ref, *refs):
        raw_ref, scale_ref, gain_ref, cos_ref, sin_ref = refs[:5]
        out_refs = refs[5:]
        cosine, sine = cos_ref[...], sin_ref[...]
        for s in range(blocks):
            target = me_ref[0] ^ s
            column = pl.multiple_of((target % heads_local) * HD, HD)

            micro = target // heads_local
            for part in range(2):
                feature = pl.multiple_of(part * width + column, HD)
                values = raw_ref[micro, :, pl.ds(feature, HD)]
                values = values * scale_ref[micro, :, part : part + 1]
                values = values * gain_ref[:, pl.ds(feature, HD)]
                turned = values * cosine + pltpu.roll(values, HD // 2, 1) * sine
                out_refs[s][:, part * HD : (part + 1) * HD] = turned.astype(low)
            feature = pl.multiple_of(2 * width + column, HD)
            out_refs[s][:, 2 * HD :] = raw_ref[micro, :, pl.ds(feature, HD)].astype(low)

    return call_whole(
        body,
        [shape_of((rows, 3 * HD), low)] * blocks,
        me,
        raw,
        scales,
        gains,
        *tables,
    )


def masked_scores(k_rows, q_rows, key_seg, query_seg, key_pos=None, query_pos=None):
    scores = dot_right_t(k_rows, q_rows) * score_scale
    allowed = key_seg == query_seg
    if key_pos is not None:
        allowed = (allowed & (key_pos <= query_pos)) | (key_pos == query_pos)
    return jnp.where(allowed, scores, hidden_score)


def attention_forward(me, slots, key_seg, key_pos, query_seg, query_pos):
    blocks = len(slots)
    rows = slots[0].shape[0]
    length = blocks * rows

    def body(me_ref, *refs):
        slot_refs = refs[:blocks]
        ks_ref, kp_ref, qs_ref, qp_ref = refs[blocks : blocks + 4]
        out_refs = refs[blocks + 4 : 2 * blocks + 4]
        mixed_ref, norm_ref, q_all, k_all, v_all = refs[2 * blocks + 4 :]
        for s in range(blocks):
            place = pl.ds(pl.multiple_of((me_ref[0] ^ s) * rows, rows), rows)
            q_all[place, :] = slot_refs[s][:, :HD]
            k_all[place, :] = slot_refs[s][:, HD : 2 * HD]
            v_all[place, :] = slot_refs[s][:, 2 * HD :]
        for i in range(blocks):
            here = slice(i * rows, (i + 1) * rows)
            q_rows = q_all[here, :]
            query_seg_row = qs_ref[:, here]
            parts = [
                masked_scores(
                    k_all[here, :], q_rows, ks_ref[here, :], query_seg_row, kp_ref[here, :], qp_ref[:, here]
                )
            ]
            spans = [here]
            if i > 0:
                past = slice(0, i * rows)
                parts.append(masked_scores(k_all[past, :], q_rows, ks_ref[past, :], query_seg_row))
                spans.append(past)
            top = functools.reduce(
                jnp.maximum, [jnp.max(part, axis=0, keepdims=True) for part in parts]
            )
            total = jnp.zeros((1, rows), full)
            summed = jnp.zeros((HD, rows), full)
            for part, span in zip(parts, spans):
                expanded = jnp.exp(part - top)
                total = total + jnp.sum(expanded, axis=0, keepdims=True)
                summed = summed + dot_left_t(v_all[span, :], expanded.astype(low))
            mixed_ref[here, :] = jnp.transpose(summed / total)
            norm_ref[:, here] = top + jnp.log(total)
        for s in range(blocks):
            place = pl.ds(pl.multiple_of((me_ref[0] ^ s) * rows, rows), rows)
            out_refs[s][...] = mixed_ref[place, :].astype(low)

    return call_whole(
        body,
        [shape_of((rows, HD), low)] * blocks
        + [shape_of((length, HD), full), shape_of((1, length), full)],
        me,
        *slots,
        key_seg,
        key_pos,
        query_seg,
        query_pos,
        scratch=[pltpu.VMEM((length, HD), low)] * 3,
        flops=2 * length * length * HD,
    )


def attention_backward(me, slots, grad_slots, mixed, norm, key_seg, key_pos, query_seg, query_pos):
    blocks = len(slots)
    rows = slots[0].shape[0]
    length = blocks * rows

    def body(me_ref, *refs):
        slot_refs = refs[:blocks]
        grad_refs = refs[blocks : 2 * blocks]
        mixed_ref, norm_ref, ks_ref, kp_ref, qs_ref, qp_ref = refs[2 * blocks : 2 * blocks + 6]
        out_refs = refs[2 * blocks + 6 : 3 * blocks + 6]
        q_all, k_all, v_all, g_all, dq_all, dk_all, dv_all = refs[3 * blocks + 6 :]
        for s in range(blocks):
            place = pl.ds(pl.multiple_of((me_ref[0] ^ s) * rows, rows), rows)
            q_all[place, :] = slot_refs[s][:, :HD]
            k_all[place, :] = slot_refs[s][:, HD : 2 * HD]
            v_all[place, :] = slot_refs[s][:, 2 * HD :]
            g_all[place, :] = grad_refs[s][...]
        for i in range(blocks):
            here = slice(i * rows, (i + 1) * rows)
            q_rows = q_all[here, :]
            g_rows = g_all[here, :]
            query_seg_row = qs_ref[:, here]
            norm_row = norm_ref[:, here]
            delta = jnp.sum(
                jnp.transpose(g_rows.astype(full) * mixed_ref[here, :]), axis=0, keepdims=True
            )
            spans = [here] + ([slice(0, i * rows)] if i > 0 else [])
            grad_query = jnp.zeros((HD, rows), full)
            for n, span in enumerate(spans):
                k_rows = k_all[span, :]
                if n == 0:
                    scores = masked_scores(
                        k_rows, q_rows, ks_ref[span, :], query_seg_row, kp_ref[span, :], qp_ref[:, here]
                    )
                else:
                    scores = masked_scores(k_rows, q_rows, ks_ref[span, :], query_seg_row)
                weights = jnp.exp(scores - norm_row)
                grad_probs = dot_right_t(v_all[span, :], g_rows)
                grad_scores = (weights * (grad_probs - delta)).astype(low)
                key_term = dot_plain(grad_scores, q_rows)
                value_term = dot_plain(weights.astype(low), g_rows)
                if n == 0:
                    dk_all[span, :] = key_term
                    dv_all[span, :] = value_term
                else:
                    dk_all[span, :] += key_term
                    dv_all[span, :] += value_term
                grad_query = grad_query + dot_left_t(k_rows, grad_scores)
            dq_all[here, :] = jnp.transpose(grad_query)
        for s in range(blocks):
            place = pl.ds(pl.multiple_of((me_ref[0] ^ s) * rows, rows), rows)
            out_refs[s][:, :HD] = (dq_all[place, :] * score_scale).astype(low)
            out_refs[s][:, HD : 2 * HD] = (dk_all[place, :] * score_scale).astype(low)
            out_refs[s][:, 2 * HD :] = dv_all[place, :].astype(low)

    return call_whole(
        body,
        [shape_of((rows, 3 * HD), low)] * blocks,
        me,
        *slots,
        *grad_slots,
        mixed,
        norm,
        key_seg,
        key_pos,
        query_seg,
        query_pos,
        scratch=[pltpu.VMEM((length, HD), low)] * 4 + [pltpu.VMEM((length, HD), full)] * 3,
        flops=5 * length * length * HD,
    )


def assemble_mixed(me, slots, micro_count, heads_local):
    rows = slots[0].shape[0]
    blocks = len(slots)

    def body(me_ref, *refs):
        out_ref = refs[blocks]
        for s in range(blocks):
            source = me_ref[0] ^ s
            column = pl.multiple_of((source % heads_local) * HD, HD)
            out_ref[source // heads_local, :, pl.ds(column, HD)] = refs[s][...]

    return call_whole(
        body, [shape_of((micro_count, rows, heads_local * HD), low)], me, *slots
    )[0]


def split_mixed(me, mixed, blocks, heads_local):
    micro_count, rows = mixed.shape[:2]

    def body(me_ref, mixed_ref, *out_refs):
        for s in range(blocks):
            target = me_ref[0] ^ s
            column = pl.multiple_of((target % heads_local) * HD, HD)
            out_refs[s][...] = mixed_ref[target // heads_local, :, pl.ds(column, HD)]

    return call_whole(body, [shape_of((rows, HD), low)] * blocks, me, mixed)


def receive_grads(me, slots, tables, micro_count, heads_local):
    rows = slots[0].shape[0]
    blocks = len(slots)
    width = heads_local * HD

    def body(me_ref, *refs):
        cos_ref, sin_ref, norm_ref, value_ref = refs[blocks:]
        cosine, sine = cos_ref[...], sin_ref[...]
        for s in range(blocks):
            source = me_ref[0] ^ s
            micro = source // heads_local
            column = pl.multiple_of((source % heads_local) * HD, HD)
            for part in range(2):
                grads = refs[s][:, part * HD : (part + 1) * HD].astype(full)
                turned = grads * cosine - pltpu.roll(grads, HD // 2, 1) * sine
                norm_ref[micro, :, pl.ds(part * width + column, HD)] = turned
            value_ref[micro, :, pl.ds(column, HD)] = refs[s][:, 2 * HD :]

    return call_whole(
        body,
        [
            shape_of((micro_count, rows, 2 * width), full),
            shape_of((micro_count, rows, width), low),
        ],
        me,
        *slots,
        *tables,
    )


def turn(values, tables):
    return values * tables[0][:, None, :] + jnp.roll(values, HD // 2, axis=-1) * tables[1][:, None, :]


def turn_back(grads, tables):
    return grads * tables[0][:, None, :] - jnp.roll(grads, HD // 2, axis=-1) * tables[1][:, None, :]


def block_scores(query_view, key_rows, query_mark, key_mark):
    scores = score_scale * jnp.einsum(
        "qhd,khd->hqk", query_view, key_rows, preferred_element_type=full
    )
    query_seg, query_pos = query_mark
    key_seg, key_pos = key_mark
    allowed = (query_seg[:, None] == key_seg[None, :]) & (key_pos[None, :] <= query_pos[:, None])
    allowed = allowed | (key_pos[None, :] == query_pos[:, None])
    return jnp.where(allowed[None], scores, hidden_score)


def gathered_forward(query_view, query_mark, stacked):
    rows, heads = query_view.shape[:2]

    def step(running, block):
        key_rows, value_rows, key_seg, key_pos = block
        top, total, summed = running
        scores = block_scores(query_view, key_rows, query_mark, (key_seg, key_pos))
        new_top = jnp.maximum(top, jnp.max(scores, axis=-1))
        shrink = jnp.exp(top - new_top)
        expanded = jnp.where(scores > hidden_score, jnp.exp(scores - new_top[..., None]), 0.0)
        new_total = total * shrink + jnp.sum(expanded, axis=-1)
        new_summed = summed * shrink[..., None] + jnp.einsum(
            "hqk,khd->hqd", expanded.astype(low), value_rows, preferred_element_type=full
        )
        return ((new_top, new_total, new_summed), None)

    start = (
        jnp.full((heads, rows), hidden_score, full),
        jnp.zeros((heads, rows), full),
        jnp.zeros((heads, rows, HD), full),
    )
    top, total, summed = lax.scan(step, start, stacked)[0]
    return jnp.swapaxes(summed / total[..., None], 0, 1), top + jnp.log(total)


def gathered_backward(query_view, grad_view, mixed, norm, query_mark, stacked):
    delta = jnp.sum(grad_view.astype(full) * mixed, axis=2).T

    def step(running, block):
        key_rows, value_rows, key_seg, key_pos = block
        scores = block_scores(query_view, key_rows, query_mark, (key_seg, key_pos))
        weights = jnp.exp(scores - norm[..., None])
        grad_probs = jnp.einsum("qhd,khd->hqk", grad_view, value_rows, preferred_element_type=full)
        grad_scores = (weights * (grad_probs - delta[..., None])).astype(low)
        grad_query = running + jnp.einsum(
            "hqk,khd->qhd", grad_scores, key_rows, preferred_element_type=full
        )
        grad_keys = jnp.einsum("hqk,qhd->khd", grad_scores, query_view, preferred_element_type=full)
        grad_values = jnp.einsum(
            "hqk,qhd->khd", weights.astype(low), grad_view, preferred_element_type=full
        )
        return (
            grad_query,
            jnp.concatenate([grad_keys * score_scale, grad_values], axis=1).astype(low),
        )

    grad_query, key_terms = lax.scan(step, jnp.zeros(query_view.shape, full), stacked)
    return grad_query * score_scale, key_terms


class GatheredAttention:
    def __init__(self, raw, scales, gains, tables, codes, positions):
        blocks, rows = positions.shape
        self.tables, self.rows = tables, rows
        width = gains.shape[1] // 2
        shape = (rows, width // HD, HD)
        self.sets = []
        for m in range(raw.shape[0]):
            values = raw[m]
            views = []
            for part in range(2):
                cut = values[:, part * width : (part + 1) * width]
                normed = cut * scales[m, :, part : part + 1] * gains[:, part * width : (part + 1) * width]
                views.append(turn(normed.reshape(shape), tables).astype(low))
            value_view = values[:, 2 * width :].astype(low).reshape(shape)
            seg_all = (codes[m] // 2).reshape(blocks, rows)
            key_seg = jnp.where(codes[m] % 2 == 1, codes[m] // 2, -1).reshape(blocks, rows)
            place = lax.axis_index("blk")
            mark = tuple(
                lax.dynamic_index_in_dim(mark, place, 0, keepdims=False)
                for mark in (seg_all, positions)
            )
            stacked = (
                lax.all_gather(views[1], "blk"),
                lax.all_gather(value_view, "blk"),
                key_seg,
                positions,
            )
            self.sets.append((views[0], mark, stacked))

    def forward(self):
        results = [gathered_forward(*one) for one in self.sets]
        self.kept = results
        return jnp.stack(
            [mixed.reshape(self.rows, -1).astype(low) for mixed, norm in results]
        )

    def backward(self, grad_mixed):
        norms, values = [], []
        for m, (view, mark, stacked) in enumerate(self.sets):
            grad_query, terms = gathered_backward(
                view, grad_mixed[m].reshape(view.shape), *self.kept[m], mark, stacked
            )
            own = lax.psum_scatter(terms, "blk", scatter_dimension=0, tiled=False)
            heads = view.shape[1]
            both = [turn_back(grad_query, self.tables)]
            both.append(turn_back(own[:, :heads].astype(full), self.tables))
            norms.append(jnp.concatenate([g.reshape(self.rows, -1) for g in both], axis=1))
            values.append(own[:, heads:].reshape(self.rows, -1))
        return jnp.stack(norms), jnp.stack(values)


class ExchangedAttention:
    def __init__(self, raw, scales, gains, tables, codes, positions):
        self.blocks, self.tables = positions.shape[0], tables
        self.heads = gains.shape[1] // (2 * HD)
        self.micro_count = raw.shape[0]
        place = lax.axis_index("blk")
        self.me = place.astype(jnp.int32).reshape(1)
        self.slots = exchange_slots(
            send_views(self.me, raw, scales, gains, tables, self.heads), "blk"
        )
        codes = lax.dynamic_index_in_dim(codes, place // self.heads, 0, keepdims=False)
        seg_all = codes // 2
        seg_key = jnp.where(codes % 2 == 1, seg_all, -1)
        pos_all = positions.reshape(-1)
        self.marks = (seg_key[:, None], pos_all[:, None], seg_all[None, :], pos_all[None, :])

    def forward(self):
        results = attention_forward(self.me, self.slots, *self.marks)
        self.kept = results[self.blocks :]
        return assemble_mixed(
            self.me,
            exchange_slots(results[: self.blocks], "blk"),
            self.micro_count,
            self.heads,
        )

    def backward(self, grad_mixed):
        grad_slots = exchange_slots(
            split_mixed(self.me, grad_mixed, self.blocks, self.heads), "blk"
        )
        back_slots = exchange_slots(
            attention_backward(self.me, self.slots, grad_slots, *self.kept, *self.marks), "blk"
        )
        return receive_grads(self.me, back_slots, self.tables, self.micro_count, self.heads)


def on_device(
    tokens,
    cotangent,
    segments,
    padding,
    query_weight,
    key_weight,
    value_weight,
    output_weight,
    query_gain,
    key_gain,
    attn_gain,
    gate_weight,
    up_weight,
    down_weight,
    ffn_gain,
):
    micro_count, local_rows, model_width = tokens.shape
    blocks = lax.axis_size("blk")
    head_size = lax.axis_size("head")
    group_rows = local_rows * head_size
    width = query_weight.shape[1]
    heads_local = width // HD
    hidden_width = gate_weight.shape[1]
    micros = range(micro_count)
    block_index = lax.axis_index("blk")
    head_index = lax.axis_index("head")
    me = block_index.astype(jnp.int32).reshape(1)
    slot_owner = head_index ^ jnp.arange(head_size, dtype=jnp.int32)
    group_order = (
        slot_owner[:, None] * local_rows + jnp.arange(local_rows, dtype=jnp.int32)[None, :]
    ).reshape(group_rows)
    tables = rotary_tables(block_index * group_rows + group_order)

    def gather_weights(*parts):
        return lax.all_gather(jnp.concatenate(parts, axis=1), "blk", axis=0, tiled=True)

    qkv_full = gather_weights(query_weight, key_weight, value_weight)
    output_full_t = gather_weights(output_weight.T)
    ffn_full = gather_weights(gate_weight, up_weight, down_weight.T)

    codes = jnp.concatenate(gather_slots(segments * 2 + padding, "head"), axis=1)
    codes = gather_doubling(codes, "blk")
    codes = codes[block_index ^ jnp.arange(blocks, dtype=jnp.int32)].swapaxes(0, 1)

    token_slots = [slot for m in micros for slot in gather_slots(tokens[m], "head")]
    token_rows, raw, squares = project_qkv(token_slots, qkv_full)

    def by_micro(values):
        return values.reshape(micro_count, group_rows, -1)

    def sum_token_heads(values):
        values = values.reshape(2 * micro_count, group_rows)
        return sum_heads(values).reshape(2, micro_count * group_rows).T

    scales = lax.rsqrt(sum_token_heads(squares) / model_width + epsilon)
    gain_row = jnp.concatenate([query_gain, key_gain])[None, :]
    positions = jnp.arange(blocks, dtype=jnp.int32)[:, None] * group_rows + group_order[None, :]
    exchanged = blocks == micro_count * heads_local and blocks & (blocks - 1) == 0
    attention = (ExchangedAttention if exchanged else GatheredAttention)(
        by_micro(raw), by_micro(scales), gain_row, tables, codes.reshape(micro_count, -1), positions
    )
    mixed = attention.forward()

    attn_slots = project_output(mixed, output_full_t, micro_count, head_size)
    attn_gain, ffn_gain = attn_gain[None, :], ffn_gain[None, :]
    outputs, kept = [], []
    grad_hiddens, grad_attn_slots = [], []
    gain_grads = []
    for m in micros:
        arrived = exchange_slots(attn_slots[m * head_size : (m + 1) * head_size], "head")
        hidden, hidden_low, attn_hat, attn_scale = after_attention(arrived, tokens[m], attn_gain)
        (hidden_rows, gate, up, middle), slots = ffn_forward(
            gather_slots(hidden_low, "head"), ffn_full
        )
        output, grad_down, ffn_gain_grad = after_ffn(
            exchange_slots(slots, "head"), hidden, cotangent[m], ffn_gain
        )
        outputs.append(output)
        (grad_rows, grad_gate, grad_up), slots = ffn_backward(
            gather_slots(grad_down, "head"), gate, up, ffn_full
        )
        kept.append((hidden_rows, grad_rows, grad_gate, grad_up, middle))
        grad_hidden, grad_attn, attn_gain_grad = before_attention(
            exchange_slots(slots, "head"), cotangent[m], attn_hat, attn_scale, attn_gain
        )
        grad_hiddens.append(grad_hidden)
        grad_attn_slots += gather_slots(grad_attn, "head")
        gain_grads.append(jnp.concatenate([attn_gain_grad, ffn_gain_grad], axis=1))

    ffn_terms = ffn_weight_terms(*zip(*kept))
    ffn_grad = lax.psum_scatter(ffn_terms, "blk", scatter_dimension=0, tiled=True).astype(full)
    gate_grad, up_grad, down_grad_t = jnp.split(ffn_grad, 3, axis=1)

    grad_attn_rows, grad_mixed = project_mixed_grad(grad_attn_slots, output_full_t)
    output_grad = to_owner(me, grad_attn_rows, mixed.reshape(-1, width)).T
    grad_norm, grad_value = attention.backward(by_micro(grad_mixed))
    grad_norm = grad_norm.reshape(-1, 2 * width)
    grad_value = grad_value.reshape(-1, width)
    dots, qk_gain_grad = norm_gradients(raw, scales, gain_row, grad_norm)
    mean_dots = sum_token_heads(dots) / model_width
    results = project_input_grad(
        raw, scales, mean_dots, gain_row, grad_norm, grad_value, qkv_full, micro_count * head_size
    )
    qkv_grad = to_owner(me, token_rows, results[0])
    input_grads = [
        sum(
            slot.astype(full)
            for slot in exchange_slots(
                results[1 + m * head_size : 1 + (m + 1) * head_size], "head"
            )
        )
        + grad_hiddens[m]
        for m in micros
    ]

    rows_grad = sum_doubling(jnp.concatenate([sum(gain_grads), qk_gain_grad], axis=1)[0], "blk")
    qk_gain_grad = rows_grad[2 * model_width :]
    rows_grad = sum_doubling(rows_grad[: 2 * model_width], "head")
    return (
        jnp.stack(outputs),
        jnp.stack(input_grads),
        qkv_grad[:, :width],
        qkv_grad[:, width : 2 * width],
        qkv_grad[:, 2 * width :],
        output_grad,
        qk_gain_grad[:width],
        qk_gain_grad[width:],
        rows_grad[:model_width],
        gate_grad,
        up_grad,
        down_grad_t.T,
        rows_grad[model_width:],
    )


def solution(mesh):
    return jax.shard_map(
        on_device,
        mesh=mesh,
        in_specs=(
            P(None, ("blk", "head"), None),
            P(None, ("blk", "head"), None),
            P(None, ("blk", "head")),
            P(None, ("blk", "head")),
            P("blk", "head"),
            P("blk", "head"),
            P("blk", "head"),
            P("head", "blk"),
            P("head"),
            P("head"),
            P(),
            P("blk", "head"),
            P("blk", "head"),
            P("head", "blk"),
            P(),
        ),
        out_specs=(
            P(None, ("blk", "head"), None),
            P(None, ("blk", "head"), None),
            P("blk", "head"),
            P("blk", "head"),
            P("blk", "head"),
            P("head", "blk"),
            P("head"),
            P("head"),
            P(),
            P("blk", "head"),
            P("blk", "head"),
            P("head", "blk"),
            P(),
        ),
        check_vma=False,
    )
```

```python
import functools
import math

import jax
import jax.numpy as jnp
from jax import lax
from jax.experimental import pallas as pl
from jax.experimental.pallas import tpu as pltpu
from jax.sharding import PartitionSpec as P

HD = 128

epsilon = 1e-06
theta = 500000.0
widest = 512
score_scale = HD ** (-0.5)
hidden_score = -1e30
low = jnp.bfloat16
full = jnp.float32
vmem_grant = 56 * 1024 * 1024


def dot_plain(left_side, right_side):
    return jnp.dot(left_side, right_side, preferred_element_type=full)


def dot_right_t(left_side, right_side):
    return lax.dot_general(
        left_side, right_side, (((1,), (1,)), ((), ())), preferred_element_type=full
    )


def dot_left_t(left_side, right_side):
    return lax.dot_general(
        left_side, right_side, (((0,), (0,)), ((), ())), preferred_element_type=full
    )


def rms_scale(values):
    return lax.rsqrt(jnp.mean(values * values, axis=-1, keepdims=True) + epsilon)


def xor_pairs(size, mask):
    return [(i, i ^ mask) for i in range(size)]


def gather_slots(values, axis):
    size = lax.axis_size(axis)
    return [values] + [lax.ppermute(values, axis, xor_pairs(size, s)) for s in range(1, size)]


def exchange_slots(slots, axis):
    size = lax.axis_size(axis)
    return [slots[0]] + [
        lax.ppermute(slots[s], axis, xor_pairs(size, s)) for s in range(1, size)
    ]


def gather_doubling(values, axis):
    held = values[None]
    step = 1
    while step < lax.axis_size(axis):
        arrived = lax.ppermute(held, axis, xor_pairs(lax.axis_size(axis), step))
        held = jnp.concatenate([held, arrived], axis=0)
        step *= 2
    return held


def sum_doubling(values, axis):
    step = 1
    while step < lax.axis_size(axis):
        values = values + lax.ppermute(values, axis, xor_pairs(lax.axis_size(axis), step))
        step *= 2
    return values


def after(values, *others):
    return lax.optimization_barrier((values, others))[0]


inward = [(0, 1), (3, 2)]
outward = [(1, 0), (2, 3)]
middle = [(1, 2), (2, 1)]


def send_rows(values, pairs):
    return lax.ppermute(values, "head", pairs)


def gather_parts(values):
    if lax.axis_size("head") != 4:
        return gather_slots(values, "head")
    second = send_rows(values, xor_pairs(4, 2))
    first = send_rows(values, xor_pairs(4, 1))
    across = send_rows(values, middle)
    return [values, first, second, across, send_rows(second, outward)]


def layout_of(count):
    return [(0,), (1,), (2,), (3, 4)] if count == 5 else [(s,) for s in range(count)]


def reduce_parts(slots):
    if lax.axis_size("head") != 4:
        return exchange_slots(slots, "head")
    arrived = send_rows(slots[3], inward)
    first = send_rows(slots[1], xor_pairs(4, 1))
    across = send_rows(slots[3], middle)
    passed = (slots[2].astype(full) + arrived.astype(full)).astype(low)
    return [slots[0], first, across, send_rows(passed, xor_pairs(4, 2))]


def exchange_chips(slots):
    size = lax.axis_size("blk")
    return [slots[0]] + [
        lax.ppermute(slots[m], "blk", xor_pairs(size, 2 * m)) for m in range(1, size // 2)
    ]


def swap_cores(values):
    return lax.ppermute(values, "blk", xor_pairs(lax.axis_size("blk"), 1))


def sum_full(arrays):
    return sum(array.astype(full) for array in arrays)


def sum_heads(values):
    size = lax.axis_size("head")
    total = None
    for s, arrived in enumerate(gather_slots(values, "head")):
        slots = jnp.split(arrived, size, axis=1)
        ordered = jnp.concatenate([slots[t ^ s] for t in range(size)], axis=1)
        total = ordered if total is None else total + ordered
    return total


def rotary_tables(positions):
    half_size = HD // 2
    inverse = theta ** (-2.0 * jnp.arange(half_size, dtype=jnp.int32).astype(full) / HD)
    angles = positions.astype(full)[:, None] * inverse[None, :]
    cosine, sine = jnp.cos(angles), jnp.sin(angles)
    return (
        jnp.concatenate([cosine, cosine], axis=1),
        jnp.concatenate([-sine, sine], axis=1),
    )


def shape_of(shape, dtype):
    return jax.ShapeDtypeStruct(shape, dtype)


def sizes_of(arrays):
    return sum(a.size * a.dtype.itemsize for a in arrays)


def call_whole(body, outs, *args, scalars=1, scratch=(), flops=0):
    return pl.pallas_call(
        body,
        out_shape=outs,
        in_specs=[pl.BlockSpec(memory_space=pltpu.SMEM)] * scalars
        + [pl.BlockSpec(memory_space=pltpu.VMEM)] * (len(args) - scalars),
        out_specs=[pl.BlockSpec(memory_space=pltpu.VMEM)] * len(outs),
        scratch_shapes=list(scratch),
        compiler_params=pltpu.CompilerParams(vmem_limit_bytes=vmem_grant),
        cost_estimate=pl.CostEstimate(
            flops=flops,
            bytes_accessed=sizes_of(args) + sizes_of(outs),
            transcendentals=0,
        ),
    )(*args)


def call_grid(body, steps, outs, in_specs, out_specs, *args, scratch=(), flops=0):
    return pl.pallas_call(
        body,
        grid=(steps,),
        out_shape=outs,
        in_specs=in_specs,
        out_specs=out_specs,
        scratch_shapes=list(scratch),
        compiler_params=pltpu.CompilerParams(vmem_limit_bytes=vmem_grant),
        cost_estimate=pl.CostEstimate(
            flops=flops, bytes_accessed=sizes_of(args) + sizes_of(outs), transcendentals=0
        ),
    )(*args)


def fixed(shape):
    return pl.BlockSpec(shape, lambda i: (0,) * len(shape))


scalar_spec = pl.BlockSpec(memory_space=pltpu.SMEM)


def tile_of(size):
    return math.gcd(size, widest)


def column_tile(rows, tile, first=0):
    return pl.BlockSpec((rows, tile), lambda i: (0, first + i))


def slot_cuts(micro_count, count, rows):
    for s in range(count):
        for m in range(micro_count):
            first = (m * count + s) * rows
            yield s, slice(m * rows, (m + 1) * rows), slice(first, first + rows)


def put_slots(out_refs, values, micro_count):
    rows = out_refs[0].shape[0] // micro_count
    for s, inner, outer in slot_cuts(micro_count, len(out_refs), rows):
        out_refs[s][inner, :] = values[outer].astype(out_refs[s].dtype)


def fill_rows(rows_ref, part_refs, micro_count):
    layout = layout_of(len(part_refs))
    rows = part_refs[0].shape[0] // micro_count
    for s, inner, outer in slot_cuts(micro_count, len(layout), rows):
        rows_ref[outer, :] = functools.reduce(
            jnp.add, [part_refs[part][inner, :] for part in layout[s]]
        )


def sum_slots(refs):
    return sum(ref[...].astype(full) for ref in refs)


def ffn_forward(slots, weights, micro_count):
    n = len(slots)
    local_rows, width = slots[0].shape
    count = len(layout_of(n))
    rows, hidden = count * local_rows, weights.shape[1] // 3
    tile = tile_of(hidden)
    steps = hidden // tile

    def body(*refs):
        wg_ref, wu_ref, wd_ref = refs[n : n + 3]
        rows_ref, gate_ref, up_ref, middle_ref = refs[n + 3 : n + 7]
        out_refs, total = refs[n + 7 : -1], refs[-1]
        step = pl.program_id(0)

        @pl.when(step == 0)
        def _():
            fill_rows(rows_ref, refs[:n], micro_count)

        values = rows_ref[...]
        gate = dot_plain(values, wg_ref[...])
        up = dot_plain(values, wu_ref[...])
        gate_ref[...] = gate.astype(low)
        up_ref[...] = up.astype(low)
        middle = (gate * jax.nn.sigmoid(gate) * up).astype(low)
        middle_ref[...] = middle
        term = dot_right_t(middle, wd_ref[...])

        @pl.when(step == 0)
        def _():
            total[...] = term

        @pl.when(step > 0)
        def _():
            total[...] += term

        @pl.when(step == steps - 1)
        def _():
            put_slots(out_refs, total[...], micro_count)

    results = call_grid(
        body,
        steps,
        [shape_of((rows, width), low)]
        + [shape_of((rows, hidden), low)] * 3
        + [shape_of((local_rows, width), low)] * count,
        [fixed((local_rows, width))] * n + [column_tile(width, tile, k * steps) for k in range(3)],
        [fixed((rows, width))] + [column_tile(rows, tile)] * 3 + [fixed((local_rows, width))] * count,
        *slots,
        weights,
        weights,
        weights,
        scratch=[pltpu.VMEM((rows, width), full)],
        flops=6 * rows * width * hidden,
    )
    return results[:4], results[4:]


def ffn_backward(slots, gate, up, weights, micro_count):
    n = len(slots)
    local_rows, width = slots[0].shape
    rows, hidden = gate.shape
    count = rows // local_rows
    tile = tile_of(hidden)
    steps = hidden // tile

    def body(*refs):
        gate_ref, up_ref, wg_ref, wu_ref, wd_ref = refs[n : n + 5]
        rows_ref, gg_ref, gu_ref = refs[n + 5 : n + 8]
        out_refs, total = refs[n + 8 : -1], refs[-1]
        step = pl.program_id(0)

        @pl.when(step == 0)
        def _():
            fill_rows(rows_ref, refs[:n], micro_count)

        grad_middle = dot_plain(rows_ref[...], wd_ref[...])
        gate_values = gate_ref[...].astype(full)
        sigmoid = jax.nn.sigmoid(gate_values)
        silu = gate_values * sigmoid
        grad_up = (grad_middle * silu).astype(low)
        grad_gate = (
            grad_middle * up_ref[...].astype(full) * (sigmoid + silu * (1.0 - sigmoid))
        ).astype(low)
        gg_ref[...] = grad_gate
        gu_ref[...] = grad_up
        term = dot_right_t(grad_gate, wg_ref[...]) + dot_right_t(grad_up, wu_ref[...])

        @pl.when(step == 0)
        def _():
            total[...] = term

        @pl.when(step > 0)
        def _():
            total[...] += term

        @pl.when(step == steps - 1)
        def _():
            put_slots(out_refs, total[...], micro_count)

    results = call_grid(
        body,
        steps,
        [shape_of((rows, width), low)]
        + [shape_of((rows, hidden), low)] * 2
        + [shape_of((local_rows, width), low)] * count,
        [fixed((local_rows, width))] * n
        + [column_tile(rows, tile)] * 2
        + [column_tile(width, tile, k * steps) for k in range(3)],
        [fixed((rows, width))] + [column_tile(rows, tile)] * 2 + [fixed((local_rows, width))] * count,
        *slots,
        gate,
        up,
        weights,
        weights,
        weights,
        scratch=[pltpu.VMEM((rows, width), full)],
        flops=6 * rows * width * hidden,
    )
    return results[:3], results[3:]


def ffn_weight_term(held, part, lefts, rights):
    n = len(lefts)
    rows, width = lefts[0].shape
    hidden = rights[0].shape[1]
    tile = tile_of(hidden)
    steps = hidden // tile

    def body(*refs):
        out_ref, left_t = refs[-2:]

        @pl.when(pl.program_id(0) == 0)
        def _():
            for m in range(n):
                left_t[:, m * rows : (m + 1) * rows] = jnp.transpose(refs[m][...])

        right = jnp.concatenate([ref[...] for ref in refs[n : 2 * n]], axis=0)
        out_ref[...] = dot_plain(left_t[...], right).astype(low)

    shape = shape_of((width, 3 * hidden), low)
    return pl.pallas_call(
        body,
        grid=(steps,),
        out_shape=shape,
        in_specs=[fixed((rows, width))] * n
        + [column_tile(rows, tile)] * n
        + [pl.BlockSpec(memory_space=pl.ANY)] * len(held),
        out_specs=column_tile(width, tile, part * steps),
        scratch_shapes=[pltpu.VMEM((width, n * rows), low)],
        input_output_aliases={2 * n: 0} if held else {},
        compiler_params=pltpu.CompilerParams(vmem_limit_bytes=vmem_grant),
        cost_estimate=pl.CostEstimate(
            flops=2 * n * rows * width * hidden,
            bytes_accessed=sizes_of(lefts) + width * hidden * 2,
            transcendentals=0,
        ),
    )(*lefts, *rights, *held)


def widen_ffn(grads):
    rows, hidden = grads.shape[0], grads.shape[1] // 3

    def body(grad_ref, gate_ref, up_ref, down_ref):
        gate_ref[...] = grad_ref[:, :hidden].astype(full)
        up_ref[...] = grad_ref[:, hidden : 2 * hidden].astype(full)
        down_ref[...] = jnp.transpose(grad_ref[:, 2 * hidden :]).astype(full)

    return call_whole(
        body,
        [shape_of((rows, hidden), full)] * 2 + [shape_of((hidden, rows), full)],
        grads,
        scalars=0,
    )


def after_attention(arrived, tokens, gain):
    n = len(arrived)

    def body(*refs):
        token_ref, gain_ref, hidden_ref, low_ref, hat_ref, scale_ref = refs[n:]
        attn = sum_slots(refs[:n])
        scale = rms_scale(attn)
        hat = attn * scale
        hidden = token_ref[...].astype(full) + hat * gain_ref[...]
        hidden_ref[...] = hidden
        low_ref[...] = hidden.astype(low)
        hat_ref[...] = hat
        scale_ref[...] = scale

    shape = tokens.shape
    return call_whole(
        body,
        [shape_of(shape, full), shape_of(shape, low), shape_of(shape, full), shape_of((shape[0], 1), full)],
        *arrived,
        tokens,
        gain,
        scalars=0,
    )


def after_ffn(arrived, hidden, cotangent, gain):
    n = len(arrived)

    def body(*refs):
        hidden_ref, grad_ref, gain_ref, out_ref, low_ref, gain_grad_ref = refs[n:]
        down = sum_slots(refs[:n])
        scale = rms_scale(down)
        hat = down * scale
        out_ref[...] = (hidden_ref[...] + hat * gain_ref[...]).astype(low)
        grad_out = grad_ref[...].astype(full)
        gain_grad_ref[...] = jnp.sum(grad_out * hat, axis=0, keepdims=True)
        grad = grad_out * gain_ref[...]
        low_ref[...] = (scale * (grad - hat * jnp.mean(grad * hat, axis=1, keepdims=True))).astype(low)

    shape = hidden.shape
    return call_whole(
        body,
        [shape_of(shape, low), shape_of(shape, low), shape_of((1, shape[1]), full)],
        *arrived,
        hidden,
        cotangent,
        gain,
        scalars=0,
    )


def before_attention(arrived, cotangent, hat, scale, gain):
    n = len(arrived)

    def body(*refs):
        grad_ref, hat_ref, scale_ref, gain_ref, hidden_ref, low_ref, gain_grad_ref = refs[n:]
        grad_hidden = sum_slots(refs[:n]) + grad_ref[...].astype(full)
        hidden_ref[...] = grad_hidden
        hat = hat_ref[...]
        gain_grad_ref[...] = jnp.sum(grad_hidden * hat, axis=0, keepdims=True)
        grad = grad_hidden * gain_ref[...]
        low_ref[...] = (
            scale_ref[...] * (grad - hat * jnp.mean(grad * hat, axis=1, keepdims=True))
        ).astype(low)

    shape = hat.shape
    return call_whole(
        body,
        [shape_of(shape, full), shape_of(shape, low), shape_of((1, shape[1]), full)],
        *arrived,
        cotangent,
        hat,
        scale,
        gain,
        scalars=0,
    )


def project_qkv(token_slots, weights, micro_count):
    count = len(token_slots)
    local_rows, width = token_slots[0].shape
    rows, features = len(layout_of(count)) * local_rows, weights.shape[1]
    part = features // 3
    tile = tile_of(part)
    steps = features // tile
    part_steps = part // tile

    def body(*refs):
        weight_ref, rows_ref, raw_ref, square_ref, totals = refs[count:]
        step = pl.program_id(0)

        @pl.when(step == 0)
        def _():
            fill_rows(rows_ref, refs[:count], micro_count)
            totals[...] = jnp.zeros_like(totals)

        raw = dot_plain(rows_ref[...], weight_ref[...])
        raw_ref[...] = raw
        sums = jnp.sum(raw * raw, axis=1, keepdims=True)
        for k in range(2):

            @pl.when(step // part_steps == k)
            def _():
                totals[:, k : k + 1] += sums

        @pl.when(step == steps - 1)
        def _():
            square_ref[...] = jnp.transpose(totals[...])[:2, :]

    return call_grid(
        body,
        steps,
        [shape_of((rows, width), low), shape_of((rows, features), full), shape_of((2, rows), full)],
        [fixed((local_rows, width))] * count + [column_tile(width, tile)],
        [fixed((rows, width)), column_tile(rows, tile), fixed((2, rows))],
        *token_slots,
        weights,
        scratch=[pltpu.VMEM((rows, 128), full)],
        flops=2 * rows * width * features,
    )


def project_output(mixed, weights_t, head_size):
    micro_count, rows, features = mixed.shape
    width = weights_t.shape[0]
    local_rows = micro_count * rows // head_size

    def body(mixed_ref, weight_ref, *out_refs):
        values = dot_right_t(mixed_ref[...].reshape(micro_count * rows, features), weight_ref[...])
        put_slots(out_refs, values, micro_count)

    return call_whole(
        body,
        [shape_of((local_rows, width), low)] * head_size,
        mixed,
        weights_t,
        scalars=0,
        flops=2 * micro_count * rows * width * features,
    )


def project_mixed_grad(grad_slots, weights_t, micro_count):
    count = len(grad_slots)
    local_rows, width = grad_slots[0].shape
    rows, features = len(layout_of(count)) * local_rows, weights_t.shape[1]

    def body(*refs):
        weight_ref, rows_ref, out_ref = refs[count:]
        fill_rows(rows_ref, refs[:count], micro_count)
        out_ref[...] = dot_plain(rows_ref[...], weight_ref[...]).astype(low)

    return call_whole(
        body,
        [shape_of((rows, width), low), shape_of((rows, features), low)],
        *grad_slots,
        weights_t,
        scalars=0,
        flops=2 * rows * width * features,
    )


def norm_gradients(raw, scales, gains, grads):
    rows, features = grads.shape
    width = features // 2

    def body(raw_ref, scale_ref, gain_ref, grad_ref, dot_ref, gain_grad_ref, totals):
        totals[...] = jnp.zeros_like(totals)
        for k in range(2):
            cut = slice(k * width, (k + 1) * width)
            terms = grad_ref[:, cut] * (raw_ref[:, cut] * scale_ref[:, k : k + 1])
            gain_grad_ref[:, cut] = jnp.sum(terms, axis=0, keepdims=True)
            totals[:, k : k + 1] = jnp.sum(terms * gain_ref[:, cut], axis=1, keepdims=True)
        dot_ref[...] = jnp.transpose(totals[...])[:2, :]

    return call_whole(
        body,
        [shape_of((2, rows), full), shape_of((1, features), full)],
        raw,
        scales,
        gains,
        grads,
        scalars=0,
        scratch=[pltpu.VMEM((rows, 128), full)],
    )


def project_input_grad(raw, scales, dots, gains, grads, grad_value, weights, slot_count, micro_count):
    rows, features = grad_value.shape[0], weights.shape[1]
    width = features // 3
    out_width = weights.shape[0]
    local_rows = rows // slot_count
    tile = tile_of(out_width)
    steps = out_width // tile

    def body(raw_ref, scale_ref, dot_ref, gain_ref, grad_ref, value_ref, weight_ref, low_ref, *out_refs):
        @pl.when(pl.program_id(0) == 0)
        def _():
            for k in range(2):
                cut = slice(k * width, (k + 1) * width)
                scale = scale_ref[:, k : k + 1]
                hat = raw_ref[:, cut] * scale
                grad_hat = grad_ref[:, cut] * gain_ref[:, cut]
                low_ref[:, cut] = (scale * (grad_hat - hat * dot_ref[:, k : k + 1])).astype(low)

        terms = dot_right_t(low_ref[...], weight_ref[:, : 2 * width])
        terms += dot_right_t(value_ref[...], weight_ref[:, 2 * width :])
        put_slots(out_refs, terms, micro_count)

    return call_grid(
        body,
        steps,
        [shape_of((rows, 2 * width), low)]
        + [shape_of((local_rows, out_width), low)] * slot_count,
        [
            fixed((rows, 2 * width)),
            fixed((rows, 2)),
            fixed((rows, 2)),
            fixed((1, 2 * width)),
            fixed((rows, 2 * width)),
            fixed((rows, width)),
            pl.BlockSpec((tile, features), lambda i: (i, 0)),
        ],
        [fixed((rows, 2 * width))]
        + [pl.BlockSpec((local_rows, tile), lambda i: (0, i))] * slot_count,
        raw,
        scales,
        dots,
        gains,
        grads,
        grad_value,
        weights,
        flops=2 * rows * features * out_width,
    )


def weight_term_slots(me, lefts, rights, blocks):
    n = len(lefts)
    rows, width = lefts[0].shape
    features = rights[0].shape[1]
    part = width // blocks
    half = blocks // 2

    def body(me_ref, *refs):
        odd_ref, even_ref, left_t, right_all = refs[2 * n :]
        step = pl.program_id(0)

        @pl.when(step == 0)
        def _():
            for m in range(n):
                cut = slice(m * rows, (m + 1) * rows)
                left_t[:, cut] = jnp.transpose(refs[m][...])
                right_all[cut, :] = refs[n + m][...]

        slot = jnp.where(step < half, 2 * step + 1, 2 * step - blocks)
        place = pl.multiple_of((me_ref[0] ^ slot) * part, part)
        term = dot_plain(left_t[pl.ds(place, part), :], right_all[...]).astype(low)

        @pl.when(step < half)
        def _():
            odd_ref[0] = term

        @pl.when(step >= half)
        def _():
            even_ref[0] = term

    return call_grid(
        body,
        blocks,
        [shape_of((half, part, features), low)] * 2,
        [scalar_spec] + [fixed((rows, width))] * n + [fixed((rows, features))] * n,
        [
            pl.BlockSpec((1, part, features), lambda i: (jnp.minimum(i, half - 1), 0, 0)),
            pl.BlockSpec((1, part, features), lambda i: (jnp.maximum(i - half, 0), 0, 0)),
        ],
        me,
        *lefts,
        *rights,
        scratch=[pltpu.VMEM((width, n * rows), low), pltpu.VMEM((n * rows, features), low)],
        flops=2 * n * rows * width * features,
    )


def to_owner(terms, *others):
    odd, even = terms
    blocks = 2 * even.shape[0]
    arrived = swap_cores(odd)
    even = after(even, *others)
    pairs = [even[k].astype(full) + arrived[k].astype(full) for k in range(blocks // 2)]
    slots = exchange_chips([pairs[0]] + [pair.astype(low) for pair in pairs[1:]])
    return sum(slot.astype(full) for slot in slots)


def send_views(me, raw, scales, gains, tables, heads_local):
    micro_count, rows = raw.shape[:2]
    blocks = micro_count * heads_local
    width = heads_local * HD

    def body(me_ref, *refs):
        raw_ref, scale_ref, gain_ref, cos_ref, sin_ref = refs[:5]
        out_refs = refs[5:]
        cosine, sine = cos_ref[...], sin_ref[...]
        for s in range(blocks):
            target = me_ref[0] ^ s
            column = pl.multiple_of((target % heads_local) * HD, HD)

            micro = target // heads_local
            for part in range(2):
                feature = pl.multiple_of(part * width + column, HD)
                values = raw_ref[micro, :, pl.ds(feature, HD)]
                values = values * scale_ref[micro, :, part : part + 1]
                values = values * gain_ref[:, pl.ds(feature, HD)]
                turned = values * cosine + pltpu.roll(values, HD // 2, 1) * sine
                out_refs[s][:, part * HD : (part + 1) * HD] = turned.astype(low)
            feature = pl.multiple_of(2 * width + column, HD)
            out_refs[s][:, 2 * HD :] = raw_ref[micro, :, pl.ds(feature, HD)].astype(low)

    return call_whole(
        body,
        [shape_of((rows, 3 * HD), low)] * blocks,
        me,
        raw,
        scales,
        gains,
        *tables,
    )


def masked_scores(k_rows, q_rows, key_seg, query_seg, key_pos=None, query_pos=None):
    scores = dot_right_t(k_rows, q_rows) * score_scale
    allowed = key_seg == query_seg
    if key_pos is not None:
        allowed = (allowed & (key_pos <= query_pos)) | (key_pos == query_pos)
    return jnp.where(allowed, scores, hidden_score)


def attention_forward(me, slots, key_seg, key_pos, query_seg, query_pos):
    blocks = len(slots)
    rows = slots[0].shape[0]
    length = blocks * rows

    def body(me_ref, *refs):
        slot_refs = refs[:blocks]
        ks_ref, kp_ref, qs_ref, qp_ref = refs[blocks : blocks + 4]
        out_refs = refs[blocks + 4 : 2 * blocks + 4]
        mixed_ref, norm_ref, q_all, k_all, v_all = refs[2 * blocks + 4 :]
        for s in range(blocks):
            place = pl.ds(pl.multiple_of((me_ref[0] ^ s) * rows, rows), rows)
            q_all[place, :] = slot_refs[s][:, :HD]
            k_all[place, :] = slot_refs[s][:, HD : 2 * HD]
            v_all[place, :] = slot_refs[s][:, 2 * HD :]
        for i in range(blocks):
            here = slice(i * rows, (i + 1) * rows)
            q_rows = q_all[here, :]
            query_seg_row = qs_ref[:, here]
            parts = [
                masked_scores(
                    k_all[here, :], q_rows, ks_ref[here, :], query_seg_row, kp_ref[here, :], qp_ref[:, here]
                )
            ]
            spans = [here]
            if i > 0:
                past = slice(0, i * rows)
                parts.append(masked_scores(k_all[past, :], q_rows, ks_ref[past, :], query_seg_row))
                spans.append(past)
            top = functools.reduce(
                jnp.maximum, [jnp.max(part, axis=0, keepdims=True) for part in parts]
            )
            total = jnp.zeros((1, rows), full)
            summed = jnp.zeros((HD, rows), full)
            for part, span in zip(parts, spans):
                expanded = jnp.exp(part - top)
                total = total + jnp.sum(expanded, axis=0, keepdims=True)
                summed = summed + dot_left_t(v_all[span, :], expanded.astype(low))
            mixed_ref[here, :] = jnp.transpose(summed / total)
            norm_ref[:, here] = top + jnp.log(total)
        for s in range(blocks):
            place = pl.ds(pl.multiple_of((me_ref[0] ^ s) * rows, rows), rows)
            out_refs[s][...] = mixed_ref[place, :].astype(low)

    return call_whole(
        body,
        [shape_of((rows, HD), low)] * blocks
        + [shape_of((length, HD), full), shape_of((1, length), full)],
        me,
        *slots,
        key_seg,
        key_pos,
        query_seg,
        query_pos,
        scratch=[pltpu.VMEM((length, HD), low)] * 3,
        flops=2 * length * length * HD,
    )


def attention_backward(me, slots, grad_slots, mixed, norm, key_seg, key_pos, query_seg, query_pos):
    blocks = len(slots)
    rows = slots[0].shape[0]
    length = blocks * rows

    def body(me_ref, *refs):
        slot_refs = refs[:blocks]
        grad_refs = refs[blocks : 2 * blocks]
        mixed_ref, norm_ref, ks_ref, kp_ref, qs_ref, qp_ref = refs[2 * blocks : 2 * blocks + 6]
        out_refs = refs[2 * blocks + 6 : 3 * blocks + 6]
        q_all, k_all, v_all, g_all, dq_all, dk_all, dv_all = refs[3 * blocks + 6 :]
        for s in range(blocks):
            place = pl.ds(pl.multiple_of((me_ref[0] ^ s) * rows, rows), rows)
            q_all[place, :] = slot_refs[s][:, :HD]
            k_all[place, :] = slot_refs[s][:, HD : 2 * HD]
            v_all[place, :] = slot_refs[s][:, 2 * HD :]
            g_all[place, :] = grad_refs[s][...]
        for i in range(blocks):
            here = slice(i * rows, (i + 1) * rows)
            q_rows = q_all[here, :]
            g_rows = g_all[here, :]
            query_seg_row = qs_ref[:, here]
            norm_row = norm_ref[:, here]
            delta = jnp.sum(
                jnp.transpose(g_rows.astype(full) * mixed_ref[here, :]), axis=0, keepdims=True
            )
            spans = [here] + ([slice(0, i * rows)] if i > 0 else [])
            grad_query = jnp.zeros((HD, rows), full)
            for n, span in enumerate(spans):
                k_rows = k_all[span, :]
                if n == 0:
                    scores = masked_scores(
                        k_rows, q_rows, ks_ref[span, :], query_seg_row, kp_ref[span, :], qp_ref[:, here]
                    )
                else:
                    scores = masked_scores(k_rows, q_rows, ks_ref[span, :], query_seg_row)
                weights = jnp.exp(scores - norm_row)
                grad_probs = dot_right_t(v_all[span, :], g_rows)
                grad_scores = (weights * (grad_probs - delta)).astype(low)
                key_term = dot_plain(grad_scores, q_rows)
                value_term = dot_plain(weights.astype(low), g_rows)
                if n == 0:
                    dk_all[span, :] = key_term
                    dv_all[span, :] = value_term
                else:
                    dk_all[span, :] += key_term
                    dv_all[span, :] += value_term
                grad_query = grad_query + dot_left_t(k_rows, grad_scores)
            dq_all[here, :] = jnp.transpose(grad_query)
        for s in range(blocks):
            place = pl.ds(pl.multiple_of((me_ref[0] ^ s) * rows, rows), rows)
            out_refs[s][:, :HD] = (dq_all[place, :] * score_scale).astype(low)
            out_refs[s][:, HD : 2 * HD] = (dk_all[place, :] * score_scale).astype(low)
            out_refs[s][:, 2 * HD :] = dv_all[place, :].astype(low)

    return call_whole(
        body,
        [shape_of((rows, 3 * HD), low)] * blocks,
        me,
        *slots,
        *grad_slots,
        mixed,
        norm,
        key_seg,
        key_pos,
        query_seg,
        query_pos,
        scratch=[pltpu.VMEM((length, HD), low)] * 4 + [pltpu.VMEM((length, HD), full)] * 3,
        flops=5 * length * length * HD,
    )


def assemble_mixed(me, slots, micro_count, heads_local):
    rows = slots[0].shape[0]
    blocks = len(slots)

    def body(me_ref, *refs):
        out_ref = refs[blocks]
        for s in range(blocks):
            source = me_ref[0] ^ s
            column = pl.multiple_of((source % heads_local) * HD, HD)
            out_ref[source // heads_local, :, pl.ds(column, HD)] = refs[s][...]

    return call_whole(
        body, [shape_of((micro_count, rows, heads_local * HD), low)], me, *slots
    )[0]


def split_mixed(me, mixed, blocks, heads_local):
    micro_count, rows = mixed.shape[:2]

    def body(me_ref, mixed_ref, *out_refs):
        for s in range(blocks):
            target = me_ref[0] ^ s
            column = pl.multiple_of((target % heads_local) * HD, HD)
            out_refs[s][...] = mixed_ref[target // heads_local, :, pl.ds(column, HD)]

    return call_whole(body, [shape_of((rows, HD), low)] * blocks, me, mixed)


def receive_grads(me, slots, tables, micro_count, heads_local):
    rows = slots[0].shape[0]
    blocks = len(slots)
    width = heads_local * HD

    def body(me_ref, *refs):
        cos_ref, sin_ref, norm_ref, value_ref = refs[blocks:]
        cosine, sine = cos_ref[...], sin_ref[...]
        for s in range(blocks):
            source = me_ref[0] ^ s
            micro = source // heads_local
            column = pl.multiple_of((source % heads_local) * HD, HD)
            for part in range(2):
                grads = refs[s][:, part * HD : (part + 1) * HD].astype(full)
                turned = grads * cosine - pltpu.roll(grads, HD // 2, 1) * sine
                norm_ref[micro, :, pl.ds(part * width + column, HD)] = turned
            value_ref[micro, :, pl.ds(column, HD)] = refs[s][:, 2 * HD :]

    return call_whole(
        body,
        [
            shape_of((micro_count, rows, 2 * width), full),
            shape_of((micro_count, rows, width), low),
        ],
        me,
        *slots,
        *tables,
    )


def turn(values, tables):
    return values * tables[0][:, None, :] + jnp.roll(values, HD // 2, axis=-1) * tables[1][:, None, :]


def turn_back(grads, tables):
    return grads * tables[0][:, None, :] - jnp.roll(grads, HD // 2, axis=-1) * tables[1][:, None, :]


def block_scores(query_view, key_rows, query_mark, key_mark):
    scores = score_scale * jnp.einsum(
        "qhd,khd->hqk", query_view, key_rows, preferred_element_type=full
    )
    query_seg, query_pos = query_mark
    key_seg, key_pos = key_mark
    allowed = (query_seg[:, None] == key_seg[None, :]) & (key_pos[None, :] <= query_pos[:, None])
    allowed = allowed | (key_pos[None, :] == query_pos[:, None])
    return jnp.where(allowed[None], scores, hidden_score)


def gathered_forward(query_view, query_mark, stacked):
    rows, heads = query_view.shape[:2]

    def step(running, block):
        key_rows, value_rows, key_seg, key_pos = block
        top, total, summed = running
        scores = block_scores(query_view, key_rows, query_mark, (key_seg, key_pos))
        new_top = jnp.maximum(top, jnp.max(scores, axis=-1))
        shrink = jnp.exp(top - new_top)
        expanded = jnp.where(scores > hidden_score, jnp.exp(scores - new_top[..., None]), 0.0)
        new_total = total * shrink + jnp.sum(expanded, axis=-1)
        new_summed = summed * shrink[..., None] + jnp.einsum(
            "hqk,khd->hqd", expanded.astype(low), value_rows, preferred_element_type=full
        )
        return ((new_top, new_total, new_summed), None)

    start = (
        jnp.full((heads, rows), hidden_score, full),
        jnp.zeros((heads, rows), full),
        jnp.zeros((heads, rows, HD), full),
    )
    top, total, summed = lax.scan(step, start, stacked)[0]
    return jnp.swapaxes(summed / total[..., None], 0, 1), top + jnp.log(total)


def gathered_backward(query_view, grad_view, mixed, norm, query_mark, stacked):
    delta = jnp.sum(grad_view.astype(full) * mixed, axis=2).T

    def step(running, block):
        key_rows, value_rows, key_seg, key_pos = block
        scores = block_scores(query_view, key_rows, query_mark, (key_seg, key_pos))
        weights = jnp.exp(scores - norm[..., None])
        grad_probs = jnp.einsum("qhd,khd->hqk", grad_view, value_rows, preferred_element_type=full)
        grad_scores = (weights * (grad_probs - delta[..., None])).astype(low)
        grad_query = running + jnp.einsum(
            "hqk,khd->qhd", grad_scores, key_rows, preferred_element_type=full
        )
        grad_keys = jnp.einsum("hqk,qhd->khd", grad_scores, query_view, preferred_element_type=full)
        grad_values = jnp.einsum(
            "hqk,qhd->khd", weights.astype(low), grad_view, preferred_element_type=full
        )
        return (
            grad_query,
            jnp.concatenate([grad_keys * score_scale, grad_values], axis=1).astype(low),
        )

    grad_query, key_terms = lax.scan(step, jnp.zeros(query_view.shape, full), stacked)
    return grad_query * score_scale, key_terms


class GatheredAttention:
    def __init__(self, raw, scales, gains, tables, codes, positions):
        blocks, rows = positions.shape
        self.tables, self.rows = tables, rows
        width = gains.shape[1] // 2
        shape = (rows, width // HD, HD)
        self.sets = []
        for m in range(raw.shape[0]):
            values = raw[m]
            views = []
            for part in range(2):
                cut = values[:, part * width : (part + 1) * width]
                normed = cut * scales[m, :, part : part + 1] * gains[:, part * width : (part + 1) * width]
                views.append(turn(normed.reshape(shape), tables).astype(low))
            value_view = values[:, 2 * width :].astype(low).reshape(shape)
            seg_all = (codes[m] // 2).reshape(blocks, rows)
            key_seg = jnp.where(codes[m] % 2 == 1, codes[m] // 2, -1).reshape(blocks, rows)
            place = lax.axis_index("blk")
            mark = tuple(
                lax.dynamic_index_in_dim(mark, place, 0, keepdims=False)
                for mark in (seg_all, positions)
            )
            stacked = (
                lax.all_gather(views[1], "blk"),
                lax.all_gather(value_view, "blk"),
                key_seg,
                positions,
            )
            self.sets.append((views[0], mark, stacked))

    def forward(self):
        results = [gathered_forward(*one) for one in self.sets]
        self.kept = results
        return jnp.stack(
            [mixed.reshape(self.rows, -1).astype(low) for mixed, norm in results]
        )

    def backward(self, grad_mixed, *others):
        norms, values = [], []
        for m, (view, mark, stacked) in enumerate(self.sets):
            grad_query, terms = gathered_backward(
                view, grad_mixed[m].reshape(view.shape), *self.kept[m], mark, stacked
            )
            own = lax.psum_scatter(terms, "blk", scatter_dimension=0, tiled=False)
            heads = view.shape[1]
            both = [turn_back(grad_query, self.tables)]
            both.append(turn_back(own[:, :heads].astype(full), self.tables))
            norms.append(jnp.concatenate([g.reshape(self.rows, -1) for g in both], axis=1))
            values.append(own[:, heads:].reshape(self.rows, -1))
        return jnp.stack(norms), jnp.stack(values)


class ExchangedAttention:
    def __init__(self, raw, scales, gains, tables, codes, positions):
        self.blocks, self.tables = positions.shape[0], tables
        self.heads = gains.shape[1] // (2 * HD)
        self.micro_count = raw.shape[0]
        place = lax.axis_index("blk")
        self.me = place.astype(jnp.int32).reshape(1)
        self.slots = exchange_slots(
            send_views(self.me, raw, scales, gains, tables, self.heads), "blk"
        )
        codes = lax.dynamic_index_in_dim(codes, place // self.heads, 0, keepdims=False)
        seg_all = codes // 2
        seg_key = jnp.where(codes % 2 == 1, seg_all, -1)
        pos_all = positions.reshape(-1)
        self.marks = (seg_key[:, None], pos_all[:, None], seg_all[None, :], pos_all[None, :])

    def forward(self):
        results = attention_forward(self.me, self.slots, *self.marks)
        self.kept = results[self.blocks :]
        return assemble_mixed(
            self.me,
            exchange_slots(results[: self.blocks], "blk"),
            self.micro_count,
            self.heads,
        )

    def backward(self, grad_mixed, *others):
        grad_slots = exchange_slots(
            split_mixed(self.me, grad_mixed, self.blocks, self.heads), "blk"
        )
        grad_slots = [after(grad_slots[0], *others)] + grad_slots[1:]
        back_slots = exchange_slots(
            attention_backward(self.me, self.slots, grad_slots, *self.kept, *self.marks), "blk"
        )
        return receive_grads(self.me, back_slots, self.tables, self.micro_count, self.heads)


def on_device(
    tokens,
    cotangent,
    segments,
    padding,
    query_weight,
    key_weight,
    value_weight,
    output_weight,
    query_gain,
    key_gain,
    attn_gain,
    gate_weight,
    up_weight,
    down_weight,
    ffn_gain,
):
    micro_count, local_rows, model_width = tokens.shape
    blocks = lax.axis_size("blk")
    head_size = lax.axis_size("head")
    group_rows = local_rows * head_size
    width = query_weight.shape[1]
    heads_local = width // HD
    block_index = lax.axis_index("blk")
    head_index = lax.axis_index("head")
    me = block_index.astype(jnp.int32).reshape(1)
    slot_owner = head_index ^ jnp.arange(head_size, dtype=jnp.int32)
    group_order = (
        slot_owner[:, None] * local_rows + jnp.arange(local_rows, dtype=jnp.int32)[None, :]
    ).reshape(group_rows)
    tables = rotary_tables(block_index * group_rows + group_order)

    def gather_weights(*parts):
        return lax.all_gather(jnp.concatenate(parts, axis=1), "blk", axis=0, tiled=True)

    qkv_full = gather_weights(query_weight, key_weight, value_weight)
    output_full_t = gather_weights(output_weight.T)
    ffn_full = gather_weights(gate_weight, up_weight, down_weight.T)

    def by_micro(values):
        return values.reshape(micro_count, -1, values.shape[-1])

    def all_rows(values):
        return values.reshape(-1, values.shape[-1])

    def sum_token_heads(values):
        values = values.reshape(2 * micro_count, group_rows)
        return sum_heads(values).reshape(2, micro_count * group_rows).T

    token_rows, raw, squares = project_qkv(gather_parts(all_rows(tokens)), qkv_full, micro_count)
    codes = jnp.concatenate(gather_slots(segments * 2 + padding, "head"), axis=1)
    codes = gather_doubling(codes, "blk")
    codes = codes[block_index ^ jnp.arange(blocks, dtype=jnp.int32)].swapaxes(0, 1)

    scales = lax.rsqrt(sum_token_heads(squares) / model_width + epsilon)
    gain_row = jnp.concatenate([query_gain, key_gain])[None, :]
    positions = jnp.arange(blocks, dtype=jnp.int32)[:, None] * group_rows + group_order[None, :]
    exchanged = blocks == micro_count * heads_local and blocks & (blocks - 1) == 0
    attention = (ExchangedAttention if exchanged else GatheredAttention)(
        by_micro(raw), by_micro(scales), gain_row, tables, codes.reshape(micro_count, -1), positions
    )
    mixed = attention.forward()

    attn_gain, ffn_gain = attn_gain[None, :], ffn_gain[None, :]
    token_own, grad_own = all_rows(tokens), all_rows(cotangent)
    arrived = reduce_parts(project_output(mixed, output_full_t, head_size))
    hidden, hidden_low, attn_hat, attn_scale = after_attention(arrived, token_own, attn_gain)
    (hidden_rows, gate, up, middle_rows), slots = ffn_forward(
        gather_parts(hidden_low), ffn_full, micro_count
    )
    output, grad_down, ffn_gain_grad = after_ffn(reduce_parts(slots), hidden, grad_own, ffn_gain)
    (grad_rows, grad_gate, grad_up), slots = ffn_backward(
        gather_parts(grad_down), gate, up, ffn_full, micro_count
    )
    arrived = reduce_parts(slots)
    grad_hidden, grad_attn, attn_gain_grad = before_attention(
        arrived, grad_own, attn_hat, attn_scale, attn_gain
    )
    ffn_terms = ffn_weight_term([], 2, [grad_rows], [middle_rows])
    ffn_terms = ffn_weight_term([ffn_terms], 0, [hidden_rows], [grad_gate])
    ffn_terms = ffn_weight_term([ffn_terms], 1, [hidden_rows], [grad_up])
    ffn_terms = after(ffn_terms, *arrived)
    ffn_grads = widen_ffn(
        lax.psum_scatter(ffn_terms, "blk", scatter_dimension=0, tiled=True)
    )
    norm_gain_grads = sum_doubling(
        jnp.concatenate([attn_gain_grad, ffn_gain_grad], axis=1)[0], "blk"
    )
    norm_gain_grads = sum_doubling(norm_gain_grads, "head")

    grad_attn_rows, grad_mixed = project_mixed_grad(
        gather_parts(grad_attn), output_full_t, micro_count
    )
    output_terms = weight_term_slots(me, [grad_attn_rows], [all_rows(mixed)], blocks)
    grad_norm, grad_value = attention.backward(by_micro(grad_mixed), *output_terms)
    grad_norm, grad_value = all_rows(grad_norm), all_rows(grad_value)
    dots, qk_gain_grad = norm_gradients(raw, scales, gain_row, grad_norm)
    mean_dots = sum_token_heads(after(dots, norm_gain_grads)) / model_width
    value_terms = weight_term_slots(me, [token_rows], [grad_value], blocks)
    results = project_input_grad(
        raw, scales, mean_dots, gain_row, grad_norm, grad_value, qkv_full, head_size, micro_count
    )
    input_grad = sum_full(reduce_parts(results[1:])) + grad_hidden
    output_grad = to_owner(output_terms).T
    value_grad = to_owner(value_terms)
    qk_grad = to_owner(weight_term_slots(me, [token_rows], [results[0]], blocks), *ffn_grads)

    qk_gain_grad = sum_doubling(qk_gain_grad[0], "blk")
    return (
        by_micro(output),
        by_micro(input_grad),
        qk_grad[:, :width],
        qk_grad[:, width:],
        value_grad,
        output_grad,
        qk_gain_grad[:width],
        qk_gain_grad[width:],
        norm_gain_grads[:model_width],
        *ffn_grads,
        norm_gain_grads[model_width:],
    )


def solution(mesh):
    return jax.shard_map(
        on_device,
        mesh=mesh,
        in_specs=(
            P(None, ("blk", "head"), None),
            P(None, ("blk", "head"), None),
            P(None, ("blk", "head")),
            P(None, ("blk", "head")),
            P("blk", "head"),
            P("blk", "head"),
            P("blk", "head"),
            P("head", "blk"),
            P("head"),
            P("head"),
            P(),
            P("blk", "head"),
            P("blk", "head"),
            P("head", "blk"),
            P(),
        ),
        out_specs=(
            P(None, ("blk", "head"), None),
            P(None, ("blk", "head"), None),
            P("blk", "head"),
            P("blk", "head"),
            P("blk", "head"),
            P("head", "blk"),
            P("head"),
            P("head"),
            P(),
            P("blk", "head"),
            P("blk", "head"),
            P("head", "blk"),
            P(),
        ),
        check_vma=False,
    )
```

```python
import functools
import math

import jax
import jax.numpy as jnp
from jax import lax
from jax.experimental import pallas as pl
from jax.experimental.pallas import tpu as pltpu
from jax.sharding import PartitionSpec as P

HD = 128

epsilon = 1e-06
theta = 500000.0
widest = 512
score_scale = HD ** (-0.5)
hidden_score = -1e30
low = jnp.bfloat16
full = jnp.float32
vmem_grant = 56 * 1024 * 1024


def dot_plain(left_side, right_side):
    return jnp.dot(left_side, right_side, preferred_element_type=full)


def dot_right_t(left_side, right_side):
    return lax.dot_general(
        left_side, right_side, (((1,), (1,)), ((), ())), preferred_element_type=full
    )


def dot_left_t(left_side, right_side):
    return lax.dot_general(
        left_side, right_side, (((0,), (0,)), ((), ())), preferred_element_type=full
    )


def rms_scale(values):
    return lax.rsqrt(jnp.mean(values * values, axis=-1, keepdims=True) + epsilon)


def xor_pairs(size, mask):
    return [(i, i ^ mask) for i in range(size)]


def gather_slots(values, axis):
    size = lax.axis_size(axis)
    return [values] + [lax.ppermute(values, axis, xor_pairs(size, s)) for s in range(1, size)]


def exchange_slots(slots, axis):
    size = lax.axis_size(axis)
    return [slots[0]] + [
        lax.ppermute(slots[s], axis, xor_pairs(size, s)) for s in range(1, size)
    ]


def gather_doubling(values, axis):
    held = values[None]
    step = 1
    while step < lax.axis_size(axis):
        arrived = lax.ppermute(held, axis, xor_pairs(lax.axis_size(axis), step))
        held = jnp.concatenate([held, arrived], axis=0)
        step *= 2
    return held


def sum_doubling(values, axis):
    step = 1
    while step < lax.axis_size(axis):
        values = values + lax.ppermute(values, axis, xor_pairs(lax.axis_size(axis), step))
        step *= 2
    return values


def after(values, *others):
    return lax.optimization_barrier((values, others))[0]


inward = [(0, 1), (3, 2)]
outward = [(1, 0), (2, 3)]
middle = [(1, 2), (2, 1)]


def send_rows(values, pairs):
    return lax.ppermute(values, "head", pairs)


def gather_parts(values):
    if lax.axis_size("head") != 4:
        return gather_slots(values, "head")
    second = send_rows(values, xor_pairs(4, 2))
    first = send_rows(values, xor_pairs(4, 1))
    across = send_rows(values, middle)
    return [values, first, second, across, send_rows(second, outward)]


def layout_of(count):
    return [(0,), (1,), (2,), (3, 4)] if count == 5 else [(s,) for s in range(count)]


def reduce_parts(slots):
    if lax.axis_size("head") != 4:
        return exchange_slots(slots, "head")
    arrived = send_rows(slots[3], inward)
    first = send_rows(slots[1], xor_pairs(4, 1))
    across = send_rows(slots[3], middle)
    passed = (slots[2].astype(full) + arrived.astype(full)).astype(low)
    return [slots[0], first, across, send_rows(passed, xor_pairs(4, 2))]


def exchange_chips(slots):
    size = lax.axis_size("blk")
    return [slots[0]] + [
        lax.ppermute(slots[m], "blk", xor_pairs(size, 2 * m)) for m in range(1, size // 2)
    ]


def swap_cores(values):
    return lax.ppermute(values, "blk", xor_pairs(lax.axis_size("blk"), 1))


def sum_full(arrays):
    return sum(array.astype(full) for array in arrays)


def sum_heads(values, others=None):
    size = lax.axis_size("head")
    count = values.size
    sent = values.reshape(-1)
    if others is not None:
        sent = jnp.concatenate([sent, others])
    total = 0.0
    for s, arrived in enumerate(gather_slots(sent, "head")):
        slots = jnp.split(arrived[:count].reshape(values.shape), size, axis=1)
        ordered = jnp.concatenate([slots[t ^ s] for t in range(size)], axis=1)
        total = total + jnp.concatenate([ordered.reshape(-1), arrived[count:]])
    return total[:count].reshape(values.shape), total[count:]


def rotary_tables(positions):
    half_size = HD // 2
    inverse = theta ** (-2.0 * jnp.arange(half_size, dtype=jnp.int32).astype(full) / HD)
    angles = positions.astype(full)[:, None] * inverse[None, :]
    cosine, sine = jnp.cos(angles), jnp.sin(angles)
    return (
        jnp.concatenate([cosine, cosine], axis=1),
        jnp.concatenate([-sine, sine], axis=1),
    )


def shape_of(shape, dtype):
    return jax.ShapeDtypeStruct(shape, dtype)


def sizes_of(arrays):
    return sum(a.size * a.dtype.itemsize for a in arrays)


def call_whole(body, outs, *args, scalars=1, scratch=(), flops=0):
    return pl.pallas_call(
        body,
        out_shape=outs,
        in_specs=[pl.BlockSpec(memory_space=pltpu.SMEM)] * scalars
        + [pl.BlockSpec(memory_space=pltpu.VMEM)] * (len(args) - scalars),
        out_specs=[pl.BlockSpec(memory_space=pltpu.VMEM)] * len(outs),
        scratch_shapes=list(scratch),
        compiler_params=pltpu.CompilerParams(vmem_limit_bytes=vmem_grant),
        cost_estimate=pl.CostEstimate(
            flops=flops,
            bytes_accessed=sizes_of(args) + sizes_of(outs),
            transcendentals=0,
        ),
    )(*args)


def call_grid(body, steps, outs, in_specs, out_specs, *args, scratch=(), flops=0):
    return pl.pallas_call(
        body,
        grid=(steps,),
        out_shape=outs,
        in_specs=in_specs,
        out_specs=out_specs,
        scratch_shapes=list(scratch),
        compiler_params=pltpu.CompilerParams(vmem_limit_bytes=vmem_grant),
        cost_estimate=pl.CostEstimate(
            flops=flops, bytes_accessed=sizes_of(args) + sizes_of(outs), transcendentals=0
        ),
    )(*args)


def fixed(shape):
    return pl.BlockSpec(shape, lambda i: (0,) * len(shape))


scalar_spec = pl.BlockSpec(memory_space=pltpu.SMEM)


def tile_of(size):
    return math.gcd(size, widest)


def column_tile(rows, tile, first=0):
    return pl.BlockSpec((rows, tile), lambda i: (0, first + i))


def slot_cuts(micro_count, count, rows):
    for s in range(count):
        for m in range(micro_count):
            first = (m * count + s) * rows
            yield s, slice(m * rows, (m + 1) * rows), slice(first, first + rows)


def put_slots(out_refs, values, micro_count):
    rows = out_refs[0].shape[0] // micro_count
    for s, inner, outer in slot_cuts(micro_count, len(out_refs), rows):
        out_refs[s][inner, :] = values[outer].astype(out_refs[s].dtype)


def fill_rows(rows_ref, part_refs, micro_count):
    layout = layout_of(len(part_refs))
    rows = part_refs[0].shape[0] // micro_count
    for s, inner, outer in slot_cuts(micro_count, len(layout), rows):
        rows_ref[outer, :] = functools.reduce(
            jnp.add, [part_refs[part][inner, :] for part in layout[s]]
        )


def sum_slots(refs):
    return sum(ref[...].astype(full) for ref in refs)


def ffn_forward(slots, weights, micro_count):
    n = len(slots)
    local_rows, width = slots[0].shape
    count = len(layout_of(n))
    rows, hidden = count * local_rows, weights.shape[1] // 3
    tile = tile_of(hidden)
    steps = hidden // tile

    def body(*refs):
        wg_ref, wu_ref, wd_ref = refs[n : n + 3]
        rows_ref, gate_ref, up_ref, middle_ref = refs[n + 3 : n + 7]
        out_refs, total = refs[n + 7 : -1], refs[-1]
        step = pl.program_id(0)

        @pl.when(step == 0)
        def _():
            fill_rows(rows_ref, refs[:n], micro_count)

        values = rows_ref[...]
        gate = dot_plain(values, wg_ref[...])
        up = dot_plain(values, wu_ref[...])
        gate_ref[...] = gate.astype(low)
        up_ref[...] = up.astype(low)
        middle = (gate * jax.nn.sigmoid(gate) * up).astype(low)
        middle_ref[...] = middle
        term = dot_right_t(middle, wd_ref[...])

        @pl.when(step == 0)
        def _():
            total[...] = term

        @pl.when(step > 0)
        def _():
            total[...] += term

        @pl.when(step == steps - 1)
        def _():
            put_slots(out_refs, total[...], micro_count)

    results = call_grid(
        body,
        steps,
        [shape_of((rows, width), low)]
        + [shape_of((rows, hidden), low)] * 3
        + [shape_of((local_rows, width), low)] * count,
        [fixed((local_rows, width))] * n + [column_tile(width, tile, k * steps) for k in range(3)],
        [fixed((rows, width))] + [column_tile(rows, tile)] * 3 + [fixed((local_rows, width))] * count,
        *slots,
        weights,
        weights,
        weights,
        scratch=[pltpu.VMEM((rows, width), full)],
        flops=6 * rows * width * hidden,
    )
    return results[:4], results[4:]


def ffn_backward(slots, gate, up, weights, micro_count):
    n = len(slots)
    local_rows, width = slots[0].shape
    rows, hidden = gate.shape
    count = rows // local_rows
    tile = tile_of(hidden)
    steps = hidden // tile

    def body(*refs):
        gate_ref, up_ref, wg_ref, wu_ref, wd_ref = refs[n : n + 5]
        rows_ref, gg_ref, gu_ref = refs[n + 5 : n + 8]
        out_refs, total = refs[n + 8 : -1], refs[-1]
        step = pl.program_id(0)

        @pl.when(step == 0)
        def _():
            fill_rows(rows_ref, refs[:n], micro_count)

        grad_middle = dot_plain(rows_ref[...], wd_ref[...])
        gate_values = gate_ref[...].astype(full)
        sigmoid = jax.nn.sigmoid(gate_values)
        silu = gate_values * sigmoid
        grad_up = (grad_middle * silu).astype(low)
        grad_gate = (
            grad_middle * up_ref[...].astype(full) * (sigmoid + silu * (1.0 - sigmoid))
        ).astype(low)
        gg_ref[...] = grad_gate
        gu_ref[...] = grad_up
        term = dot_right_t(grad_gate, wg_ref[...]) + dot_right_t(grad_up, wu_ref[...])

        @pl.when(step == 0)
        def _():
            total[...] = term

        @pl.when(step > 0)
        def _():
            total[...] += term

        @pl.when(step == steps - 1)
        def _():
            put_slots(out_refs, total[...], micro_count)

    results = call_grid(
        body,
        steps,
        [shape_of((rows, width), low)]
        + [shape_of((rows, hidden), low)] * 2
        + [shape_of((local_rows, width), low)] * count,
        [fixed((local_rows, width))] * n
        + [column_tile(rows, tile)] * 2
        + [column_tile(width, tile, k * steps) for k in range(3)],
        [fixed((rows, width))] + [column_tile(rows, tile)] * 2 + [fixed((local_rows, width))] * count,
        *slots,
        gate,
        up,
        weights,
        weights,
        weights,
        scratch=[pltpu.VMEM((rows, width), full)],
        flops=6 * rows * width * hidden,
    )
    return results[:3], results[3:]


def ffn_weight_term(held, part, parts, lefts, rights):
    n = len(lefts)
    rows, width = lefts[0].shape
    hidden = rights[0].shape[1]
    tile = tile_of(hidden)
    steps = hidden // tile

    def body(*refs):
        out_ref, left_t = refs[-2:]

        @pl.when(pl.program_id(0) == 0)
        def _():
            for m in range(n):
                left_t[:, m * rows : (m + 1) * rows] = jnp.transpose(refs[m][...])

        right = jnp.concatenate([ref[...] for ref in refs[n : 2 * n]], axis=0)
        out_ref[...] = dot_plain(left_t[...], right).astype(low)

    shape = shape_of((width, parts * hidden), low)
    return pl.pallas_call(
        body,
        grid=(steps,),
        out_shape=shape,
        in_specs=[fixed((rows, width))] * n
        + [column_tile(rows, tile)] * n
        + [pl.BlockSpec(memory_space=pl.ANY)] * len(held),
        out_specs=column_tile(width, tile, part * steps),
        scratch_shapes=[pltpu.VMEM((width, n * rows), low)],
        input_output_aliases={2 * n: 0} if held else {},
        compiler_params=pltpu.CompilerParams(vmem_limit_bytes=vmem_grant),
        cost_estimate=pl.CostEstimate(
            flops=2 * n * rows * width * hidden,
            bytes_accessed=sizes_of(lefts) + width * hidden * 2,
            transcendentals=0,
        ),
    )(*lefts, *rights, *held)


def widen_ffn(grads, down_grads):
    rows, hidden = down_grads.shape

    def body(grad_ref, turned_ref, gate_ref, up_ref, down_ref):
        gate_ref[...] = grad_ref[:, :hidden].astype(full)
        up_ref[...] = grad_ref[:, hidden:].astype(full)
        down_ref[...] = jnp.transpose(turned_ref[...]).astype(full)

    return call_whole(
        body,
        [shape_of((rows, hidden), full)] * 2 + [shape_of((hidden, rows), full)],
        grads,
        down_grads,
        scalars=0,
    )


def after_attention(arrived, tokens, gain):
    n = len(arrived)

    def body(*refs):
        token_ref, gain_ref, hidden_ref, low_ref, hat_ref, scale_ref = refs[n:]
        attn = sum_slots(refs[:n])
        scale = rms_scale(attn)
        hat = attn * scale
        hidden = token_ref[...].astype(full) + hat * gain_ref[...]
        hidden_ref[...] = hidden
        low_ref[...] = hidden.astype(low)
        hat_ref[...] = hat
        scale_ref[...] = scale

    shape = tokens.shape
    return call_whole(
        body,
        [shape_of(shape, full), shape_of(shape, low), shape_of(shape, full), shape_of((shape[0], 1), full)],
        *arrived,
        tokens,
        gain,
        scalars=0,
    )


def after_ffn(arrived, hidden, cotangent, gain):
    n = len(arrived)

    def body(*refs):
        hidden_ref, grad_ref, gain_ref, out_ref, low_ref, gain_grad_ref = refs[n:]
        down = sum_slots(refs[:n])
        scale = rms_scale(down)
        hat = down * scale
        out_ref[...] = (hidden_ref[...] + hat * gain_ref[...]).astype(low)
        grad_out = grad_ref[...].astype(full)
        gain_grad_ref[...] = jnp.sum(grad_out * hat, axis=0, keepdims=True)
        grad = grad_out * gain_ref[...]
        low_ref[...] = (scale * (grad - hat * jnp.mean(grad * hat, axis=1, keepdims=True))).astype(low)

    shape = hidden.shape
    return call_whole(
        body,
        [shape_of(shape, low), shape_of(shape, low), shape_of((1, shape[1]), full)],
        *arrived,
        hidden,
        cotangent,
        gain,
        scalars=0,
    )


def before_attention(arrived, cotangent, hat, scale, gain):
    n = len(arrived)

    def body(*refs):
        grad_ref, hat_ref, scale_ref, gain_ref, hidden_ref, low_ref, gain_grad_ref = refs[n:]
        grad_hidden = sum_slots(refs[:n]) + grad_ref[...].astype(full)
        hidden_ref[...] = grad_hidden
        hat = hat_ref[...]
        gain_grad_ref[...] = jnp.sum(grad_hidden * hat, axis=0, keepdims=True)
        grad = grad_hidden * gain_ref[...]
        low_ref[...] = (
            scale_ref[...] * (grad - hat * jnp.mean(grad * hat, axis=1, keepdims=True))
        ).astype(low)

    shape = hat.shape
    return call_whole(
        body,
        [shape_of(shape, full), shape_of(shape, low), shape_of((1, shape[1]), full)],
        *arrived,
        cotangent,
        hat,
        scale,
        gain,
        scalars=0,
    )


def project_qkv(token_slots, weights, micro_count):
    count = len(token_slots)
    local_rows, width = token_slots[0].shape
    rows, features = len(layout_of(count)) * local_rows, weights.shape[1]
    part = features // 3
    tile = tile_of(part)
    steps = features // tile
    part_steps = part // tile

    def body(*refs):
        weight_ref, rows_ref, raw_ref, square_ref, totals = refs[count:]
        step = pl.program_id(0)

        @pl.when(step == 0)
        def _():
            fill_rows(rows_ref, refs[:count], micro_count)
            totals[...] = jnp.zeros_like(totals)

        raw = dot_plain(rows_ref[...], weight_ref[...])
        raw_ref[...] = raw
        sums = jnp.sum(raw * raw, axis=1, keepdims=True)
        for k in range(2):

            @pl.when(step // part_steps == k)
            def _():
                totals[:, k : k + 1] += sums

        @pl.when(step == steps - 1)
        def _():
            square_ref[...] = jnp.transpose(totals[...])[:2, :]

    return call_grid(
        body,
        steps,
        [shape_of((rows, width), low), shape_of((rows, features), full), shape_of((2, rows), full)],
        [fixed((local_rows, width))] * count + [column_tile(width, tile)],
        [fixed((rows, width)), column_tile(rows, tile), fixed((2, rows))],
        *token_slots,
        weights,
        scratch=[pltpu.VMEM((rows, 128), full)],
        flops=2 * rows * width * features,
    )


def project_output(mixed, weights_t, head_size):
    micro_count, rows, features = mixed.shape
    width = weights_t.shape[0]
    local_rows = micro_count * rows // head_size

    def body(mixed_ref, weight_ref, *out_refs):
        values = dot_right_t(mixed_ref[...].reshape(micro_count * rows, features), weight_ref[...])
        put_slots(out_refs, values, micro_count)

    return call_whole(
        body,
        [shape_of((local_rows, width), low)] * head_size,
        mixed,
        weights_t,
        scalars=0,
        flops=2 * micro_count * rows * width * features,
    )


def project_mixed_grad(grad_rows, weights_t, head_size):
    rows, width = grad_rows.shape
    features = weights_t.shape[1] // head_size

    def body(grad_ref, weight_ref, *out_refs):
        term = dot_plain(grad_ref[...], weight_ref[...]).astype(low)
        for s in range(head_size):

            @pl.when(pl.program_id(0) == s)
            def _():
                out_refs[s][...] = term

    return call_grid(
        body,
        head_size,
        [shape_of((rows, features), low)] * head_size,
        [fixed((rows, width)), column_tile(width, features)],
        [fixed((rows, features))] * head_size,
        grad_rows,
        weights_t,
        flops=2 * rows * width * weights_t.shape[1],
    )


def join_rows(parts, micro_count):
    rows, width = parts[0].shape
    count = len(parts)

    def body(*refs):
        fill_rows(refs[count], refs[:count], micro_count)

    return call_whole(
        body, [shape_of((len(layout_of(count)) * rows, width), low)], *parts, scalars=0
    )[0]


def norm_gradients(raw, scales, gains, grads):
    rows, features = grads.shape
    width = features // 2

    def body(raw_ref, scale_ref, gain_ref, grad_ref, dot_ref, gain_grad_ref, totals):
        totals[...] = jnp.zeros_like(totals)
        for k in range(2):
            cut = slice(k * width, (k + 1) * width)
            terms = grad_ref[:, cut] * (raw_ref[:, cut] * scale_ref[:, k : k + 1])
            gain_grad_ref[:, cut] = jnp.sum(terms, axis=0, keepdims=True)
            totals[:, k : k + 1] = jnp.sum(terms * gain_ref[:, cut], axis=1, keepdims=True)
        dot_ref[...] = jnp.transpose(totals[...])[:2, :]

    return call_whole(
        body,
        [shape_of((2, rows), full), shape_of((1, features), full)],
        raw,
        scales,
        gains,
        grads,
        scalars=0,
        scratch=[pltpu.VMEM((rows, 128), full)],
    )


def project_input_grad(raw, scales, dots, gains, grads, grad_value, weights, slot_count, micro_count):
    rows, features = grad_value.shape[0], weights.shape[1]
    width = features // 3
    out_width = weights.shape[0]
    local_rows = rows // slot_count
    tile = tile_of(out_width)
    steps = out_width // tile

    def body(raw_ref, scale_ref, dot_ref, gain_ref, grad_ref, value_ref, weight_ref, low_ref, *out_refs):
        @pl.when(pl.program_id(0) == 0)
        def _():
            for k in range(2):
                cut = slice(k * width, (k + 1) * width)
                scale = scale_ref[:, k : k + 1]
                hat = raw_ref[:, cut] * scale
                grad_hat = grad_ref[:, cut] * gain_ref[:, cut]
                low_ref[:, cut] = (scale * (grad_hat - hat * dot_ref[:, k : k + 1])).astype(low)

        terms = dot_right_t(low_ref[...], weight_ref[:, : 2 * width])
        terms += dot_right_t(value_ref[...], weight_ref[:, 2 * width :])
        put_slots(out_refs, terms, micro_count)

    return call_grid(
        body,
        steps,
        [shape_of((rows, 2 * width), low)]
        + [shape_of((local_rows, out_width), low)] * slot_count,
        [
            fixed((rows, 2 * width)),
            fixed((rows, 2)),
            fixed((rows, 2)),
            fixed((1, 2 * width)),
            fixed((rows, 2 * width)),
            fixed((rows, width)),
            pl.BlockSpec((tile, features), lambda i: (i, 0)),
        ],
        [fixed((rows, 2 * width))]
        + [pl.BlockSpec((local_rows, tile), lambda i: (0, i))] * slot_count,
        raw,
        scales,
        dots,
        gains,
        grads,
        grad_value,
        weights,
        flops=2 * rows * features * out_width,
    )


def weight_term_slots(me, pairs, blocks):
    n = len(pairs)
    rows, width = pairs[0][0].shape
    sizes = [right.shape[1] for _, right in pairs]
    features = sum(sizes)
    part = width // blocks
    half = blocks // 2

    def body(me_ref, *refs):
        odd_ref, even_ref = refs[2 * n : 2 * n + 2]
        lefts = refs[2 * n + 2 :]
        step = pl.program_id(0)

        @pl.when(step == 0)
        def _():
            for left_t, left in zip(lefts, refs[:n]):
                left_t[...] = jnp.transpose(left[...])

        slot = jnp.where(step < half, 2 * step + 1, 2 * step - blocks)
        place = pl.multiple_of((me_ref[0] ^ slot) * part, part)
        first = 0
        for left_t, right, size in zip(lefts, refs[n : 2 * n], sizes):
            term = dot_plain(left_t[pl.ds(place, part), :], right[...]).astype(low)
            cut = slice(first, first + size)
            first += size

            @pl.when(step < half)
            def _():
                odd_ref[0, :, cut] = term

            @pl.when(step >= half)
            def _():
                even_ref[0, :, cut] = term

    return call_grid(
        body,
        blocks,
        [shape_of((half, part, features), low)] * 2,
        [scalar_spec]
        + [fixed((rows, width))] * n
        + [fixed((rows, size)) for size in sizes],
        [
            pl.BlockSpec((1, part, features), lambda i: (jnp.minimum(i, half - 1), 0, 0)),
            pl.BlockSpec((1, part, features), lambda i: (jnp.maximum(i - half, 0), 0, 0)),
        ],
        me,
        *[left for left, _ in pairs],
        *[right for _, right in pairs],
        scratch=[pltpu.VMEM((width, rows), low)] * n,
        flops=2 * rows * width * features,
    )


def add_cores(terms):
    odd, even = terms
    arrived = swap_cores(odd)
    return [even[k].astype(full) + arrived[k].astype(full) for k in range(even.shape[0])]


def add_chips(pairs):
    return sum_full(exchange_chips([pairs[0]] + [pair.astype(low) for pair in pairs[1:]]))


def send_views(me, raw, scales, gains, tables, heads_local):
    micro_count, rows = raw.shape[:2]
    blocks = micro_count * heads_local
    width = heads_local * HD

    def body(me_ref, *refs):
        raw_ref, scale_ref, gain_ref, cos_ref, sin_ref = refs[:5]
        out_refs = refs[5:]
        cosine, sine = cos_ref[...], sin_ref[...]
        for s in range(blocks):
            target = me_ref[0] ^ s
            column = pl.multiple_of((target % heads_local) * HD, HD)

            micro = target // heads_local
            for part in range(2):
                feature = pl.multiple_of(part * width + column, HD)
                values = raw_ref[micro, :, pl.ds(feature, HD)]
                values = values * scale_ref[micro, :, part : part + 1]
                values = values * gain_ref[:, pl.ds(feature, HD)]
                turned = values * cosine + pltpu.roll(values, HD // 2, 1) * sine
                out_refs[s][:, part * HD : (part + 1) * HD] = turned.astype(low)
            feature = pl.multiple_of(2 * width + column, HD)
            out_refs[s][:, 2 * HD :] = raw_ref[micro, :, pl.ds(feature, HD)].astype(low)

    return call_whole(
        body,
        [shape_of((rows, 3 * HD), low)] * blocks,
        me,
        raw,
        scales,
        gains,
        *tables,
    )


def masked_scores(k_rows, q_rows, key_seg, query_seg, key_pos=None, query_pos=None):
    scores = dot_right_t(k_rows, q_rows) * score_scale
    allowed = key_seg == query_seg
    if key_pos is not None:
        allowed = (allowed & (key_pos <= query_pos)) | (key_pos == query_pos)
    return jnp.where(allowed, scores, hidden_score)


def attention_forward(me, slots, key_seg, key_pos, query_seg, query_pos):
    blocks = len(slots)
    rows = slots[0].shape[0]
    length = blocks * rows

    def body(me_ref, *refs):
        slot_refs = refs[:blocks]
        ks_ref, kp_ref, qs_ref, qp_ref = refs[blocks : blocks + 4]
        out_refs = refs[blocks + 4 : 2 * blocks + 4]
        mixed_ref, norm_ref, q_all, k_all, v_all = refs[2 * blocks + 4 :]
        for s in range(blocks):
            place = pl.ds(pl.multiple_of((me_ref[0] ^ s) * rows, rows), rows)
            q_all[place, :] = slot_refs[s][:, :HD]
            k_all[place, :] = slot_refs[s][:, HD : 2 * HD]
            v_all[place, :] = slot_refs[s][:, 2 * HD :]
        for i in range(blocks):
            here = slice(i * rows, (i + 1) * rows)
            q_rows = q_all[here, :]
            query_seg_row = qs_ref[:, here]
            parts = [
                masked_scores(
                    k_all[here, :], q_rows, ks_ref[here, :], query_seg_row, kp_ref[here, :], qp_ref[:, here]
                )
            ]
            spans = [here]
            if i > 0:
                past = slice(0, i * rows)
                parts.append(masked_scores(k_all[past, :], q_rows, ks_ref[past, :], query_seg_row))
                spans.append(past)
            top = functools.reduce(
                jnp.maximum, [jnp.max(part, axis=0, keepdims=True) for part in parts]
            )
            total = jnp.zeros((1, rows), full)
            summed = jnp.zeros((HD, rows), full)
            for part, span in zip(parts, spans):
                expanded = jnp.exp(part - top)
                total = total + jnp.sum(expanded, axis=0, keepdims=True)
                summed = summed + dot_left_t(v_all[span, :], expanded.astype(low))
            mixed_ref[here, :] = jnp.transpose(summed / total)
            norm_ref[:, here] = top + jnp.log(total)
        for s in range(blocks):
            place = pl.ds(pl.multiple_of((me_ref[0] ^ s) * rows, rows), rows)
            out_refs[s][...] = mixed_ref[place, :].astype(low)

    return call_whole(
        body,
        [shape_of((rows, HD), low)] * blocks
        + [shape_of((length, HD), full), shape_of((1, length), full)],
        me,
        *slots,
        key_seg,
        key_pos,
        query_seg,
        query_pos,
        scratch=[pltpu.VMEM((length, HD), low)] * 3,
        flops=2 * length * length * HD,
    )


def attention_backward(me, slots, grad_slots, mixed, norm, key_seg, key_pos, query_seg, query_pos):
    blocks = len(slots)
    rows = slots[0].shape[0]
    length = blocks * rows

    def body(me_ref, *refs):
        slot_refs = refs[:blocks]
        grad_refs = refs[blocks : 2 * blocks]
        mixed_ref, norm_ref, ks_ref, kp_ref, qs_ref, qp_ref = refs[2 * blocks : 2 * blocks + 6]
        out_refs = refs[2 * blocks + 6 : 3 * blocks + 6]
        q_all, k_all, v_all, g_all, dq_all, dk_all, dv_all = refs[3 * blocks + 6 :]
        for s in range(blocks):
            place = pl.ds(pl.multiple_of((me_ref[0] ^ s) * rows, rows), rows)
            q_all[place, :] = slot_refs[s][:, :HD]
            k_all[place, :] = slot_refs[s][:, HD : 2 * HD]
            v_all[place, :] = slot_refs[s][:, 2 * HD :]
            g_all[place, :] = grad_refs[s][...]
        for i in range(blocks):
            here = slice(i * rows, (i + 1) * rows)
            q_rows = q_all[here, :]
            g_rows = g_all[here, :]
            query_seg_row = qs_ref[:, here]
            norm_row = norm_ref[:, here]
            delta = jnp.sum(
                jnp.transpose(g_rows.astype(full) * mixed_ref[here, :]), axis=0, keepdims=True
            )
            spans = [here] + ([slice(0, i * rows)] if i > 0 else [])
            grad_query = jnp.zeros((HD, rows), full)
            for n, span in enumerate(spans):
                k_rows = k_all[span, :]
                if n == 0:
                    scores = masked_scores(
                        k_rows, q_rows, ks_ref[span, :], query_seg_row, kp_ref[span, :], qp_ref[:, here]
                    )
                else:
                    scores = masked_scores(k_rows, q_rows, ks_ref[span, :], query_seg_row)
                weights = jnp.exp(scores - norm_row)
                grad_probs = dot_right_t(v_all[span, :], g_rows)
                grad_scores = (weights * (grad_probs - delta)).astype(low)
                key_term = dot_plain(grad_scores, q_rows)
                value_term = dot_plain(weights.astype(low), g_rows)
                if n == 0:
                    dk_all[span, :] = key_term
                    dv_all[span, :] = value_term
                else:
                    dk_all[span, :] += key_term
                    dv_all[span, :] += value_term
                grad_query = grad_query + dot_left_t(k_rows, grad_scores)
            dq_all[here, :] = jnp.transpose(grad_query)
        for s in range(blocks):
            place = pl.ds(pl.multiple_of((me_ref[0] ^ s) * rows, rows), rows)
            out_refs[s][:, :HD] = (dq_all[place, :] * score_scale).astype(low)
            out_refs[s][:, HD : 2 * HD] = (dk_all[place, :] * score_scale).astype(low)
            out_refs[s][:, 2 * HD :] = dv_all[place, :].astype(low)

    return call_whole(
        body,
        [shape_of((rows, 3 * HD), low)] * blocks,
        me,
        *slots,
        *grad_slots,
        mixed,
        norm,
        key_seg,
        key_pos,
        query_seg,
        query_pos,
        scratch=[pltpu.VMEM((length, HD), low)] * 4 + [pltpu.VMEM((length, HD), full)] * 3,
        flops=5 * length * length * HD,
    )


def assemble_mixed(me, slots, micro_count, heads_local):
    rows = slots[0].shape[0]
    blocks = len(slots)

    def body(me_ref, *refs):
        out_ref = refs[blocks]
        for s in range(blocks):
            source = me_ref[0] ^ s
            column = pl.multiple_of((source % heads_local) * HD, HD)
            out_ref[source // heads_local, :, pl.ds(column, HD)] = refs[s][...]

    return call_whole(
        body, [shape_of((micro_count, rows, heads_local * HD), low)], me, *slots
    )[0]


def split_mixed(me, slots, micro_count, heads_local):
    count = len(slots)
    rows = slots[0].shape[0] // micro_count
    blocks = micro_count * heads_local

    def body(me_ref, *refs):
        for t in range(blocks):
            target = me_ref[0] ^ t
            column = pl.multiple_of((target % heads_local) * HD, HD)
            first = pl.multiple_of((target // heads_local) * rows, rows)
            for s in range(count):
                refs[count + t][s * rows : (s + 1) * rows, :] = refs[s][
                    pl.ds(first, rows), pl.ds(column, HD)
                ]

    return call_whole(body, [shape_of((count * rows, HD), low)] * blocks, me, *slots)


def receive_grads(me, slots, tables, micro_count, heads_local):
    rows = slots[0].shape[0]
    blocks = len(slots)
    width = heads_local * HD

    def body(me_ref, *refs):
        cos_ref, sin_ref, norm_ref, value_ref = refs[blocks:]
        cosine, sine = cos_ref[...], sin_ref[...]
        for s in range(blocks):
            source = me_ref[0] ^ s
            micro = source // heads_local
            column = pl.multiple_of((source % heads_local) * HD, HD)
            for part in range(2):
                grads = refs[s][:, part * HD : (part + 1) * HD].astype(full)
                turned = grads * cosine - pltpu.roll(grads, HD // 2, 1) * sine
                norm_ref[micro, :, pl.ds(part * width + column, HD)] = turned
            value_ref[micro, :, pl.ds(column, HD)] = refs[s][:, 2 * HD :]

    return call_whole(
        body,
        [
            shape_of((micro_count, rows, 2 * width), full),
            shape_of((micro_count, rows, width), low),
        ],
        me,
        *slots,
        *tables,
    )


def turn(values, tables):
    return values * tables[0][:, None, :] + jnp.roll(values, HD // 2, axis=-1) * tables[1][:, None, :]


def turn_back(grads, tables):
    return grads * tables[0][:, None, :] - jnp.roll(grads, HD // 2, axis=-1) * tables[1][:, None, :]


def block_scores(query_view, key_rows, query_mark, key_mark):
    scores = score_scale * jnp.einsum(
        "qhd,khd->hqk", query_view, key_rows, preferred_element_type=full
    )
    query_seg, query_pos = query_mark
    key_seg, key_pos = key_mark
    allowed = (query_seg[:, None] == key_seg[None, :]) & (key_pos[None, :] <= query_pos[:, None])
    allowed = allowed | (key_pos[None, :] == query_pos[:, None])
    return jnp.where(allowed[None], scores, hidden_score)


def gathered_forward(query_view, query_mark, stacked):
    rows, heads = query_view.shape[:2]

    def step(running, block):
        key_rows, value_rows, key_seg, key_pos = block
        top, total, summed = running
        scores = block_scores(query_view, key_rows, query_mark, (key_seg, key_pos))
        new_top = jnp.maximum(top, jnp.max(scores, axis=-1))
        shrink = jnp.exp(top - new_top)
        expanded = jnp.where(scores > hidden_score, jnp.exp(scores - new_top[..., None]), 0.0)
        new_total = total * shrink + jnp.sum(expanded, axis=-1)
        new_summed = summed * shrink[..., None] + jnp.einsum(
            "hqk,khd->hqd", expanded.astype(low), value_rows, preferred_element_type=full
        )
        return ((new_top, new_total, new_summed), None)

    start = (
        jnp.full((heads, rows), hidden_score, full),
        jnp.zeros((heads, rows), full),
        jnp.zeros((heads, rows, HD), full),
    )
    top, total, summed = lax.scan(step, start, stacked)[0]
    return jnp.swapaxes(summed / total[..., None], 0, 1), top + jnp.log(total)


def gathered_backward(query_view, grad_view, mixed, norm, query_mark, stacked):
    delta = jnp.sum(grad_view.astype(full) * mixed, axis=2).T

    def step(running, block):
        key_rows, value_rows, key_seg, key_pos = block
        scores = block_scores(query_view, key_rows, query_mark, (key_seg, key_pos))
        weights = jnp.exp(scores - norm[..., None])
        grad_probs = jnp.einsum("qhd,khd->hqk", grad_view, value_rows, preferred_element_type=full)
        grad_scores = (weights * (grad_probs - delta[..., None])).astype(low)
        grad_query = running + jnp.einsum(
            "hqk,khd->qhd", grad_scores, key_rows, preferred_element_type=full
        )
        grad_keys = jnp.einsum("hqk,qhd->khd", grad_scores, query_view, preferred_element_type=full)
        grad_values = jnp.einsum(
            "hqk,qhd->khd", weights.astype(low), grad_view, preferred_element_type=full
        )
        return (
            grad_query,
            jnp.concatenate([grad_keys * score_scale, grad_values], axis=1).astype(low),
        )

    grad_query, key_terms = lax.scan(step, jnp.zeros(query_view.shape, full), stacked)
    return grad_query * score_scale, key_terms


class GatheredAttention:
    def __init__(self, raw, scales, gains, tables, codes, positions):
        blocks, rows = positions.shape
        self.tables, self.rows = tables, rows
        width = gains.shape[1] // 2
        shape = (rows, width // HD, HD)
        self.sets = []
        for m in range(raw.shape[0]):
            values = raw[m]
            views = []
            for part in range(2):
                cut = values[:, part * width : (part + 1) * width]
                normed = cut * scales[m, :, part : part + 1] * gains[:, part * width : (part + 1) * width]
                views.append(turn(normed.reshape(shape), tables).astype(low))
            value_view = values[:, 2 * width :].astype(low).reshape(shape)
            seg_all = (codes[m] // 2).reshape(blocks, rows)
            key_seg = jnp.where(codes[m] % 2 == 1, codes[m] // 2, -1).reshape(blocks, rows)
            place = lax.axis_index("blk")
            mark = tuple(
                lax.dynamic_index_in_dim(mark, place, 0, keepdims=False)
                for mark in (seg_all, positions)
            )
            stacked = (
                lax.all_gather(views[1], "blk"),
                lax.all_gather(value_view, "blk"),
                key_seg,
                positions,
            )
            self.sets.append((views[0], mark, stacked))
        self.slots = [one[2][0] for one in self.sets]

    def forward(self):
        results = [gathered_forward(*one) for one in self.sets]
        self.kept = results
        return jnp.stack(
            [mixed.reshape(self.rows, -1).astype(low) for mixed, norm in results]
        )

    def backward(self, grad_parts, *others):
        grad_mixed = jnp.stack(grad_parts).reshape(len(grad_parts), len(self.sets), -1, grad_parts[0].shape[1])
        grad_mixed = grad_mixed.swapaxes(0, 1).reshape(len(self.sets), self.rows, -1)
        norms, values = [], []
        for m, (view, mark, stacked) in enumerate(self.sets):
            grad_query, terms = gathered_backward(
                view, grad_mixed[m].reshape(view.shape), *self.kept[m], mark, stacked
            )
            own = lax.psum_scatter(terms, "blk", scatter_dimension=0, tiled=False)
            heads = view.shape[1]
            both = [turn_back(grad_query, self.tables)]
            both.append(turn_back(own[:, :heads].astype(full), self.tables))
            norms.append(jnp.concatenate([g.reshape(self.rows, -1) for g in both], axis=1))
            values.append(own[:, heads:].reshape(self.rows, -1))
        return jnp.stack(norms), jnp.stack(values)


class ExchangedAttention:
    def __init__(self, raw, scales, gains, tables, codes, positions):
        self.blocks, self.tables = positions.shape[0], tables
        self.heads = gains.shape[1] // (2 * HD)
        self.micro_count = raw.shape[0]
        place = lax.axis_index("blk")
        self.me = place.astype(jnp.int32).reshape(1)
        self.slots = exchange_slots(
            send_views(self.me, raw, scales, gains, tables, self.heads), "blk"
        )
        codes = lax.dynamic_index_in_dim(codes, place // self.heads, 0, keepdims=False)
        seg_all = codes // 2
        seg_key = jnp.where(codes % 2 == 1, seg_all, -1)
        pos_all = positions.reshape(-1)
        self.marks = (seg_key[:, None], pos_all[:, None], seg_all[None, :], pos_all[None, :])

    def forward(self):
        results = attention_forward(self.me, self.slots, *self.marks)
        self.kept = results[self.blocks :]
        return assemble_mixed(
            self.me,
            exchange_slots(results[: self.blocks], "blk"),
            self.micro_count,
            self.heads,
        )

    def backward(self, grad_parts, *others):
        grad_slots = exchange_slots(
            split_mixed(self.me, grad_parts, self.micro_count, self.heads), "blk"
        )
        self.arrived = grad_slots[1:]
        back_slots = exchange_slots(
            attention_backward(self.me, self.slots, grad_slots, *self.kept, *self.marks), "blk"
        )
        back_slots = after(back_slots, *others)
        return receive_grads(self.me, back_slots, self.tables, self.micro_count, self.heads)


def on_device(
    tokens,
    cotangent,
    segments,
    padding,
    query_weight,
    key_weight,
    value_weight,
    output_weight,
    query_gain,
    key_gain,
    attn_gain,
    gate_weight,
    up_weight,
    down_weight,
    ffn_gain,
):
    micro_count, local_rows, model_width = tokens.shape
    blocks = lax.axis_size("blk")
    head_size = lax.axis_size("head")
    group_rows = local_rows * head_size
    width = query_weight.shape[1]
    heads_local = width // HD
    block_index = lax.axis_index("blk")
    head_index = lax.axis_index("head")
    me = block_index.astype(jnp.int32).reshape(1)
    slot_owner = head_index ^ jnp.arange(head_size, dtype=jnp.int32)
    group_order = (
        slot_owner[:, None] * local_rows + jnp.arange(local_rows, dtype=jnp.int32)[None, :]
    ).reshape(group_rows)
    tables = rotary_tables(block_index * group_rows + group_order)

    def gather_weights(*parts):
        return lax.all_gather(jnp.concatenate(parts, axis=1), "blk", axis=0, tiled=True)

    qkv_full = gather_weights(query_weight, key_weight, value_weight)
    output_full_t = gather_weights(output_weight.T)
    ffn_full = gather_weights(gate_weight, up_weight, down_weight.T)

    def by_micro(values):
        return values.reshape(micro_count, -1, values.shape[-1])

    def all_rows(values):
        return values.reshape(-1, values.shape[-1])

    def sum_token_heads(values, others=None):
        sums, others = sum_heads(values.reshape(2 * micro_count, group_rows), others)
        return sums.reshape(2, micro_count * group_rows).T, others

    token_rows, raw, squares = project_qkv(gather_parts(all_rows(tokens)), qkv_full, micro_count)
    codes = jnp.concatenate(gather_slots(segments * 2 + padding, "head"), axis=1)
    codes = gather_doubling(codes, "blk")
    codes = codes[block_index ^ jnp.arange(blocks, dtype=jnp.int32)].swapaxes(0, 1)

    scales = lax.rsqrt(sum_token_heads(squares)[0] / model_width + epsilon)
    gain_row = jnp.concatenate([query_gain, key_gain])[None, :]
    positions = jnp.arange(blocks, dtype=jnp.int32)[:, None] * group_rows + group_order[None, :]
    exchanged = blocks == micro_count * heads_local and blocks & (blocks - 1) == 0
    attention = (ExchangedAttention if exchanged else GatheredAttention)(
        by_micro(raw), by_micro(scales), gain_row, tables, codes.reshape(micro_count, -1), positions
    )
    output_parts = gather_slots(after(output_weight.T, attention.slots[1]), "head")
    mixed = attention.forward()

    attn_gain, ffn_gain = attn_gain[None, :], ffn_gain[None, :]
    token_own, grad_own = all_rows(tokens), all_rows(cotangent)
    arrived = reduce_parts(project_output(mixed, output_full_t, head_size))
    hidden, hidden_low, attn_hat, attn_scale = after_attention(arrived, token_own, attn_gain)
    (hidden_rows, gate, up, middle_rows), slots = ffn_forward(
        gather_parts(hidden_low), ffn_full, micro_count
    )
    output_all_t = gather_weights(*after(output_parts, gate))
    output, grad_down, ffn_gain_grad = after_ffn(reduce_parts(slots), hidden, grad_own, ffn_gain)
    grad_parts = gather_parts(grad_down)
    grad_rows = join_rows(grad_parts, micro_count)
    down_terms = ffn_weight_term([], 0, 1, [grad_rows], [middle_rows])
    (_, grad_gate, grad_up), slots = ffn_backward(
        grad_parts, after(gate, down_terms), up, ffn_full, micro_count
    )
    arrived = reduce_parts(slots)
    grad_hidden, grad_attn, attn_gain_grad = before_attention(
        arrived, grad_own, attn_hat, attn_scale, attn_gain
    )
    ffn_terms = ffn_weight_term([], 0, 2, [hidden_rows], [grad_gate])
    ffn_terms = ffn_weight_term([ffn_terms], 1, 2, [hidden_rows], [grad_up])
    ffn_terms = after(ffn_terms, *arrived)
    down_grads = lax.psum_scatter(down_terms, "blk", scatter_dimension=0, tiled=True)
    ffn_grads = widen_ffn(
        lax.psum_scatter(ffn_terms, "blk", scatter_dimension=0, tiled=True), down_grads
    )

    grad_parts = exchange_slots(project_mixed_grad(grad_attn, output_all_t, head_size), "head")
    grad_attn_parts = gather_parts(after(grad_attn, *grad_parts[1:]))
    grad_norm, grad_value = attention.backward(grad_parts, *grad_attn_parts[1:])
    grad_attn_rows = join_rows(grad_attn_parts, micro_count)
    grad_norm, grad_value = all_rows(grad_norm), all_rows(grad_value)
    dots, qk_gain_grad = norm_gradients(raw, scales, gain_row, grad_norm)
    dots, gain_grads = sum_token_heads(
        dots, jnp.concatenate([attn_gain_grad, ffn_gain_grad], axis=1)[0]
    )
    mean_dots = dots / model_width
    gain_grads = jnp.concatenate([gain_grads, qk_gain_grad[0]])
    early_terms = weight_term_slots(
        me, [(grad_attn_rows, all_rows(mixed)), (token_rows, grad_value)], blocks
    )
    mean_dots = after(mean_dots, *early_terms)
    results = project_input_grad(
        raw, scales, mean_dots, gain_row, grad_norm, grad_value, qkv_full, head_size, micro_count
    )
    input_parts = exchange_slots(results[1:], "head")
    early_grads = add_chips(add_cores(early_terms))
    output_grad = early_grads[:, :width].T
    qk_terms = weight_term_slots(me, [(token_rows, results[0])], blocks)
    qk_pairs = add_cores(qk_terms)
    gain_grads = sum_doubling(after(gain_grads, *qk_terms), "blk")
    norm_gain_grads = gain_grads[: 2 * model_width]
    qk_gain_grad = gain_grads[2 * model_width :]
    qk_slots = exchange_chips([qk_pairs[0]] + [pair.astype(low) for pair in qk_pairs[1:]])
    input_grad = sum_full(after(input_parts, *qk_slots[1:])) + grad_hidden
    qk_grad = sum_full(after(qk_slots, ffn_grads, output_grad))
    return (
        by_micro(output),
        by_micro(input_grad),
        qk_grad[:, :width],
        qk_grad[:, width:],
        early_grads[:, width:],
        output_grad,
        qk_gain_grad[:width],
        qk_gain_grad[width:],
        norm_gain_grads[:model_width],
        *ffn_grads,
        norm_gain_grads[model_width:],
    )


def solution(mesh):
    return jax.shard_map(
        on_device,
        mesh=mesh,
        in_specs=(
            P(None, ("blk", "head"), None),
            P(None, ("blk", "head"), None),
            P(None, ("blk", "head")),
            P(None, ("blk", "head")),
            P("blk", "head"),
            P("blk", "head"),
            P("blk", "head"),
            P("head", "blk"),
            P("head"),
            P("head"),
            P(),
            P("blk", "head"),
            P("blk", "head"),
            P("head", "blk"),
            P(),
        ),
        out_specs=(
            P(None, ("blk", "head"), None),
            P(None, ("blk", "head"), None),
            P("blk", "head"),
            P("blk", "head"),
            P("blk", "head"),
            P("head", "blk"),
            P("head"),
            P("head"),
            P(),
            P("blk", "head"),
            P("blk", "head"),
            P("head", "blk"),
            P(),
        ),
        check_vma=False,
    )
```

```python
import functools
import math

import jax
import jax.numpy as jnp
from jax import lax
from jax.experimental import pallas as pl
from jax.experimental.pallas import tpu as pltpu
from jax.sharding import PartitionSpec as P

HD = 128

epsilon = 1e-06
theta = 500000.0
widest = 512
score_scale = HD ** (-0.5)
hidden_score = -1e30
low = jnp.bfloat16
full = jnp.float32
vmem_grant = 56 * 1024 * 1024


def dot_plain(left_side, right_side):
    return jnp.dot(left_side, right_side, preferred_element_type=full)


def dot_right_t(left_side, right_side):
    return lax.dot_general(
        left_side, right_side, (((1,), (1,)), ((), ())), preferred_element_type=full
    )


def dot_left_t(left_side, right_side):
    return lax.dot_general(
        left_side, right_side, (((0,), (0,)), ((), ())), preferred_element_type=full
    )


def rms_scale(values):
    return lax.rsqrt(jnp.mean(values * values, axis=-1, keepdims=True) + epsilon)


def xor_pairs(size, mask):
    return [(i, i ^ mask) for i in range(size)]


def gather_slots(values, axis):
    size = lax.axis_size(axis)
    return [values] + [lax.ppermute(values, axis, xor_pairs(size, s)) for s in range(1, size)]


def exchange_slots(slots, axis):
    size = lax.axis_size(axis)
    return [slots[0]] + [
        lax.ppermute(slots[s], axis, xor_pairs(size, s)) for s in range(1, size)
    ]


def gather_doubling(values, axis):
    held = values[None]
    step = 1
    while step < lax.axis_size(axis):
        arrived = lax.ppermute(held, axis, xor_pairs(lax.axis_size(axis), step))
        held = jnp.concatenate([held, arrived], axis=0)
        step *= 2
    return held


def sum_doubling(values, axis):
    step = 1
    while step < lax.axis_size(axis):
        values = values + lax.ppermute(values, axis, xor_pairs(lax.axis_size(axis), step))
        step *= 2
    return values


def after(values, *others):
    return lax.optimization_barrier((values, others))[0]


inward = [(0, 1), (3, 2)]
outward = [(1, 0), (2, 3)]
middle = [(1, 2), (2, 1)]


def send_rows(values, pairs):
    return lax.ppermute(values, "head", pairs)


def gather_parts(values):
    if lax.axis_size("head") != 4:
        return gather_slots(values, "head")
    second = send_rows(values, xor_pairs(4, 2))
    first = send_rows(values, xor_pairs(4, 1))
    across = send_rows(values, middle)
    return [values, first, second, across, send_rows(second, outward)]


def layout_of(count):
    return [(0,), (1,), (2,), (3, 4)] if count == 5 else [(s,) for s in range(count)]


def reduce_parts(slots):
    if lax.axis_size("head") != 4:
        return exchange_slots(slots, "head")
    arrived = send_rows(slots[3], inward)
    first = send_rows(slots[1], xor_pairs(4, 1))
    across = send_rows(slots[3], middle)
    passed = (slots[2].astype(full) + arrived.astype(full)).astype(low)
    return [slots[0], first, across, send_rows(passed, xor_pairs(4, 2))]


def exchange_chips(slots):
    size = lax.axis_size("blk")
    return [slots[0]] + [
        lax.ppermute(slots[m], "blk", xor_pairs(size, 2 * m)) for m in range(1, size // 2)
    ]


def exchange_blocks(slots):
    size = len(slots)
    if size != 8:
        return exchange_slots(slots, "blk")
    arrived = {s: lax.ppermute(slots[s], "blk", xor_pairs(size, s)) for s in range(2, size - 1)}
    for s in (size - 1, 1):
        arrived[s] = lax.ppermute(after(slots[s], arrived[2]), "blk", xor_pairs(size, s))
    return [slots[0]] + [arrived[s] for s in range(1, size)]


def swap_cores(values):
    return lax.ppermute(values, "blk", xor_pairs(lax.axis_size("blk"), 1))


def sum_full(arrays):
    return sum(array.astype(full) for array in arrays)


def sum_heads(values, others=None):
    size = lax.axis_size("head")
    count = values.size
    sent = values.reshape(-1)
    if others is not None:
        sent = jnp.concatenate([sent, others])
    total = 0.0
    for s, arrived in enumerate(gather_slots(sent, "head")):
        slots = jnp.split(arrived[:count].reshape(values.shape), size, axis=1)
        ordered = jnp.concatenate([slots[t ^ s] for t in range(size)], axis=1)
        total = total + jnp.concatenate([ordered.reshape(-1), arrived[count:]])
    return total[:count].reshape(values.shape), total[count:]


def rotary_tables(positions):
    half_size = HD // 2
    inverse = theta ** (-2.0 * jnp.arange(half_size, dtype=jnp.int32).astype(full) / HD)
    angles = positions.astype(full)[:, None] * inverse[None, :]
    cosine, sine = jnp.cos(angles), jnp.sin(angles)
    return (
        jnp.concatenate([cosine, cosine], axis=1),
        jnp.concatenate([-sine, sine], axis=1),
    )


def shape_of(shape, dtype):
    return jax.ShapeDtypeStruct(shape, dtype)


def sizes_of(arrays):
    return sum(a.size * a.dtype.itemsize for a in arrays)


def call_whole(body, outs, *args, scalars=1, scratch=(), flops=0):
    return pl.pallas_call(
        body,
        out_shape=outs,
        in_specs=[pl.BlockSpec(memory_space=pltpu.SMEM)] * scalars
        + [pl.BlockSpec(memory_space=pltpu.VMEM)] * (len(args) - scalars),
        out_specs=[pl.BlockSpec(memory_space=pltpu.VMEM)] * len(outs),
        scratch_shapes=list(scratch),
        compiler_params=pltpu.CompilerParams(vmem_limit_bytes=vmem_grant),
        cost_estimate=pl.CostEstimate(
            flops=flops,
            bytes_accessed=sizes_of(args) + sizes_of(outs),
            transcendentals=0,
        ),
    )(*args)


def call_grid(body, steps, outs, in_specs, out_specs, *args, scratch=(), flops=0):
    return pl.pallas_call(
        body,
        grid=(steps,),
        out_shape=outs,
        in_specs=in_specs,
        out_specs=out_specs,
        scratch_shapes=list(scratch),
        compiler_params=pltpu.CompilerParams(vmem_limit_bytes=vmem_grant),
        cost_estimate=pl.CostEstimate(
            flops=flops, bytes_accessed=sizes_of(args) + sizes_of(outs), transcendentals=0
        ),
    )(*args)


def fixed(shape):
    return pl.BlockSpec(shape, lambda i: (0,) * len(shape))


scalar_spec = pl.BlockSpec(memory_space=pltpu.SMEM)


def tile_of(size):
    return math.gcd(size, widest)


def column_tile(rows, tile, first=0):
    return pl.BlockSpec((rows, tile), lambda i: (0, first + i))


def slot_cuts(micro_count, count, rows):
    for s in range(count):
        for m in range(micro_count):
            first = (m * count + s) * rows
            yield s, slice(m * rows, (m + 1) * rows), slice(first, first + rows)


def put_slots(out_refs, values, micro_count):
    rows = out_refs[0].shape[0] // micro_count
    for s, inner, outer in slot_cuts(micro_count, len(out_refs), rows):
        out_refs[s][inner, :] = values[outer].astype(out_refs[s].dtype)


def fill_rows(rows_ref, part_refs, micro_count):
    layout = layout_of(len(part_refs))
    rows = part_refs[0].shape[0] // micro_count
    for s, inner, outer in slot_cuts(micro_count, len(layout), rows):
        rows_ref[outer, :] = functools.reduce(
            jnp.add, [part_refs[part][inner, :] for part in layout[s]]
        )


def sum_slots(refs):
    return sum(ref[...].astype(full) for ref in refs)


def ffn_forward(slots, weights, micro_count):
    n = len(slots)
    local_rows, width = slots[0].shape
    count = len(layout_of(n))
    rows, hidden = count * local_rows, weights.shape[1] // 3
    tile = tile_of(hidden)
    steps = hidden // tile

    def body(*refs):
        wg_ref, wu_ref, wd_ref = refs[n : n + 3]
        rows_ref, gate_ref, up_ref, middle_ref = refs[n + 3 : n + 7]
        out_refs, total = refs[n + 7 : -1], refs[-1]
        step = pl.program_id(0)

        @pl.when(step == 0)
        def _():
            fill_rows(rows_ref, refs[:n], micro_count)

        values = rows_ref[...]
        gate = dot_plain(values, wg_ref[...])
        up = dot_plain(values, wu_ref[...])
        gate_ref[...] = gate.astype(low)
        up_ref[...] = up.astype(low)
        middle = (gate * jax.nn.sigmoid(gate) * up).astype(low)
        middle_ref[...] = middle
        term = dot_right_t(middle, wd_ref[...])

        @pl.when(step == 0)
        def _():
            total[...] = term

        @pl.when(step > 0)
        def _():
            total[...] += term

        @pl.when(step == steps - 1)
        def _():
            put_slots(out_refs, total[...], micro_count)

    results = call_grid(
        body,
        steps,
        [shape_of((rows, width), low)]
        + [shape_of((rows, hidden), low)] * 3
        + [shape_of((local_rows, width), low)] * count,
        [fixed((local_rows, width))] * n + [column_tile(width, tile, k * steps) for k in range(3)],
        [fixed((rows, width))] + [column_tile(rows, tile)] * 3 + [fixed((local_rows, width))] * count,
        *slots,
        weights,
        weights,
        weights,
        scratch=[pltpu.VMEM((rows, width), full)],
        flops=6 * rows * width * hidden,
    )
    return results[:4], results[4:]


def ffn_backward(slots, gate, up, weights, micro_count):
    n = len(slots)
    local_rows, width = slots[0].shape
    rows, hidden = gate.shape
    count = rows // local_rows
    tile = tile_of(hidden)
    steps = hidden // tile

    def body(*refs):
        gate_ref, up_ref, wg_ref, wu_ref, wd_ref = refs[n : n + 5]
        rows_ref, gg_ref, gu_ref = refs[n + 5 : n + 8]
        out_refs, total = refs[n + 8 : -1], refs[-1]
        step = pl.program_id(0)

        @pl.when(step == 0)
        def _():
            fill_rows(rows_ref, refs[:n], micro_count)

        grad_middle = dot_plain(rows_ref[...], wd_ref[...])
        gate_values = gate_ref[...].astype(full)
        sigmoid = jax.nn.sigmoid(gate_values)
        silu = gate_values * sigmoid
        grad_up = (grad_middle * silu).astype(low)
        grad_gate = (
            grad_middle * up_ref[...].astype(full) * (sigmoid + silu * (1.0 - sigmoid))
        ).astype(low)
        gg_ref[...] = grad_gate
        gu_ref[...] = grad_up
        term = dot_right_t(grad_gate, wg_ref[...]) + dot_right_t(grad_up, wu_ref[...])

        @pl.when(step == 0)
        def _():
            total[...] = term

        @pl.when(step > 0)
        def _():
            total[...] += term

        @pl.when(step == steps - 1)
        def _():
            put_slots(out_refs, total[...], micro_count)

    results = call_grid(
        body,
        steps,
        [shape_of((rows, width), low)]
        + [shape_of((rows, hidden), low)] * 2
        + [shape_of((local_rows, width), low)] * count,
        [fixed((local_rows, width))] * n
        + [column_tile(rows, tile)] * 2
        + [column_tile(width, tile, k * steps) for k in range(3)],
        [fixed((rows, width))] + [column_tile(rows, tile)] * 2 + [fixed((local_rows, width))] * count,
        *slots,
        gate,
        up,
        weights,
        weights,
        weights,
        scratch=[pltpu.VMEM((rows, width), full)],
        flops=6 * rows * width * hidden,
    )
    return results[:3], results[3:]


def ffn_weight_term(held, part, parts, lefts, rights):
    n = len(lefts)
    rows, width = lefts[0].shape
    hidden = rights[0].shape[1]
    tile = tile_of(hidden)
    steps = hidden // tile

    def body(*refs):
        out_ref, left_t = refs[-2:]

        @pl.when(pl.program_id(0) == 0)
        def _():
            for m in range(n):
                left_t[:, m * rows : (m + 1) * rows] = jnp.transpose(refs[m][...])

        right = jnp.concatenate([ref[...] for ref in refs[n : 2 * n]], axis=0)
        out_ref[...] = dot_plain(left_t[...], right).astype(low)

    shape = shape_of((width, parts * hidden), low)
    return pl.pallas_call(
        body,
        grid=(steps,),
        out_shape=shape,
        in_specs=[fixed((rows, width))] * n
        + [column_tile(rows, tile)] * n
        + [pl.BlockSpec(memory_space=pl.ANY)] * len(held),
        out_specs=column_tile(width, tile, part * steps),
        scratch_shapes=[pltpu.VMEM((width, n * rows), low)],
        input_output_aliases={2 * n: 0} if held else {},
        compiler_params=pltpu.CompilerParams(vmem_limit_bytes=vmem_grant),
        cost_estimate=pl.CostEstimate(
            flops=2 * n * rows * width * hidden,
            bytes_accessed=sizes_of(lefts) + width * hidden * 2,
            transcendentals=0,
        ),
    )(*lefts, *rights, *held)


def widen_ffn(grads, down_grads):
    rows, hidden = down_grads.shape

    def body(grad_ref, turned_ref, gate_ref, up_ref, down_ref):
        gate_ref[...] = grad_ref[:, :hidden].astype(full)
        up_ref[...] = grad_ref[:, hidden:].astype(full)
        down_ref[...] = jnp.transpose(turned_ref[...]).astype(full)

    return call_whole(
        body,
        [shape_of((rows, hidden), full)] * 2 + [shape_of((hidden, rows), full)],
        grads,
        down_grads,
        scalars=0,
    )


def after_attention(arrived, tokens, gain):
    n = len(arrived)

    def body(*refs):
        token_ref, gain_ref, hidden_ref, low_ref, hat_ref, scale_ref = refs[n:]
        attn = sum_slots(refs[:n])
        scale = rms_scale(attn)
        hat = attn * scale
        hidden = token_ref[...].astype(full) + hat * gain_ref[...]
        hidden_ref[...] = hidden
        low_ref[...] = hidden.astype(low)
        hat_ref[...] = hat
        scale_ref[...] = scale

    shape = tokens.shape
    return call_whole(
        body,
        [shape_of(shape, full), shape_of(shape, low), shape_of(shape, full), shape_of((shape[0], 1), full)],
        *arrived,
        tokens,
        gain,
        scalars=0,
    )


def after_ffn(arrived, hidden, cotangent, gain):
    n = len(arrived)

    def body(*refs):
        hidden_ref, grad_ref, gain_ref, out_ref, low_ref, gain_grad_ref = refs[n:]
        down = sum_slots(refs[:n])
        scale = rms_scale(down)
        hat = down * scale
        out_ref[...] = (hidden_ref[...] + hat * gain_ref[...]).astype(low)
        grad_out = grad_ref[...].astype(full)
        gain_grad_ref[...] = jnp.sum(grad_out * hat, axis=0, keepdims=True)
        grad = grad_out * gain_ref[...]
        low_ref[...] = (scale * (grad - hat * jnp.mean(grad * hat, axis=1, keepdims=True))).astype(low)

    shape = hidden.shape
    return call_whole(
        body,
        [shape_of(shape, low), shape_of(shape, low), shape_of((1, shape[1]), full)],
        *arrived,
        hidden,
        cotangent,
        gain,
        scalars=0,
    )


def before_attention(arrived, cotangent, hat, scale, gain):
    n = len(arrived)

    def body(*refs):
        grad_ref, hat_ref, scale_ref, gain_ref, hidden_ref, low_ref, gain_grad_ref = refs[n:]
        grad_hidden = sum_slots(refs[:n]) + grad_ref[...].astype(full)
        hidden_ref[...] = grad_hidden
        hat = hat_ref[...]
        gain_grad_ref[...] = jnp.sum(grad_hidden * hat, axis=0, keepdims=True)
        grad = grad_hidden * gain_ref[...]
        low_ref[...] = (
            scale_ref[...] * (grad - hat * jnp.mean(grad * hat, axis=1, keepdims=True))
        ).astype(low)

    shape = hat.shape
    return call_whole(
        body,
        [shape_of(shape, full), shape_of(shape, low), shape_of((1, shape[1]), full)],
        *arrived,
        cotangent,
        hat,
        scale,
        gain,
        scalars=0,
    )


def project_qkv(token_slots, weights, micro_count):
    count = len(token_slots)
    local_rows, width = token_slots[0].shape
    rows, features = len(layout_of(count)) * local_rows, weights.shape[1]
    part = features // 3
    tile = tile_of(part)
    steps = features // tile
    part_steps = part // tile

    def body(*refs):
        weight_ref, rows_ref, raw_ref, square_ref, totals = refs[count:]
        step = pl.program_id(0)

        @pl.when(step == 0)
        def _():
            fill_rows(rows_ref, refs[:count], micro_count)
            totals[...] = jnp.zeros_like(totals)

        raw = dot_plain(rows_ref[...], weight_ref[...])
        raw_ref[...] = raw
        sums = jnp.sum(raw * raw, axis=1, keepdims=True)
        for k in range(2):

            @pl.when(step // part_steps == k)
            def _():
                totals[:, k : k + 1] += sums

        @pl.when(step == steps - 1)
        def _():
            square_ref[...] = jnp.transpose(totals[...])[:2, :]

    return call_grid(
        body,
        steps,
        [shape_of((rows, width), low), shape_of((rows, features), full), shape_of((2, rows), full)],
        [fixed((local_rows, width))] * count + [column_tile(width, tile)],
        [fixed((rows, width)), column_tile(rows, tile), fixed((2, rows))],
        *token_slots,
        weights,
        scratch=[pltpu.VMEM((rows, 128), full)],
        flops=2 * rows * width * features,
    )


def project_output(mixed, weights_t, head_size):
    micro_count, rows, features = mixed.shape
    width = weights_t.shape[0]
    local_rows = micro_count * rows // head_size

    def body(mixed_ref, weight_ref, *out_refs):
        values = dot_right_t(mixed_ref[...].reshape(micro_count * rows, features), weight_ref[...])
        put_slots(out_refs, values, micro_count)

    return call_whole(
        body,
        [shape_of((local_rows, width), low)] * head_size,
        mixed,
        weights_t,
        scalars=0,
        flops=2 * micro_count * rows * width * features,
    )


def project_mixed_grad(grad_rows, weights_t, head_size):
    rows, width = grad_rows.shape
    features = weights_t.shape[1] // head_size

    def body(grad_ref, weight_ref, *out_refs):
        term = dot_plain(grad_ref[...], weight_ref[...]).astype(low)
        for s in range(head_size):

            @pl.when(pl.program_id(0) == s)
            def _():
                out_refs[s][...] = term

    return call_grid(
        body,
        head_size,
        [shape_of((rows, features), low)] * head_size,
        [fixed((rows, width)), column_tile(width, features)],
        [fixed((rows, features))] * head_size,
        grad_rows,
        weights_t,
        flops=2 * rows * width * weights_t.shape[1],
    )


def join_rows(parts, micro_count):
    rows, width = parts[0].shape
    count = len(parts)

    def body(*refs):
        fill_rows(refs[count], refs[:count], micro_count)

    return call_whole(
        body, [shape_of((len(layout_of(count)) * rows, width), low)], *parts, scalars=0
    )[0]


def norm_gradients(raw, scales, gains, grads):
    rows, features = grads.shape
    width = features // 2

    def body(raw_ref, scale_ref, gain_ref, grad_ref, dot_ref, gain_grad_ref, totals):
        totals[...] = jnp.zeros_like(totals)
        for k in range(2):
            cut = slice(k * width, (k + 1) * width)
            terms = grad_ref[:, cut] * (raw_ref[:, cut] * scale_ref[:, k : k + 1])
            gain_grad_ref[:, cut] = jnp.sum(terms, axis=0, keepdims=True)
            totals[:, k : k + 1] = jnp.sum(terms * gain_ref[:, cut], axis=1, keepdims=True)
        dot_ref[...] = jnp.transpose(totals[...])[:2, :]

    return call_whole(
        body,
        [shape_of((2, rows), full), shape_of((1, features), full)],
        raw,
        scales,
        gains,
        grads,
        scalars=0,
        scratch=[pltpu.VMEM((rows, 128), full)],
    )


def norm_backward(raw, scales, dots, gains, grads):
    rows, features = grads.shape
    width = features // 2

    def body(raw_ref, scale_ref, dot_ref, gain_ref, grad_ref, low_ref):
        for k in range(2):
            cut = slice(k * width, (k + 1) * width)
            scale = scale_ref[:, k : k + 1]
            hat = raw_ref[:, cut] * scale
            grad_hat = grad_ref[:, cut] * gain_ref[:, cut]
            low_ref[:, cut] = (scale * (grad_hat - hat * dot_ref[:, k : k + 1])).astype(low)

    return call_whole(
        body, [shape_of((rows, features), low)], raw, scales, dots, gains, grads, scalars=0
    )[0]


def project_input_grad(grad_qk, grad_value, weights, slot_count, micro_count):
    rows, features = grad_value.shape[0], weights.shape[1]
    width = features // 3
    out_width = weights.shape[0]
    local_rows = rows // slot_count
    tile = tile_of(out_width)
    steps = out_width // tile

    def body(qk_ref, value_ref, weight_ref, *out_refs):
        terms = dot_right_t(qk_ref[...], weight_ref[:, : 2 * width])
        terms += dot_right_t(value_ref[...], weight_ref[:, 2 * width :])
        put_slots(out_refs, terms, micro_count)

    return call_grid(
        body,
        steps,
        [shape_of((local_rows, out_width), low)] * slot_count,
        [
            fixed((rows, 2 * width)),
            fixed((rows, width)),
            pl.BlockSpec((tile, features), lambda i: (i, 0)),
        ],
        [column_tile(local_rows, tile)] * slot_count,
        grad_qk,
        grad_value,
        weights,
        flops=2 * rows * features * out_width,
    )


def weight_term_slots(me, pairs, blocks, place, places, held=()):
    n = len(pairs)
    rows, width = pairs[0][0].shape
    sizes = [right.shape[1] for _, right in pairs]
    features = sum(sizes)
    part = width // blocks
    half = blocks // 2

    def body(me_ref, *refs):
        odd_ref, even_ref = refs[-2 - n : -n]
        lefts = refs[-n:]
        step = pl.program_id(0)

        @pl.when(step == 0)
        def _():
            for left_t, left in zip(lefts, refs[:n]):
                left_t[...] = jnp.transpose(left[...])

        slot = jnp.where(step < half, 2 * step + 1, 2 * step - blocks)
        rows_at = pl.multiple_of((me_ref[0] ^ slot) * part, part)
        first = 0
        for left_t, right, size in zip(lefts, refs[n : 2 * n], sizes):
            term = dot_plain(left_t[pl.ds(rows_at, part), :], right[...]).astype(low)
            cut = slice(first, first + size)
            first += size

            @pl.when(step < half)
            def _():
                odd_ref[0, :, cut] = term

            @pl.when(step >= half)
            def _():
                even_ref[0, :, cut] = term

    outs = [shape_of((half, part, places * features), low)] * 2
    return pl.pallas_call(
        body,
        grid=(blocks,),
        out_shape=outs,
        in_specs=[scalar_spec]
        + [fixed((rows, width))] * n
        + [fixed((rows, size)) for size in sizes]
        + [pl.BlockSpec(memory_space=pl.ANY)] * len(held),
        out_specs=[
            pl.BlockSpec((1, part, features), lambda i: (jnp.minimum(i, half - 1), 0, place)),
            pl.BlockSpec((1, part, features), lambda i: (jnp.maximum(i - half, 0), 0, place)),
        ],
        scratch_shapes=[pltpu.VMEM((width, rows), low)] * n,
        input_output_aliases={1 + 2 * n + k: k for k in range(len(held))},
        compiler_params=pltpu.CompilerParams(vmem_limit_bytes=vmem_grant),
        cost_estimate=pl.CostEstimate(
            flops=2 * rows * width * features,
            bytes_accessed=n * rows * width * 2 + rows * features * 2 + width * features * 2,
            transcendentals=0,
        ),
    )(me, *[left for left, _ in pairs], *[right for _, right in pairs], *held)


def add_cores(terms, *others):
    odd, even = terms
    arrived = swap_cores(odd)
    even = after(even, *others) if others else even
    return [even[k].astype(full) + arrived[k].astype(full) for k in range(even.shape[0])]


def add_chips(pairs, *others):
    half = pairs[0].shape[1] // 2
    one, other = slice(0, half), slice(half, 2 * half)
    if len(pairs) != 4:
        slots = exchange_chips([pairs[0]] + [pair.astype(low) for pair in pairs[1:]])
        total = sum_full(slots)
        return total[:, one], total[:, other]
    along = [xor_pairs(8, 2), xor_pairs(8, 4)]
    sent = [
        jnp.stack([pairs[1][:, one], pairs[3][:, one]]).astype(low),
        jnp.stack([pairs[2][:, other], pairs[3][:, other]]).astype(low),
    ]
    arrived = [lax.ppermute(sent[k], "blk", along[k]).astype(full) for k in range(2)]
    sent = [
        (pairs[2][:, one] + arrived[0][1]).astype(low),
        (pairs[1][:, other] + arrived[1][1]).astype(low),
    ]
    sent = after(sent, *others)
    final = [lax.ppermute(sent[k], "blk", along[1 - k]).astype(full) for k in range(2)]
    return (
        pairs[0][:, one] + arrived[0][0] + final[0],
        pairs[0][:, other] + arrived[1][0] + final[1],
    )


def send_views(me, raw, scales, gains, tables, heads_local):
    micro_count, rows = raw.shape[:2]
    blocks = micro_count * heads_local
    width = heads_local * HD

    def body(me_ref, *refs):
        raw_ref, scale_ref, gain_ref, cos_ref, sin_ref = refs[:5]
        out_refs = refs[5:]
        cosine, sine = cos_ref[...], sin_ref[...]
        for s in range(blocks):
            target = me_ref[0] ^ s
            column = pl.multiple_of((target % heads_local) * HD, HD)

            micro = target // heads_local
            for part in range(2):
                feature = pl.multiple_of(part * width + column, HD)
                values = raw_ref[micro, :, pl.ds(feature, HD)]
                values = values * scale_ref[micro, :, part : part + 1]
                values = values * gain_ref[:, pl.ds(feature, HD)]
                turned = values * cosine + pltpu.roll(values, HD // 2, 1) * sine
                out_refs[s][:, part * HD : (part + 1) * HD] = turned.astype(low)
            feature = pl.multiple_of(2 * width + column, HD)
            out_refs[s][:, 2 * HD :] = raw_ref[micro, :, pl.ds(feature, HD)].astype(low)

    return call_whole(
        body,
        [shape_of((rows, 3 * HD), low)] * blocks,
        me,
        raw,
        scales,
        gains,
        *tables,
    )


def masked_scores(k_rows, q_rows, key_seg, query_seg, key_pos=None, query_pos=None):
    scores = dot_right_t(k_rows, q_rows) * score_scale
    allowed = key_seg == query_seg
    if key_pos is not None:
        allowed = (allowed & (key_pos <= query_pos)) | (key_pos == query_pos)
    return jnp.where(allowed, scores, hidden_score)


def attention_forward(me, slots, key_seg, key_pos, query_seg, query_pos):
    blocks = len(slots)
    rows = slots[0].shape[0]
    length = blocks * rows

    def body(me_ref, *refs):
        slot_refs = refs[:blocks]
        ks_ref, kp_ref, qs_ref, qp_ref = refs[blocks : blocks + 4]
        out_refs = refs[blocks + 4 : 2 * blocks + 4]
        mixed_ref, norm_ref, q_all, k_all, v_all = refs[2 * blocks + 4 :]
        for s in range(blocks):
            place = pl.ds(pl.multiple_of((me_ref[0] ^ s) * rows, rows), rows)
            q_all[place, :] = slot_refs[s][:, :HD]
            k_all[place, :] = slot_refs[s][:, HD : 2 * HD]
            v_all[place, :] = slot_refs[s][:, 2 * HD :]
        for i in range(blocks):
            here = slice(i * rows, (i + 1) * rows)
            q_rows = q_all[here, :]
            query_seg_row = qs_ref[:, here]
            parts = [
                masked_scores(
                    k_all[here, :], q_rows, ks_ref[here, :], query_seg_row, kp_ref[here, :], qp_ref[:, here]
                )
            ]
            spans = [here]
            if i > 0:
                past = slice(0, i * rows)
                parts.append(masked_scores(k_all[past, :], q_rows, ks_ref[past, :], query_seg_row))
                spans.append(past)
            top = functools.reduce(
                jnp.maximum, [jnp.max(part, axis=0, keepdims=True) for part in parts]
            )
            total = jnp.zeros((1, rows), full)
            summed = jnp.zeros((HD, rows), full)
            for part, span in zip(parts, spans):
                expanded = jnp.exp(part - top)
                total = total + jnp.sum(expanded, axis=0, keepdims=True)
                summed = summed + dot_left_t(v_all[span, :], expanded.astype(low))
            mixed_ref[here, :] = jnp.transpose(summed / total)
            norm_ref[:, here] = top + jnp.log(total)
        for s in range(blocks):
            place = pl.ds(pl.multiple_of((me_ref[0] ^ s) * rows, rows), rows)
            out_refs[s][...] = mixed_ref[place, :].astype(low)

    return call_whole(
        body,
        [shape_of((rows, HD), low)] * blocks
        + [shape_of((length, HD), full), shape_of((1, length), full)],
        me,
        *slots,
        key_seg,
        key_pos,
        query_seg,
        query_pos,
        scratch=[pltpu.VMEM((length, HD), low)] * 3,
        flops=2 * length * length * HD,
    )


def attention_backward(me, slots, grad_slots, mixed, norm, key_seg, key_pos, query_seg, query_pos):
    blocks = len(slots)
    rows = slots[0].shape[0]
    length = blocks * rows

    def body(me_ref, *refs):
        slot_refs = refs[:blocks]
        grad_refs = refs[blocks : 2 * blocks]
        mixed_ref, norm_ref, ks_ref, kp_ref, qs_ref, qp_ref = refs[2 * blocks : 2 * blocks + 6]
        out_refs = refs[2 * blocks + 6 : 3 * blocks + 6]
        q_all, k_all, v_all, g_all, dq_all, dk_all, dv_all = refs[3 * blocks + 6 :]
        for s in range(blocks):
            place = pl.ds(pl.multiple_of((me_ref[0] ^ s) * rows, rows), rows)
            q_all[place, :] = slot_refs[s][:, :HD]
            k_all[place, :] = slot_refs[s][:, HD : 2 * HD]
            v_all[place, :] = slot_refs[s][:, 2 * HD :]
            g_all[place, :] = grad_refs[s][...]
        for i in range(blocks):
            here = slice(i * rows, (i + 1) * rows)
            q_rows = q_all[here, :]
            g_rows = g_all[here, :]
            query_seg_row = qs_ref[:, here]
            norm_row = norm_ref[:, here]
            delta = jnp.sum(
                jnp.transpose(g_rows.astype(full) * mixed_ref[here, :]), axis=0, keepdims=True
            )
            spans = [here] + ([slice(0, i * rows)] if i > 0 else [])
            grad_query = jnp.zeros((HD, rows), full)
            for n, span in enumerate(spans):
                k_rows = k_all[span, :]
                if n == 0:
                    scores = masked_scores(
                        k_rows, q_rows, ks_ref[span, :], query_seg_row, kp_ref[span, :], qp_ref[:, here]
                    )
                else:
                    scores = masked_scores(k_rows, q_rows, ks_ref[span, :], query_seg_row)
                weights = jnp.exp(scores - norm_row)
                grad_probs = dot_right_t(v_all[span, :], g_rows)
                grad_scores = (weights * (grad_probs - delta)).astype(low)
                key_term = dot_plain(grad_scores, q_rows)
                value_term = dot_plain(weights.astype(low), g_rows)
                if n == 0:
                    dk_all[span, :] = key_term
                    dv_all[span, :] = value_term
                else:
                    dk_all[span, :] += key_term
                    dv_all[span, :] += value_term
                grad_query = grad_query + dot_left_t(k_rows, grad_scores)
            dq_all[here, :] = jnp.transpose(grad_query)
        for s in range(blocks):
            place = pl.ds(pl.multiple_of((me_ref[0] ^ s) * rows, rows), rows)
            out_refs[s][:, :HD] = (dq_all[place, :] * score_scale).astype(low)
            out_refs[s][:, HD : 2 * HD] = (dk_all[place, :] * score_scale).astype(low)
            out_refs[s][:, 2 * HD :] = dv_all[place, :].astype(low)

    return call_whole(
        body,
        [shape_of((rows, 3 * HD), low)] * blocks,
        me,
        *slots,
        *grad_slots,
        mixed,
        norm,
        key_seg,
        key_pos,
        query_seg,
        query_pos,
        scratch=[pltpu.VMEM((length, HD), low)] * 4 + [pltpu.VMEM((length, HD), full)] * 3,
        flops=5 * length * length * HD,
    )


def assemble_mixed(me, slots, micro_count, heads_local):
    rows = slots[0].shape[0]
    blocks = len(slots)

    def body(me_ref, *refs):
        out_ref = refs[blocks]
        for s in range(blocks):
            source = me_ref[0] ^ s
            column = pl.multiple_of((source % heads_local) * HD, HD)
            out_ref[source // heads_local, :, pl.ds(column, HD)] = refs[s][...]

    return call_whole(
        body, [shape_of((micro_count, rows, heads_local * HD), low)], me, *slots
    )[0]


def split_mixed(me, slots, micro_count, heads_local):
    count = len(slots)
    rows = slots[0].shape[0] // micro_count
    blocks = micro_count * heads_local

    def body(me_ref, *refs):
        for t in range(blocks):
            target = me_ref[0] ^ t
            column = pl.multiple_of((target % heads_local) * HD, HD)
            first = pl.multiple_of((target // heads_local) * rows, rows)
            for s in range(count):
                refs[count + t][s * rows : (s + 1) * rows, :] = refs[s][
                    pl.ds(first, rows), pl.ds(column, HD)
                ]

    return call_whole(body, [shape_of((count * rows, HD), low)] * blocks, me, *slots)


def receive_grads(me, slots, tables, micro_count, heads_local):
    rows = slots[0].shape[0]
    blocks = len(slots)
    width = heads_local * HD

    def body(me_ref, *refs):
        cos_ref, sin_ref, norm_ref, value_ref = refs[blocks:]
        cosine, sine = cos_ref[...], sin_ref[...]
        for s in range(blocks):
            source = me_ref[0] ^ s
            micro = source // heads_local
            column = pl.multiple_of((source % heads_local) * HD, HD)
            for part in range(2):
                grads = refs[s][:, part * HD : (part + 1) * HD].astype(full)
                turned = grads * cosine - pltpu.roll(grads, HD // 2, 1) * sine
                norm_ref[micro, :, pl.ds(part * width + column, HD)] = turned
            value_ref[micro, :, pl.ds(column, HD)] = refs[s][:, 2 * HD :]

    return call_whole(
        body,
        [
            shape_of((micro_count, rows, 2 * width), full),
            shape_of((micro_count, rows, width), low),
        ],
        me,
        *slots,
        *tables,
    )


def turn(values, tables):
    return values * tables[0][:, None, :] + jnp.roll(values, HD // 2, axis=-1) * tables[1][:, None, :]


def turn_back(grads, tables):
    return grads * tables[0][:, None, :] - jnp.roll(grads, HD // 2, axis=-1) * tables[1][:, None, :]


def block_scores(query_view, key_rows, query_mark, key_mark):
    scores = score_scale * jnp.einsum(
        "qhd,khd->hqk", query_view, key_rows, preferred_element_type=full
    )
    query_seg, query_pos = query_mark
    key_seg, key_pos = key_mark
    allowed = (query_seg[:, None] == key_seg[None, :]) & (key_pos[None, :] <= query_pos[:, None])
    allowed = allowed | (key_pos[None, :] == query_pos[:, None])
    return jnp.where(allowed[None], scores, hidden_score)


def gathered_forward(query_view, query_mark, stacked):
    rows, heads = query_view.shape[:2]

    def step(running, block):
        key_rows, value_rows, key_seg, key_pos = block
        top, total, summed = running
        scores = block_scores(query_view, key_rows, query_mark, (key_seg, key_pos))
        new_top = jnp.maximum(top, jnp.max(scores, axis=-1))
        shrink = jnp.exp(top - new_top)
        expanded = jnp.where(scores > hidden_score, jnp.exp(scores - new_top[..., None]), 0.0)
        new_total = total * shrink + jnp.sum(expanded, axis=-1)
        new_summed = summed * shrink[..., None] + jnp.einsum(
            "hqk,khd->hqd", expanded.astype(low), value_rows, preferred_element_type=full
        )
        return ((new_top, new_total, new_summed), None)

    start = (
        jnp.full((heads, rows), hidden_score, full),
        jnp.zeros((heads, rows), full),
        jnp.zeros((heads, rows, HD), full),
    )
    top, total, summed = lax.scan(step, start, stacked)[0]
    return jnp.swapaxes(summed / total[..., None], 0, 1), top + jnp.log(total)


def gathered_backward(query_view, grad_view, mixed, norm, query_mark, stacked):
    delta = jnp.sum(grad_view.astype(full) * mixed, axis=2).T

    def step(running, block):
        key_rows, value_rows, key_seg, key_pos = block
        scores = block_scores(query_view, key_rows, query_mark, (key_seg, key_pos))
        weights = jnp.exp(scores - norm[..., None])
        grad_probs = jnp.einsum("qhd,khd->hqk", grad_view, value_rows, preferred_element_type=full)
        grad_scores = (weights * (grad_probs - delta[..., None])).astype(low)
        grad_query = running + jnp.einsum(
            "hqk,khd->qhd", grad_scores, key_rows, preferred_element_type=full
        )
        grad_keys = jnp.einsum("hqk,qhd->khd", grad_scores, query_view, preferred_element_type=full)
        grad_values = jnp.einsum(
            "hqk,qhd->khd", weights.astype(low), grad_view, preferred_element_type=full
        )
        return (
            grad_query,
            jnp.concatenate([grad_keys * score_scale, grad_values], axis=1).astype(low),
        )

    grad_query, key_terms = lax.scan(step, jnp.zeros(query_view.shape, full), stacked)
    return grad_query * score_scale, key_terms


class GatheredAttention:
    def __init__(self, raw, scales, gains, tables, codes, positions):
        blocks, rows = positions.shape
        self.tables, self.rows = tables, rows
        width = gains.shape[1] // 2
        shape = (rows, width // HD, HD)
        self.sets = []
        for m in range(raw.shape[0]):
            values = raw[m]
            views = []
            for part in range(2):
                cut = values[:, part * width : (part + 1) * width]
                normed = cut * scales[m, :, part : part + 1] * gains[:, part * width : (part + 1) * width]
                views.append(turn(normed.reshape(shape), tables).astype(low))
            value_view = values[:, 2 * width :].astype(low).reshape(shape)
            seg_all = (codes[m] // 2).reshape(blocks, rows)
            key_seg = jnp.where(codes[m] % 2 == 1, codes[m] // 2, -1).reshape(blocks, rows)
            place = lax.axis_index("blk")
            mark = tuple(
                lax.dynamic_index_in_dim(mark, place, 0, keepdims=False)
                for mark in (seg_all, positions)
            )
            stacked = (
                lax.all_gather(views[1], "blk"),
                lax.all_gather(value_view, "blk"),
                key_seg,
                positions,
            )
            self.sets.append((views[0], mark, stacked))
        self.slots = [one[2][0] for one in self.sets]

    def forward(self):
        results = [gathered_forward(*one) for one in self.sets]
        self.kept = results
        return jnp.stack(
            [mixed.reshape(self.rows, -1).astype(low) for mixed, norm in results]
        )

    def backward(self, grad_parts, *others):
        grad_mixed = jnp.stack(grad_parts).reshape(len(grad_parts), len(self.sets), -1, grad_parts[0].shape[1])
        grad_mixed = grad_mixed.swapaxes(0, 1).reshape(len(self.sets), self.rows, -1)
        norms, values = [], []
        for m, (view, mark, stacked) in enumerate(self.sets):
            grad_query, terms = gathered_backward(
                view, grad_mixed[m].reshape(view.shape), *self.kept[m], mark, stacked
            )
            own = lax.psum_scatter(terms, "blk", scatter_dimension=0, tiled=False)
            heads = view.shape[1]
            both = [turn_back(grad_query, self.tables)]
            both.append(turn_back(own[:, :heads].astype(full), self.tables))
            norms.append(jnp.concatenate([g.reshape(self.rows, -1) for g in both], axis=1))
            values.append(own[:, heads:].reshape(self.rows, -1))
        return jnp.stack(norms), jnp.stack(values)


class ExchangedAttention:
    def __init__(self, raw, scales, gains, tables, codes, positions):
        self.blocks, self.tables = positions.shape[0], tables
        self.heads = gains.shape[1] // (2 * HD)
        self.micro_count = raw.shape[0]
        place = lax.axis_index("blk")
        self.me = place.astype(jnp.int32).reshape(1)
        self.slots = exchange_blocks(
            send_views(self.me, raw, scales, gains, tables, self.heads)
        )
        codes = lax.dynamic_index_in_dim(codes, place // self.heads, 0, keepdims=False)
        seg_all = codes // 2
        seg_key = jnp.where(codes % 2 == 1, seg_all, -1)
        pos_all = positions.reshape(-1)
        self.marks = (seg_key[:, None], pos_all[:, None], seg_all[None, :], pos_all[None, :])

    def forward(self):
        results = attention_forward(self.me, self.slots, *self.marks)
        self.kept = results[self.blocks :]
        return assemble_mixed(
            self.me,
            exchange_slots(results[: self.blocks], "blk"),
            self.micro_count,
            self.heads,
        )

    def backward(self, grad_parts, *others):
        grad_slots = exchange_slots(
            split_mixed(self.me, grad_parts, self.micro_count, self.heads), "blk"
        )
        self.arrived = grad_slots[1:]
        back_slots = exchange_slots(
            attention_backward(self.me, self.slots, grad_slots, *self.kept, *self.marks), "blk"
        )
        back_slots = after(back_slots, *others)
        return receive_grads(self.me, back_slots, self.tables, self.micro_count, self.heads)


def on_device(
    tokens,
    cotangent,
    segments,
    padding,
    query_weight,
    key_weight,
    value_weight,
    output_weight,
    query_gain,
    key_gain,
    attn_gain,
    gate_weight,
    up_weight,
    down_weight,
    ffn_gain,
):
    micro_count, local_rows, model_width = tokens.shape
    blocks = lax.axis_size("blk")
    head_size = lax.axis_size("head")
    group_rows = local_rows * head_size
    width = query_weight.shape[1]
    heads_local = width // HD
    block_index = lax.axis_index("blk")
    head_index = lax.axis_index("head")
    me = block_index.astype(jnp.int32).reshape(1)
    slot_owner = head_index ^ jnp.arange(head_size, dtype=jnp.int32)
    group_order = (
        slot_owner[:, None] * local_rows + jnp.arange(local_rows, dtype=jnp.int32)[None, :]
    ).reshape(group_rows)
    tables = rotary_tables(block_index * group_rows + group_order)

    def gather_weights(*parts):
        return lax.all_gather(jnp.concatenate(parts, axis=1), "blk", axis=0, tiled=True)

    qkv_full = gather_weights(query_weight, key_weight, value_weight)
    output_full_t = gather_weights(output_weight.T)
    ffn_full = gather_weights(gate_weight, up_weight, down_weight.T)

    def by_micro(values):
        return values.reshape(micro_count, -1, values.shape[-1])

    def all_rows(values):
        return values.reshape(-1, values.shape[-1])

    def sum_token_heads(values, others=None):
        sums, others = sum_heads(values.reshape(2 * micro_count, group_rows), others)
        return sums.reshape(2, micro_count * group_rows).T, others

    token_rows, raw, squares = project_qkv(gather_parts(all_rows(tokens)), qkv_full, micro_count)
    codes = jnp.concatenate(gather_slots(segments * 2 + padding, "head"), axis=1)
    codes = gather_doubling(codes, "blk")
    codes = codes[block_index ^ jnp.arange(blocks, dtype=jnp.int32)].swapaxes(0, 1)

    scales = lax.rsqrt(sum_token_heads(squares)[0] / model_width + epsilon)
    gain_row = jnp.concatenate([query_gain, key_gain])[None, :]
    positions = jnp.arange(blocks, dtype=jnp.int32)[:, None] * group_rows + group_order[None, :]
    exchanged = blocks == micro_count * heads_local and blocks & (blocks - 1) == 0
    attention = (ExchangedAttention if exchanged else GatheredAttention)(
        by_micro(raw), by_micro(scales), gain_row, tables, codes.reshape(micro_count, -1), positions
    )
    output_parts = gather_slots(after(output_weight.T, attention.slots[1]), "head")
    mixed = attention.forward()

    attn_gain, ffn_gain = attn_gain[None, :], ffn_gain[None, :]
    token_own, grad_own = all_rows(tokens), all_rows(cotangent)
    arrived = reduce_parts(project_output(mixed, output_full_t, head_size))
    hidden, hidden_low, attn_hat, attn_scale = after_attention(arrived, token_own, attn_gain)
    (hidden_rows, gate, up, middle_rows), slots = ffn_forward(
        gather_parts(hidden_low), ffn_full, micro_count
    )
    output_all_t = gather_weights(*after(output_parts, gate))
    output, grad_down, ffn_gain_grad = after_ffn(reduce_parts(slots), hidden, grad_own, ffn_gain)
    grad_parts = gather_parts(grad_down)
    grad_rows = join_rows(grad_parts, micro_count)
    down_terms = ffn_weight_term([], 0, 1, [grad_rows], [middle_rows])
    (_, grad_gate, grad_up), slots = ffn_backward(
        grad_parts, after(gate, down_terms), up, ffn_full, micro_count
    )
    arrived = reduce_parts(slots)
    grad_hidden, grad_attn, attn_gain_grad = before_attention(
        arrived, grad_own, attn_hat, attn_scale, attn_gain
    )
    ffn_terms = ffn_weight_term([], 0, 2, [hidden_rows], [grad_gate])
    ffn_terms = ffn_weight_term([ffn_terms], 1, 2, [hidden_rows], [grad_up])
    ffn_terms = after(ffn_terms, *arrived)
    down_grads = lax.psum_scatter(down_terms, "blk", scatter_dimension=0, tiled=True)
    ffn_grads = widen_ffn(
        lax.psum_scatter(ffn_terms, "blk", scatter_dimension=0, tiled=True), down_grads
    )

    grad_parts = exchange_slots(project_mixed_grad(grad_attn, output_all_t, head_size), "head")
    grad_attn_parts = gather_parts(after(grad_attn, *grad_parts[1:]))
    grad_norm, grad_value = attention.backward(grad_parts, *grad_attn_parts[1:])
    grad_attn_rows = join_rows(grad_attn_parts, micro_count)
    grad_norm, grad_value = all_rows(grad_norm), all_rows(grad_value)
    dots, qk_gain_grad = norm_gradients(raw, scales, gain_row, grad_norm)
    dots, gain_grads = sum_token_heads(
        dots, jnp.concatenate([attn_gain_grad, ffn_gain_grad], axis=1)[0]
    )
    mean_dots = dots / model_width
    gain_grads = jnp.concatenate([gain_grads, qk_gain_grad[0]])
    grad_qk = norm_backward(raw, scales, mean_dots, gain_row, grad_norm)
    early_terms = weight_term_slots(
        me, [(grad_attn_rows, all_rows(mixed)), (token_rows, grad_value)], blocks, 0, 2
    )
    hops = [gain_grads]
    for k in range(blocks.bit_length() - 1):
        hops.append(hops[-1] + lax.ppermute(hops[-1], "blk", xor_pairs(blocks, 1 << k)))
    norm_gain_grads = hops[-1][: 2 * model_width]
    qk_gain_grad = hops[-1][2 * model_width :]
    terms = weight_term_slots(
        me, [(token_rows, after(grad_qk, hops[1]))], blocks, 1, 2, early_terms
    )
    slots = project_input_grad(
        after(grad_qk, *terms), grad_value, qkv_full, head_size, micro_count
    )
    pairs = add_cores(terms, hops[-1], *slots)
    input_parts = reduce_parts(slots)
    early_grads, qk_grad = add_chips(pairs, *ffn_grads, input_parts[1])
    output_grad = early_grads[:, :width].T
    input_grad = sum_full(input_parts) + grad_hidden
    return (
        by_micro(output),
        by_micro(input_grad),
        qk_grad[:, :width],
        qk_grad[:, width:],
        early_grads[:, width:],
        output_grad,
        qk_gain_grad[:width],
        qk_gain_grad[width:],
        norm_gain_grads[:model_width],
        *ffn_grads,
        norm_gain_grads[model_width:],
    )


def solution(mesh):
    return jax.shard_map(
        on_device,
        mesh=mesh,
        in_specs=(
            P(None, ("blk", "head"), None),
            P(None, ("blk", "head"), None),
            P(None, ("blk", "head")),
            P(None, ("blk", "head")),
            P("blk", "head"),
            P("blk", "head"),
            P("blk", "head"),
            P("head", "blk"),
            P("head"),
            P("head"),
            P(),
            P("blk", "head"),
            P("blk", "head"),
            P("head", "blk"),
            P(),
        ),
        out_specs=(
            P(None, ("blk", "head"), None),
            P(None, ("blk", "head"), None),
            P("blk", "head"),
            P("blk", "head"),
            P("blk", "head"),
            P("head", "blk"),
            P("head"),
            P("head"),
            P(),
            P("blk", "head"),
            P("blk", "head"),
            P("head", "blk"),
            P(),
        ),
        check_vma=False,
    )
```

```python
import functools
import math

import jax
import jax.numpy as jnp
from jax import lax
from jax.experimental import pallas as pl
from jax.experimental.pallas import tpu as pltpu
from jax.sharding import PartitionSpec as P

HD = 128

epsilon = 1e-06
theta = 500000.0
widest = 512
score_scale = HD ** (-0.5)
hidden_score = -1e30
low = jnp.bfloat16
full = jnp.float32
vmem_grant = 56 * 1024 * 1024


def dot_plain(left_side, right_side):
    return jnp.dot(left_side, right_side, preferred_element_type=full)


def dot_right_t(left_side, right_side):
    return lax.dot_general(
        left_side, right_side, (((1,), (1,)), ((), ())), preferred_element_type=full
    )


def dot_left_t(left_side, right_side):
    return lax.dot_general(
        left_side, right_side, (((0,), (0,)), ((), ())), preferred_element_type=full
    )


def rms_scale(values):
    return lax.rsqrt(jnp.mean(values * values, axis=-1, keepdims=True) + epsilon)


def xor_pairs(size, mask):
    return [(i, i ^ mask) for i in range(size)]


def gather_slots(values, axis):
    size = lax.axis_size(axis)
    return [values] + [lax.ppermute(values, axis, xor_pairs(size, s)) for s in range(1, size)]


def exchange_slots(slots, axis):
    size = lax.axis_size(axis)
    return [slots[0]] + [
        lax.ppermute(slots[s], axis, xor_pairs(size, s)) for s in range(1, size)
    ]


def gather_doubling(values, axis):
    held = values[None]
    step = 1
    while step < lax.axis_size(axis):
        arrived = lax.ppermute(held, axis, xor_pairs(lax.axis_size(axis), step))
        held = jnp.concatenate([held, arrived], axis=0)
        step *= 2
    return held


def sum_doubling(values, axis):
    step = 1
    while step < lax.axis_size(axis):
        values = values + lax.ppermute(values, axis, xor_pairs(lax.axis_size(axis), step))
        step *= 2
    return values


def after(values, *others):
    return lax.optimization_barrier((values, others))[0]


inward = [(0, 1), (3, 2)]
outward = [(1, 0), (2, 3)]
middle = [(1, 2), (2, 1)]


def send_rows(values, pairs):
    return lax.ppermute(values, "head", pairs)


def gather_parts(values):
    if lax.axis_size("head") != 4:
        return gather_slots(values, "head")
    second = send_rows(values, xor_pairs(4, 2))
    first = send_rows(values, xor_pairs(4, 1))
    across = send_rows(values, middle)
    return [values, first, second, across, send_rows(second, outward)]


def layout_of(count):
    return [(0,), (1,), (2,), (3, 4)] if count == 5 else [(s,) for s in range(count)]


def reduce_parts(slots):
    if lax.axis_size("head") != 4:
        return exchange_slots(slots, "head")
    arrived = send_rows(slots[3], inward)
    first = send_rows(slots[1], xor_pairs(4, 1))
    across = send_rows(slots[3], middle)
    passed = (slots[2].astype(full) + arrived.astype(full)).astype(low)
    return [slots[0], first, across, send_rows(passed, xor_pairs(4, 2))]


def exchange_chips(slots):
    size = lax.axis_size("blk")
    return [slots[0]] + [
        lax.ppermute(slots[m], "blk", xor_pairs(size, 2 * m)) for m in range(1, size // 2)
    ]


def exchange_blocks(slots):
    size = len(slots)
    if size != 8:
        return exchange_slots(slots, "blk")
    arrived = {s: lax.ppermute(slots[s], "blk", xor_pairs(size, s)) for s in range(2, size - 1)}
    for s in (size - 1, 1):
        arrived[s] = lax.ppermute(after(slots[s], arrived[2]), "blk", xor_pairs(size, s))
    return [slots[0]] + [arrived[s] for s in range(1, size)]


def swap_cores(values):
    return lax.ppermute(values, "blk", xor_pairs(lax.axis_size("blk"), 1))


def sum_full(arrays):
    return sum(array.astype(full) for array in arrays)


def sum_heads(values, others=None):
    size = lax.axis_size("head")
    count = values.size
    sent = values.reshape(-1)
    if others is not None:
        sent = jnp.concatenate([sent, others])
    total = 0.0
    for s, arrived in enumerate(gather_slots(sent, "head")):
        slots = jnp.split(arrived[:count].reshape(values.shape), size, axis=1)
        ordered = jnp.concatenate([slots[t ^ s] for t in range(size)], axis=1)
        total = total + jnp.concatenate([ordered.reshape(-1), arrived[count:]])
    return total[:count].reshape(values.shape), total[count:]


def rotary_tables(positions):
    half_size = HD // 2
    inverse = theta ** (-2.0 * jnp.arange(half_size, dtype=jnp.int32).astype(full) / HD)
    angles = positions.astype(full)[:, None] * inverse[None, :]
    cosine, sine = jnp.cos(angles), jnp.sin(angles)
    return (
        jnp.concatenate([cosine, cosine], axis=1),
        jnp.concatenate([-sine, sine], axis=1),
    )


def shape_of(shape, dtype):
    return jax.ShapeDtypeStruct(shape, dtype)


def sizes_of(arrays):
    return sum(a.size * a.dtype.itemsize for a in arrays)


def call_whole(body, outs, *args, scalars=1, scratch=(), flops=0):
    return pl.pallas_call(
        body,
        out_shape=outs,
        in_specs=[pl.BlockSpec(memory_space=pltpu.SMEM)] * scalars
        + [pl.BlockSpec(memory_space=pltpu.VMEM)] * (len(args) - scalars),
        out_specs=[pl.BlockSpec(memory_space=pltpu.VMEM)] * len(outs),
        scratch_shapes=list(scratch),
        compiler_params=pltpu.CompilerParams(vmem_limit_bytes=vmem_grant),
        cost_estimate=pl.CostEstimate(
            flops=flops,
            bytes_accessed=sizes_of(args) + sizes_of(outs),
            transcendentals=0,
        ),
    )(*args)


def call_grid(body, steps, outs, in_specs, out_specs, *args, scratch=(), flops=0):
    return pl.pallas_call(
        body,
        grid=(steps,),
        out_shape=outs,
        in_specs=in_specs,
        out_specs=out_specs,
        scratch_shapes=list(scratch),
        compiler_params=pltpu.CompilerParams(vmem_limit_bytes=vmem_grant),
        cost_estimate=pl.CostEstimate(
            flops=flops, bytes_accessed=sizes_of(args) + sizes_of(outs), transcendentals=0
        ),
    )(*args)


def fixed(shape):
    return pl.BlockSpec(shape, lambda i: (0,) * len(shape))


scalar_spec = pl.BlockSpec(memory_space=pltpu.SMEM)


def tile_of(size):
    return math.gcd(size, widest)


def column_tile(rows, tile, first=0):
    return pl.BlockSpec((rows, tile), lambda i: (0, first + i))


def slot_cuts(micro_count, count, rows):
    for s in range(count):
        for m in range(micro_count):
            first = (m * count + s) * rows
            yield s, slice(m * rows, (m + 1) * rows), slice(first, first + rows)


def put_slots(out_refs, values, micro_count):
    rows = out_refs[0].shape[0] // micro_count
    for s, inner, outer in slot_cuts(micro_count, len(out_refs), rows):
        out_refs[s][inner, :] = values[outer].astype(out_refs[s].dtype)


def fill_rows(rows_ref, part_refs, micro_count):
    layout = layout_of(len(part_refs))
    rows = part_refs[0].shape[0] // micro_count
    for s, inner, outer in slot_cuts(micro_count, len(layout), rows):
        rows_ref[outer, :] = functools.reduce(
            jnp.add, [part_refs[part][inner, :] for part in layout[s]]
        )


def sum_slots(refs):
    return sum(ref[...].astype(full) for ref in refs)


def ffn_forward(slots, weights, micro_count):
    n = len(slots)
    local_rows, width = slots[0].shape
    count = len(layout_of(n))
    rows, hidden = count * local_rows, weights.shape[1] // 3
    tile = tile_of(hidden)
    steps = hidden // tile

    def body(*refs):
        wg_ref, wu_ref, wd_ref = refs[n : n + 3]
        rows_ref, gate_ref, up_ref, middle_ref = refs[n + 3 : n + 7]
        out_refs, total = refs[n + 7 : -1], refs[-1]
        step = pl.program_id(0)

        @pl.when(step == 0)
        def _():
            fill_rows(rows_ref, refs[:n], micro_count)

        values = rows_ref[...]
        gate = dot_plain(values, wg_ref[...])
        up = dot_plain(values, wu_ref[...])
        gate_ref[...] = gate.astype(low)
        up_ref[...] = up.astype(low)
        middle = (gate * jax.nn.sigmoid(gate) * up).astype(low)
        middle_ref[...] = middle
        term = dot_right_t(middle, wd_ref[...])

        @pl.when(step == 0)
        def _():
            total[...] = term

        @pl.when(step > 0)
        def _():
            total[...] += term

        @pl.when(step == steps - 1)
        def _():
            put_slots(out_refs, total[...], micro_count)

    results = call_grid(
        body,
        steps,
        [shape_of((rows, width), low)]
        + [shape_of((rows, hidden), low)] * 3
        + [shape_of((local_rows, width), low)] * count,
        [fixed((local_rows, width))] * n + [column_tile(width, tile, k * steps) for k in range(3)],
        [fixed((rows, width))] + [column_tile(rows, tile)] * 3 + [fixed((local_rows, width))] * count,
        *slots,
        weights,
        weights,
        weights,
        scratch=[pltpu.VMEM((rows, width), full)],
        flops=6 * rows * width * hidden,
    )
    return results[:4], results[4:]


def ffn_backward(slots, gate, up, weights, micro_count):
    n = len(slots)
    local_rows, width = slots[0].shape
    rows, hidden = gate.shape
    count = rows // local_rows
    tile = tile_of(hidden)
    steps = hidden // tile

    def body(*refs):
        gate_ref, up_ref, wg_ref, wu_ref, wd_ref = refs[n : n + 5]
        rows_ref, gg_ref, gu_ref = refs[n + 5 : n + 8]
        out_refs, total = refs[n + 8 : -1], refs[-1]
        step = pl.program_id(0)

        @pl.when(step == 0)
        def _():
            fill_rows(rows_ref, refs[:n], micro_count)

        grad_middle = dot_plain(rows_ref[...], wd_ref[...])
        gate_values = gate_ref[...].astype(full)
        sigmoid = jax.nn.sigmoid(gate_values)
        silu = gate_values * sigmoid
        grad_up = (grad_middle * silu).astype(low)
        grad_gate = (
            grad_middle * up_ref[...].astype(full) * (sigmoid + silu * (1.0 - sigmoid))
        ).astype(low)
        gg_ref[...] = grad_gate
        gu_ref[...] = grad_up
        term = dot_right_t(grad_gate, wg_ref[...]) + dot_right_t(grad_up, wu_ref[...])

        @pl.when(step == 0)
        def _():
            total[...] = term

        @pl.when(step > 0)
        def _():
            total[...] += term

        @pl.when(step == steps - 1)
        def _():
            put_slots(out_refs, total[...], micro_count)

    results = call_grid(
        body,
        steps,
        [shape_of((rows, width), low)]
        + [shape_of((rows, hidden), low)] * 2
        + [shape_of((local_rows, width), low)] * count,
        [fixed((local_rows, width))] * n
        + [column_tile(rows, tile)] * 2
        + [column_tile(width, tile, k * steps) for k in range(3)],
        [fixed((rows, width))] + [column_tile(rows, tile)] * 2 + [fixed((local_rows, width))] * count,
        *slots,
        gate,
        up,
        weights,
        weights,
        weights,
        scratch=[pltpu.VMEM((rows, width), full)],
        flops=6 * rows * width * hidden,
    )
    return results[:3], results[3:]


def ffn_weight_term(held, part, parts, lefts, rights):
    n = len(lefts)
    rows, width = lefts[0].shape
    hidden = rights[0].shape[1]
    tile = tile_of(hidden)
    steps = hidden // tile

    def body(*refs):
        out_ref, left_t = refs[-2:]

        @pl.when(pl.program_id(0) == 0)
        def _():
            for m in range(n):
                left_t[:, m * rows : (m + 1) * rows] = jnp.transpose(refs[m][...])

        right = jnp.concatenate([ref[...] for ref in refs[n : 2 * n]], axis=0)
        out_ref[...] = dot_plain(left_t[...], right).astype(low)

    shape = shape_of((width, parts * hidden), low)
    return pl.pallas_call(
        body,
        grid=(steps,),
        out_shape=shape,
        in_specs=[fixed((rows, width))] * n
        + [column_tile(rows, tile)] * n
        + [pl.BlockSpec(memory_space=pl.ANY)] * len(held),
        out_specs=column_tile(width, tile, part * steps),
        scratch_shapes=[pltpu.VMEM((width, n * rows), low)],
        input_output_aliases={2 * n: 0} if held else {},
        compiler_params=pltpu.CompilerParams(vmem_limit_bytes=vmem_grant),
        cost_estimate=pl.CostEstimate(
            flops=2 * n * rows * width * hidden,
            bytes_accessed=sizes_of(lefts) + width * hidden * 2,
            transcendentals=0,
        ),
    )(*lefts, *rights, *held)


def down_weight_term(parts, right, micro_count):
    n = len(parts)
    width = parts[0].shape[1]
    rows, hidden = right.shape
    tile = tile_of(hidden)

    def body(*refs):
        right_ref, out_ref, left, left_t = refs[n:]

        @pl.when(pl.program_id(0) == 0)
        def _():
            fill_rows(left, refs[:n], micro_count)
            left_t[...] = jnp.transpose(left[...])

        out_ref[...] = dot_plain(left_t[...], right_ref[...]).astype(low)

    return call_grid(
        body,
        hidden // tile,
        [shape_of((width, hidden), low)],
        [fixed(part.shape) for part in parts] + [column_tile(rows, tile)],
        [column_tile(width, tile)],
        *parts,
        right,
        scratch=[pltpu.VMEM((rows, width), low), pltpu.VMEM((width, rows), low)],
        flops=2 * rows * width * hidden,
    )[0]


def widen_ffn(grads, down_grads):
    rows, hidden = down_grads.shape

    def body(grad_ref, turned_ref, gate_ref, up_ref, down_ref):
        gate_ref[...] = grad_ref[:, :hidden].astype(full)
        up_ref[...] = grad_ref[:, hidden:].astype(full)
        down_ref[...] = jnp.transpose(turned_ref[...]).astype(full)

    return call_whole(
        body,
        [shape_of((rows, hidden), full)] * 2 + [shape_of((hidden, rows), full)],
        grads,
        down_grads,
        scalars=0,
    )


def after_attention(arrived, tokens, gain):
    n = len(arrived)

    def body(*refs):
        token_ref, gain_ref, hidden_ref, low_ref, hat_ref, scale_ref = refs[n:]
        attn = sum_slots(refs[:n])
        scale = rms_scale(attn)
        hat = attn * scale
        hidden = token_ref[...].astype(full) + hat * gain_ref[...]
        hidden_ref[...] = hidden
        low_ref[...] = hidden.astype(low)
        hat_ref[...] = hat
        scale_ref[...] = scale

    shape = tokens.shape
    return call_whole(
        body,
        [shape_of(shape, full), shape_of(shape, low), shape_of(shape, full), shape_of((shape[0], 1), full)],
        *arrived,
        tokens,
        gain,
        scalars=0,
    )


def after_ffn(arrived, hidden, cotangent, gain):
    n = len(arrived)

    def body(*refs):
        hidden_ref, grad_ref, gain_ref, out_ref, low_ref, gain_grad_ref = refs[n:]
        down = sum_slots(refs[:n])
        scale = rms_scale(down)
        hat = down * scale
        out_ref[...] = (hidden_ref[...] + hat * gain_ref[...]).astype(low)
        grad_out = grad_ref[...].astype(full)
        gain_grad_ref[...] = jnp.sum(grad_out * hat, axis=0, keepdims=True)
        grad = grad_out * gain_ref[...]
        low_ref[...] = (scale * (grad - hat * jnp.mean(grad * hat, axis=1, keepdims=True))).astype(low)

    shape = hidden.shape
    return call_whole(
        body,
        [shape_of(shape, low), shape_of(shape, low), shape_of((1, shape[1]), full)],
        *arrived,
        hidden,
        cotangent,
        gain,
        scalars=0,
    )


def before_attention(arrived, cotangent, hat, scale, gain):
    n = len(arrived)

    def body(*refs):
        grad_ref, hat_ref, scale_ref, gain_ref, hidden_ref, low_ref, gain_grad_ref = refs[n:]
        grad_hidden = sum_slots(refs[:n]) + grad_ref[...].astype(full)
        hidden_ref[...] = grad_hidden
        hat = hat_ref[...]
        gain_grad_ref[...] = jnp.sum(grad_hidden * hat, axis=0, keepdims=True)
        grad = grad_hidden * gain_ref[...]
        low_ref[...] = (
            scale_ref[...] * (grad - hat * jnp.mean(grad * hat, axis=1, keepdims=True))
        ).astype(low)

    shape = hat.shape
    return call_whole(
        body,
        [shape_of(shape, full), shape_of(shape, low), shape_of((1, shape[1]), full)],
        *arrived,
        cotangent,
        hat,
        scale,
        gain,
        scalars=0,
    )


def project_qkv(token_slots, weights, micro_count):
    count = len(token_slots)
    local_rows, width = token_slots[0].shape
    rows, features = len(layout_of(count)) * local_rows, weights.shape[1]
    part = features // 3
    tile = tile_of(part)
    steps = features // tile
    part_steps = part // tile

    def body(*refs):
        weight_ref, rows_ref, raw_ref, square_ref, totals = refs[count:]
        step = pl.program_id(0)

        @pl.when(step == 0)
        def _():
            fill_rows(rows_ref, refs[:count], micro_count)
            totals[...] = jnp.zeros_like(totals)

        raw = dot_plain(rows_ref[...], weight_ref[...])
        raw_ref[...] = raw
        sums = jnp.sum(raw * raw, axis=1, keepdims=True)
        for k in range(2):

            @pl.when(step // part_steps == k)
            def _():
                totals[:, k : k + 1] += sums

        @pl.when(step == steps - 1)
        def _():
            square_ref[...] = jnp.transpose(totals[...])[:2, :]

    return call_grid(
        body,
        steps,
        [shape_of((rows, width), low), shape_of((rows, features), full), shape_of((2, rows), full)],
        [fixed((local_rows, width))] * count + [column_tile(width, tile)],
        [fixed((rows, width)), column_tile(rows, tile), fixed((2, rows))],
        *token_slots,
        weights,
        scratch=[pltpu.VMEM((rows, 128), full)],
        flops=2 * rows * width * features,
    )


def project_output(mixed, weights_t, head_size):
    micro_count, rows, features = mixed.shape
    width = weights_t.shape[0]
    local_rows = micro_count * rows // head_size

    def body(mixed_ref, weight_ref, *out_refs):
        values = dot_right_t(mixed_ref[...].reshape(micro_count * rows, features), weight_ref[...])
        put_slots(out_refs, values, micro_count)

    return call_whole(
        body,
        [shape_of((local_rows, width), low)] * head_size,
        mixed,
        weights_t,
        scalars=0,
        flops=2 * micro_count * rows * width * features,
    )


def project_mixed_grad(grad_rows, weights_t, head_size):
    rows, width = grad_rows.shape
    features = weights_t.shape[1] // head_size

    def body(grad_ref, weight_ref, *out_refs):
        term = dot_plain(grad_ref[...], weight_ref[...]).astype(low)
        for s in range(head_size):

            @pl.when(pl.program_id(0) == s)
            def _():
                out_refs[s][...] = term

    return call_grid(
        body,
        head_size,
        [shape_of((rows, features), low)] * head_size,
        [fixed((rows, width)), column_tile(width, features)],
        [fixed((rows, features))] * head_size,
        grad_rows,
        weights_t,
        flops=2 * rows * width * weights_t.shape[1],
    )


def join_rows(parts, micro_count):
    rows, width = parts[0].shape
    count = len(parts)

    def body(*refs):
        fill_rows(refs[count], refs[:count], micro_count)

    return call_whole(
        body, [shape_of((len(layout_of(count)) * rows, width), low)], *parts, scalars=0
    )[0]


def norm_gradients(raw, scales, gains, grads):
    rows, features = grads.shape
    width = features // 2

    def body(raw_ref, scale_ref, gain_ref, grad_ref, dot_ref, gain_grad_ref, totals):
        totals[...] = jnp.zeros_like(totals)
        for k in range(2):
            cut = slice(k * width, (k + 1) * width)
            terms = grad_ref[:, cut] * (raw_ref[:, cut] * scale_ref[:, k : k + 1])
            gain_grad_ref[:, cut] = jnp.sum(terms, axis=0, keepdims=True)
            totals[:, k : k + 1] = jnp.sum(terms * gain_ref[:, cut], axis=1, keepdims=True)
        dot_ref[...] = jnp.transpose(totals[...])[:2, :]

    return call_whole(
        body,
        [shape_of((2, rows), full), shape_of((1, features), full)],
        raw,
        scales,
        gains,
        grads,
        scalars=0,
        scratch=[pltpu.VMEM((rows, 128), full)],
    )


def norm_backward(raw, scales, dots, gains, grads):
    rows, features = grads.shape
    width = features // 2

    def body(raw_ref, scale_ref, dot_ref, gain_ref, grad_ref, low_ref):
        for k in range(2):
            cut = slice(k * width, (k + 1) * width)
            scale = scale_ref[:, k : k + 1]
            hat = raw_ref[:, cut] * scale
            grad_hat = grad_ref[:, cut] * gain_ref[:, cut]
            low_ref[:, cut] = (scale * (grad_hat - hat * dot_ref[:, k : k + 1])).astype(low)

    return call_whole(
        body, [shape_of((rows, features), low)], raw, scales, dots, gains, grads, scalars=0
    )[0]


def project_input_grad(grad_qk, grad_value, weights, slot_count, micro_count):
    rows, features = grad_value.shape[0], weights.shape[1]
    width = features // 3
    out_width = weights.shape[0]
    local_rows = rows // slot_count
    tile = tile_of(out_width)
    steps = out_width // tile

    def body(qk_ref, value_ref, weight_ref, *out_refs):
        terms = dot_right_t(qk_ref[...], weight_ref[:, : 2 * width])
        terms += dot_right_t(value_ref[...], weight_ref[:, 2 * width :])
        put_slots(out_refs, terms, micro_count)

    return call_grid(
        body,
        steps,
        [shape_of((local_rows, out_width), low)] * slot_count,
        [
            fixed((rows, 2 * width)),
            fixed((rows, width)),
            pl.BlockSpec((tile, features), lambda i: (i, 0)),
        ],
        [column_tile(local_rows, tile)] * slot_count,
        grad_qk,
        grad_value,
        weights,
        flops=2 * rows * features * out_width,
    )


def weight_term_slots(me, pairs, blocks, place, places, held=()):
    n = len(pairs)
    rows, width = pairs[0][0].shape
    sizes = [right.shape[1] for _, right in pairs]
    features = sum(sizes)
    part = width // blocks
    half = blocks // 2

    def body(me_ref, *refs):
        odd_ref, even_ref = refs[-2 - n : -n]
        lefts = refs[-n:]
        step = pl.program_id(0)

        @pl.when(step == 0)
        def _():
            for left_t, left in zip(lefts, refs[:n]):
                left_t[...] = jnp.transpose(left[...])

        slot = jnp.where(step < half, 2 * step + 1, 2 * step - blocks)
        rows_at = pl.multiple_of((me_ref[0] ^ slot) * part, part)
        first = 0
        for left_t, right, size in zip(lefts, refs[n : 2 * n], sizes):
            term = dot_plain(left_t[pl.ds(rows_at, part), :], right[...]).astype(low)
            cut = slice(first, first + size)
            first += size

            @pl.when(step < half)
            def _():
                odd_ref[0, :, cut] = term

            @pl.when(step >= half)
            def _():
                even_ref[0, :, cut] = term

    outs = [shape_of((half, part, places * features), low)] * 2
    return pl.pallas_call(
        body,
        grid=(blocks,),
        out_shape=outs,
        in_specs=[scalar_spec]
        + [fixed((rows, width))] * n
        + [fixed((rows, size)) for size in sizes]
        + [pl.BlockSpec(memory_space=pl.ANY)] * len(held),
        out_specs=[
            pl.BlockSpec((1, part, features), lambda i: (jnp.minimum(i, half - 1), 0, place)),
            pl.BlockSpec((1, part, features), lambda i: (jnp.maximum(i - half, 0), 0, place)),
        ],
        scratch_shapes=[pltpu.VMEM((width, rows), low)] * n,
        input_output_aliases={1 + 2 * n + k: k for k in range(len(held))},
        compiler_params=pltpu.CompilerParams(vmem_limit_bytes=vmem_grant),
        cost_estimate=pl.CostEstimate(
            flops=2 * rows * width * features,
            bytes_accessed=n * rows * width * 2 + rows * features * 2 + width * features * 2,
            transcendentals=0,
        ),
    )(me, *[left for left, _ in pairs], *[right for _, right in pairs], *held)


def add_cores(terms, *others):
    odd, even = terms
    arrived = swap_cores(odd)
    even = after(even, *others) if others else even
    return [even[k].astype(full) + arrived[k].astype(full) for k in range(even.shape[0])]


def add_chips(pairs, *others):
    half = pairs[0].shape[1] // 2
    one, other = slice(0, half), slice(half, 2 * half)
    if len(pairs) != 4:
        slots = exchange_chips([pairs[0]] + [pair.astype(low) for pair in pairs[1:]])
        total = sum_full(slots)
        return total[:, one], total[:, other]
    along = [xor_pairs(8, 2), xor_pairs(8, 4)]
    sent = [
        jnp.stack([pairs[1][:, one], pairs[3][:, one]]).astype(low),
        jnp.stack([pairs[2][:, other], pairs[3][:, other]]).astype(low),
    ]
    arrived = [lax.ppermute(sent[k], "blk", along[k]).astype(full) for k in range(2)]
    sent = [
        (pairs[2][:, one] + arrived[0][1]).astype(low),
        (pairs[1][:, other] + arrived[1][1]).astype(low),
    ]
    sent = after(sent, *others)
    final = [lax.ppermute(sent[k], "blk", along[1 - k]).astype(full) for k in range(2)]
    return (
        pairs[0][:, one] + arrived[0][0] + final[0],
        pairs[0][:, other] + arrived[1][0] + final[1],
    )


def send_views(me, raw, scales, gains, tables, heads_local):
    micro_count, rows = raw.shape[:2]
    blocks = micro_count * heads_local
    width = heads_local * HD

    def body(me_ref, *refs):
        raw_ref, scale_ref, gain_ref, cos_ref, sin_ref = refs[:5]
        out_refs = refs[5:]
        cosine, sine = cos_ref[...], sin_ref[...]
        for s in range(blocks):
            target = me_ref[0] ^ s
            column = pl.multiple_of((target % heads_local) * HD, HD)

            micro = target // heads_local
            for part in range(2):
                feature = pl.multiple_of(part * width + column, HD)
                values = raw_ref[micro, :, pl.ds(feature, HD)]
                values = values * scale_ref[micro, :, part : part + 1]
                values = values * gain_ref[:, pl.ds(feature, HD)]
                turned = values * cosine + pltpu.roll(values, HD // 2, 1) * sine
                out_refs[s][:, part * HD : (part + 1) * HD] = turned.astype(low)
            feature = pl.multiple_of(2 * width + column, HD)
            out_refs[s][:, 2 * HD :] = raw_ref[micro, :, pl.ds(feature, HD)].astype(low)

    return call_whole(
        body,
        [shape_of((rows, 3 * HD), low)] * blocks,
        me,
        raw,
        scales,
        gains,
        *tables,
    )


def masked_scores(k_rows, q_rows, key_seg, query_seg, key_pos=None, query_pos=None):
    scores = dot_right_t(k_rows, q_rows) * score_scale
    allowed = key_seg == query_seg
    if key_pos is not None:
        allowed = (allowed & (key_pos <= query_pos)) | (key_pos == query_pos)
    return jnp.where(allowed, scores, hidden_score)


def attention_forward(me, slots, key_seg, key_pos, query_seg, query_pos):
    blocks = len(slots)
    rows = slots[0].shape[0]
    length = blocks * rows

    def body(me_ref, *refs):
        slot_refs = refs[:blocks]
        ks_ref, kp_ref, qs_ref, qp_ref = refs[blocks : blocks + 4]
        out_refs = refs[blocks + 4 : 2 * blocks + 4]
        mixed_ref, norm_ref, q_all, k_all, v_all = refs[2 * blocks + 4 :]
        for s in range(blocks):
            place = pl.ds(pl.multiple_of((me_ref[0] ^ s) * rows, rows), rows)
            q_all[place, :] = slot_refs[s][:, :HD]
            k_all[place, :] = slot_refs[s][:, HD : 2 * HD]
            v_all[place, :] = slot_refs[s][:, 2 * HD :]
        for i in range(blocks):
            here = slice(i * rows, (i + 1) * rows)
            q_rows = q_all[here, :]
            query_seg_row = qs_ref[:, here]
            parts = [
                masked_scores(
                    k_all[here, :], q_rows, ks_ref[here, :], query_seg_row, kp_ref[here, :], qp_ref[:, here]
                )
            ]
            spans = [here]
            if i > 0:
                past = slice(0, i * rows)
                parts.append(masked_scores(k_all[past, :], q_rows, ks_ref[past, :], query_seg_row))
                spans.append(past)
            top = functools.reduce(
                jnp.maximum, [jnp.max(part, axis=0, keepdims=True) for part in parts]
            )
            total = jnp.zeros((1, rows), full)
            summed = jnp.zeros((HD, rows), full)
            for part, span in zip(parts, spans):
                expanded = jnp.exp(part - top)
                total = total + jnp.sum(expanded, axis=0, keepdims=True)
                summed = summed + dot_left_t(v_all[span, :], expanded.astype(low))
            mixed_ref[here, :] = jnp.transpose(summed / total)
            norm_ref[:, here] = top + jnp.log(total)
        for s in range(blocks):
            place = pl.ds(pl.multiple_of((me_ref[0] ^ s) * rows, rows), rows)
            out_refs[s][...] = mixed_ref[place, :].astype(low)

    return call_whole(
        body,
        [shape_of((rows, HD), low)] * blocks
        + [shape_of((length, HD), full), shape_of((1, length), full)],
        me,
        *slots,
        key_seg,
        key_pos,
        query_seg,
        query_pos,
        scratch=[pltpu.VMEM((length, HD), low)] * 3,
        flops=2 * length * length * HD,
    )


def attention_backward(me, slots, grad_slots, mixed, norm, key_seg, key_pos, query_seg, query_pos):
    blocks = len(slots)
    rows = slots[0].shape[0]
    length = blocks * rows

    def body(me_ref, *refs):
        slot_refs = refs[:blocks]
        grad_refs = refs[blocks : 2 * blocks]
        mixed_ref, norm_ref, ks_ref, kp_ref, qs_ref, qp_ref = refs[2 * blocks : 2 * blocks + 6]
        out_refs = refs[2 * blocks + 6 : 3 * blocks + 6]
        q_all, k_all, v_all, g_all, dq_all, dk_all, dv_all = refs[3 * blocks + 6 :]
        for s in range(blocks):
            place = pl.ds(pl.multiple_of((me_ref[0] ^ s) * rows, rows), rows)
            q_all[place, :] = slot_refs[s][:, :HD]
            k_all[place, :] = slot_refs[s][:, HD : 2 * HD]
            v_all[place, :] = slot_refs[s][:, 2 * HD :]
            g_all[place, :] = grad_refs[s][...]
        for i in range(blocks):
            here = slice(i * rows, (i + 1) * rows)
            q_rows = q_all[here, :]
            g_rows = g_all[here, :]
            query_seg_row = qs_ref[:, here]
            norm_row = norm_ref[:, here]
            delta = jnp.sum(
                jnp.transpose(g_rows.astype(full) * mixed_ref[here, :]), axis=0, keepdims=True
            )
            spans = [here] + ([slice(0, i * rows)] if i > 0 else [])
            grad_query = jnp.zeros((HD, rows), full)
            for n, span in enumerate(spans):
                k_rows = k_all[span, :]
                if n == 0:
                    scores = masked_scores(
                        k_rows, q_rows, ks_ref[span, :], query_seg_row, kp_ref[span, :], qp_ref[:, here]
                    )
                else:
                    scores = masked_scores(k_rows, q_rows, ks_ref[span, :], query_seg_row)
                weights = jnp.exp(scores - norm_row)
                grad_probs = dot_right_t(v_all[span, :], g_rows)
                grad_scores = (weights * (grad_probs - delta)).astype(low)
                key_term = dot_plain(grad_scores, q_rows)
                value_term = dot_plain(weights.astype(low), g_rows)
                if n == 0:
                    dk_all[span, :] = key_term
                    dv_all[span, :] = value_term
                else:
                    dk_all[span, :] += key_term
                    dv_all[span, :] += value_term
                grad_query = grad_query + dot_left_t(k_rows, grad_scores)
            dq_all[here, :] = jnp.transpose(grad_query)
        for s in range(blocks):
            place = pl.ds(pl.multiple_of((me_ref[0] ^ s) * rows, rows), rows)
            out_refs[s][:, :HD] = (dq_all[place, :] * score_scale).astype(low)
            out_refs[s][:, HD : 2 * HD] = (dk_all[place, :] * score_scale).astype(low)
            out_refs[s][:, 2 * HD :] = dv_all[place, :].astype(low)

    return call_whole(
        body,
        [shape_of((rows, 3 * HD), low)] * blocks,
        me,
        *slots,
        *grad_slots,
        mixed,
        norm,
        key_seg,
        key_pos,
        query_seg,
        query_pos,
        scratch=[pltpu.VMEM((length, HD), low)] * 4 + [pltpu.VMEM((length, HD), full)] * 3,
        flops=5 * length * length * HD,
    )


def assemble_mixed(me, slots, micro_count, heads_local):
    rows = slots[0].shape[0]
    blocks = len(slots)

    def body(me_ref, *refs):
        out_ref = refs[blocks]
        for s in range(blocks):
            source = me_ref[0] ^ s
            column = pl.multiple_of((source % heads_local) * HD, HD)
            out_ref[source // heads_local, :, pl.ds(column, HD)] = refs[s][...]

    return call_whole(
        body, [shape_of((micro_count, rows, heads_local * HD), low)], me, *slots
    )[0]


def split_mixed(me, slots, micro_count, heads_local):
    count = len(slots)
    rows = slots[0].shape[0] // micro_count
    blocks = micro_count * heads_local

    def body(me_ref, *refs):
        for t in range(blocks):
            target = me_ref[0] ^ t
            column = pl.multiple_of((target % heads_local) * HD, HD)
            first = pl.multiple_of((target // heads_local) * rows, rows)
            for s in range(count):
                refs[count + t][s * rows : (s + 1) * rows, :] = refs[s][
                    pl.ds(first, rows), pl.ds(column, HD)
                ]

    return call_whole(body, [shape_of((count * rows, HD), low)] * blocks, me, *slots)


def receive_grads(me, slots, tables, micro_count, heads_local):
    rows = slots[0].shape[0]
    blocks = len(slots)
    width = heads_local * HD

    def body(me_ref, *refs):
        cos_ref, sin_ref, norm_ref, value_ref = refs[blocks:]
        cosine, sine = cos_ref[...], sin_ref[...]
        for s in range(blocks):
            source = me_ref[0] ^ s
            micro = source // heads_local
            column = pl.multiple_of((source % heads_local) * HD, HD)
            for part in range(2):
                grads = refs[s][:, part * HD : (part + 1) * HD].astype(full)
                turned = grads * cosine - pltpu.roll(grads, HD // 2, 1) * sine
                norm_ref[micro, :, pl.ds(part * width + column, HD)] = turned
            value_ref[micro, :, pl.ds(column, HD)] = refs[s][:, 2 * HD :]

    return call_whole(
        body,
        [
            shape_of((micro_count, rows, 2 * width), full),
            shape_of((micro_count, rows, width), low),
        ],
        me,
        *slots,
        *tables,
    )


def turn(values, tables):
    return values * tables[0][:, None, :] + jnp.roll(values, HD // 2, axis=-1) * tables[1][:, None, :]


def turn_back(grads, tables):
    return grads * tables[0][:, None, :] - jnp.roll(grads, HD // 2, axis=-1) * tables[1][:, None, :]


def block_scores(query_view, key_rows, query_mark, key_mark):
    scores = score_scale * jnp.einsum(
        "qhd,khd->hqk", query_view, key_rows, preferred_element_type=full
    )
    query_seg, query_pos = query_mark
    key_seg, key_pos = key_mark
    allowed = (query_seg[:, None] == key_seg[None, :]) & (key_pos[None, :] <= query_pos[:, None])
    allowed = allowed | (key_pos[None, :] == query_pos[:, None])
    return jnp.where(allowed[None], scores, hidden_score)


def gathered_forward(query_view, query_mark, stacked):
    rows, heads = query_view.shape[:2]

    def step(running, block):
        key_rows, value_rows, key_seg, key_pos = block
        top, total, summed = running
        scores = block_scores(query_view, key_rows, query_mark, (key_seg, key_pos))
        new_top = jnp.maximum(top, jnp.max(scores, axis=-1))
        shrink = jnp.exp(top - new_top)
        expanded = jnp.where(scores > hidden_score, jnp.exp(scores - new_top[..., None]), 0.0)
        new_total = total * shrink + jnp.sum(expanded, axis=-1)
        new_summed = summed * shrink[..., None] + jnp.einsum(
            "hqk,khd->hqd", expanded.astype(low), value_rows, preferred_element_type=full
        )
        return ((new_top, new_total, new_summed), None)

    start = (
        jnp.full((heads, rows), hidden_score, full),
        jnp.zeros((heads, rows), full),
        jnp.zeros((heads, rows, HD), full),
    )
    top, total, summed = lax.scan(step, start, stacked)[0]
    return jnp.swapaxes(summed / total[..., None], 0, 1), top + jnp.log(total)


def gathered_backward(query_view, grad_view, mixed, norm, query_mark, stacked):
    delta = jnp.sum(grad_view.astype(full) * mixed, axis=2).T

    def step(running, block):
        key_rows, value_rows, key_seg, key_pos = block
        scores = block_scores(query_view, key_rows, query_mark, (key_seg, key_pos))
        weights = jnp.exp(scores - norm[..., None])
        grad_probs = jnp.einsum("qhd,khd->hqk", grad_view, value_rows, preferred_element_type=full)
        grad_scores = (weights * (grad_probs - delta[..., None])).astype(low)
        grad_query = running + jnp.einsum(
            "hqk,khd->qhd", grad_scores, key_rows, preferred_element_type=full
        )
        grad_keys = jnp.einsum("hqk,qhd->khd", grad_scores, query_view, preferred_element_type=full)
        grad_values = jnp.einsum(
            "hqk,qhd->khd", weights.astype(low), grad_view, preferred_element_type=full
        )
        return (
            grad_query,
            jnp.concatenate([grad_keys * score_scale, grad_values], axis=1).astype(low),
        )

    grad_query, key_terms = lax.scan(step, jnp.zeros(query_view.shape, full), stacked)
    return grad_query * score_scale, key_terms


class GatheredAttention:
    def __init__(self, raw, scales, gains, tables, codes, positions):
        blocks, rows = positions.shape
        self.tables, self.rows = tables, rows
        width = gains.shape[1] // 2
        shape = (rows, width // HD, HD)
        self.sets = []
        for m in range(raw.shape[0]):
            values = raw[m]
            views = []
            for part in range(2):
                cut = values[:, part * width : (part + 1) * width]
                normed = cut * scales[m, :, part : part + 1] * gains[:, part * width : (part + 1) * width]
                views.append(turn(normed.reshape(shape), tables).astype(low))
            value_view = values[:, 2 * width :].astype(low).reshape(shape)
            seg_all = (codes[m] // 2).reshape(blocks, rows)
            key_seg = jnp.where(codes[m] % 2 == 1, codes[m] // 2, -1).reshape(blocks, rows)
            place = lax.axis_index("blk")
            mark = tuple(
                lax.dynamic_index_in_dim(mark, place, 0, keepdims=False)
                for mark in (seg_all, positions)
            )
            stacked = (
                lax.all_gather(views[1], "blk"),
                lax.all_gather(value_view, "blk"),
                key_seg,
                positions,
            )
            self.sets.append((views[0], mark, stacked))
        self.slots = [one[2][0] for one in self.sets]

    def forward(self):
        results = [gathered_forward(*one) for one in self.sets]
        self.kept = results
        return jnp.stack(
            [mixed.reshape(self.rows, -1).astype(low) for mixed, norm in results]
        )

    def backward(self, grad_parts, *others):
        grad_mixed = jnp.stack(grad_parts).reshape(len(grad_parts), len(self.sets), -1, grad_parts[0].shape[1])
        grad_mixed = grad_mixed.swapaxes(0, 1).reshape(len(self.sets), self.rows, -1)
        norms, values = [], []
        for m, (view, mark, stacked) in enumerate(self.sets):
            grad_query, terms = gathered_backward(
                view, grad_mixed[m].reshape(view.shape), *self.kept[m], mark, stacked
            )
            own = lax.psum_scatter(terms, "blk", scatter_dimension=0, tiled=False)
            heads = view.shape[1]
            both = [turn_back(grad_query, self.tables)]
            both.append(turn_back(own[:, :heads].astype(full), self.tables))
            norms.append(jnp.concatenate([g.reshape(self.rows, -1) for g in both], axis=1))
            values.append(own[:, heads:].reshape(self.rows, -1))
        return jnp.stack(norms), jnp.stack(values)


class ExchangedAttention:
    def __init__(self, raw, scales, gains, tables, codes, positions):
        self.blocks, self.tables = positions.shape[0], tables
        self.heads = gains.shape[1] // (2 * HD)
        self.micro_count = raw.shape[0]
        place = lax.axis_index("blk")
        self.me = place.astype(jnp.int32).reshape(1)
        self.slots = exchange_blocks(
            send_views(self.me, raw, scales, gains, tables, self.heads)
        )
        codes = lax.dynamic_index_in_dim(codes, place // self.heads, 0, keepdims=False)
        seg_all = codes // 2
        seg_key = jnp.where(codes % 2 == 1, seg_all, -1)
        pos_all = positions.reshape(-1)
        self.marks = (seg_key[:, None], pos_all[:, None], seg_all[None, :], pos_all[None, :])

    def forward(self):
        results = attention_forward(self.me, self.slots, *self.marks)
        self.kept = results[self.blocks :]
        return assemble_mixed(
            self.me,
            exchange_slots(results[: self.blocks], "blk"),
            self.micro_count,
            self.heads,
        )

    def backward(self, grad_parts, *others):
        grad_slots = exchange_slots(
            split_mixed(self.me, grad_parts, self.micro_count, self.heads), "blk"
        )
        self.arrived = grad_slots[1:]
        back_slots = exchange_blocks(
            attention_backward(self.me, self.slots, grad_slots, *self.kept, *self.marks)
        )
        back_slots = after(back_slots, *others)
        return receive_grads(self.me, back_slots, self.tables, self.micro_count, self.heads)


def on_device(
    tokens,
    cotangent,
    segments,
    padding,
    query_weight,
    key_weight,
    value_weight,
    output_weight,
    query_gain,
    key_gain,
    attn_gain,
    gate_weight,
    up_weight,
    down_weight,
    ffn_gain,
):
    micro_count, local_rows, model_width = tokens.shape
    blocks = lax.axis_size("blk")
    head_size = lax.axis_size("head")
    group_rows = local_rows * head_size
    width = query_weight.shape[1]
    heads_local = width // HD
    block_index = lax.axis_index("blk")
    head_index = lax.axis_index("head")
    me = block_index.astype(jnp.int32).reshape(1)
    slot_owner = head_index ^ jnp.arange(head_size, dtype=jnp.int32)
    group_order = (
        slot_owner[:, None] * local_rows + jnp.arange(local_rows, dtype=jnp.int32)[None, :]
    ).reshape(group_rows)
    tables = rotary_tables(block_index * group_rows + group_order)

    def gather_weights(*parts):
        return lax.all_gather(jnp.concatenate(parts, axis=1), "blk", axis=0, tiled=True)

    qkv_full = gather_weights(query_weight, key_weight, value_weight)
    output_full_t = gather_weights(output_weight.T)
    ffn_full = gather_weights(gate_weight, up_weight, down_weight.T)

    def by_micro(values):
        return values.reshape(micro_count, -1, values.shape[-1])

    def all_rows(values):
        return values.reshape(-1, values.shape[-1])

    def sum_token_heads(values, others=None):
        sums, others = sum_heads(values.reshape(2 * micro_count, group_rows), others)
        return sums.reshape(2, micro_count * group_rows).T, others

    token_rows, raw, squares = project_qkv(gather_parts(all_rows(tokens)), qkv_full, micro_count)
    codes = jnp.concatenate(gather_slots(segments * 2 + padding, "head"), axis=1)
    codes = gather_doubling(codes, "blk")
    codes = codes[block_index ^ jnp.arange(blocks, dtype=jnp.int32)].swapaxes(0, 1)

    scales = lax.rsqrt(sum_token_heads(squares)[0] / model_width + epsilon)
    gain_row = jnp.concatenate([query_gain, key_gain])[None, :]
    positions = jnp.arange(blocks, dtype=jnp.int32)[:, None] * group_rows + group_order[None, :]
    exchanged = blocks == micro_count * heads_local and blocks & (blocks - 1) == 0
    attention = (ExchangedAttention if exchanged else GatheredAttention)(
        by_micro(raw), by_micro(scales), gain_row, tables, codes.reshape(micro_count, -1), positions
    )
    output_parts = gather_slots(after(output_weight.T, attention.slots[1]), "head")
    mixed = attention.forward()

    attn_gain, ffn_gain = attn_gain[None, :], ffn_gain[None, :]
    token_own, grad_own = all_rows(tokens), all_rows(cotangent)
    arrived = reduce_parts(project_output(mixed, output_full_t, head_size))
    hidden, hidden_low, attn_hat, attn_scale = after_attention(arrived, token_own, attn_gain)
    (hidden_rows, gate, up, middle_rows), slots = ffn_forward(
        gather_parts(hidden_low), ffn_full, micro_count
    )
    output_all_t = gather_weights(*after(output_parts, gate))
    output, grad_down, ffn_gain_grad = after_ffn(reduce_parts(slots), hidden, grad_own, ffn_gain)
    grad_parts = gather_parts(grad_down)
    down_terms = down_weight_term(grad_parts, middle_rows, micro_count)
    (_, grad_gate, grad_up), slots = ffn_backward(
        grad_parts, after(gate, down_terms), up, ffn_full, micro_count
    )
    arrived = reduce_parts(slots)
    grad_hidden, grad_attn, attn_gain_grad = before_attention(
        arrived, grad_own, attn_hat, attn_scale, attn_gain
    )
    ffn_terms = ffn_weight_term([], 0, 2, [hidden_rows], [grad_gate])
    ffn_terms = ffn_weight_term([ffn_terms], 1, 2, [hidden_rows], [grad_up])
    ffn_terms = after(ffn_terms, *arrived)
    down_grads = lax.psum_scatter(down_terms, "blk", scatter_dimension=0, tiled=True)
    ffn_grads = widen_ffn(
        lax.psum_scatter(ffn_terms, "blk", scatter_dimension=0, tiled=True), down_grads
    )

    grad_parts = exchange_slots(project_mixed_grad(grad_attn, output_all_t, head_size), "head")
    grad_attn_parts = gather_parts(after(grad_attn, *grad_parts[1:]))
    grad_norm, grad_value = attention.backward(grad_parts, *grad_attn_parts[1:])
    grad_attn_rows = join_rows(grad_attn_parts, micro_count)
    grad_norm, grad_value = all_rows(grad_norm), all_rows(grad_value)
    dots, qk_gain_grad = norm_gradients(raw, scales, gain_row, grad_norm)
    dots, gain_grads = sum_token_heads(
        dots, jnp.concatenate([attn_gain_grad, ffn_gain_grad], axis=1)[0]
    )
    mean_dots = dots / model_width
    gain_grads = jnp.concatenate([gain_grads, qk_gain_grad[0]])
    grad_qk = norm_backward(raw, scales, mean_dots, gain_row, grad_norm)
    early_terms = weight_term_slots(
        me, [(grad_attn_rows, all_rows(mixed)), (token_rows, grad_value)], blocks, 0, 2
    )
    hops = [gain_grads]
    for k in range(blocks.bit_length() - 1):
        hops.append(hops[-1] + lax.ppermute(hops[-1], "blk", xor_pairs(blocks, 1 << k)))
    norm_gain_grads = hops[-1][: 2 * model_width]
    qk_gain_grad = hops[-1][2 * model_width :]
    terms = weight_term_slots(
        me, [(token_rows, after(grad_qk, hops[1]))], blocks, 1, 2, early_terms
    )
    slots = project_input_grad(
        after(grad_qk, *terms), grad_value, qkv_full, head_size, micro_count
    )
    pairs = add_cores(terms, hops[-1], *slots)
    input_parts = reduce_parts(slots)
    early_grads, qk_grad = add_chips(pairs, *ffn_grads, input_parts[1])
    output_grad = early_grads[:, :width].T
    input_grad = sum_full(input_parts) + grad_hidden
    return (
        by_micro(output),
        by_micro(input_grad),
        qk_grad[:, :width],
        qk_grad[:, width:],
        early_grads[:, width:],
        output_grad,
        qk_gain_grad[:width],
        qk_gain_grad[width:],
        norm_gain_grads[:model_width],
        *ffn_grads,
        norm_gain_grads[model_width:],
    )


def solution(mesh):
    return jax.shard_map(
        on_device,
        mesh=mesh,
        in_specs=(
            P(None, ("blk", "head"), None),
            P(None, ("blk", "head"), None),
            P(None, ("blk", "head")),
            P(None, ("blk", "head")),
            P("blk", "head"),
            P("blk", "head"),
            P("blk", "head"),
            P("head", "blk"),
            P("head"),
            P("head"),
            P(),
            P("blk", "head"),
            P("blk", "head"),
            P("head", "blk"),
            P(),
        ),
        out_specs=(
            P(None, ("blk", "head"), None),
            P(None, ("blk", "head"), None),
            P("blk", "head"),
            P("blk", "head"),
            P("blk", "head"),
            P("head", "blk"),
            P("head"),
            P("head"),
            P(),
            P("blk", "head"),
            P("blk", "head"),
            P("head", "blk"),
            P(),
        ),
        check_vma=False,
    )
```

```python
import functools
import math

import jax
import jax.numpy as jnp
from jax import lax
from jax.experimental import pallas as pl
from jax.experimental.pallas import tpu as pltpu
from jax.sharding import PartitionSpec as P

HD = 128

epsilon = 1e-06
theta = 500000.0
widest = 512
score_scale = HD ** (-0.5)
hidden_score = -1e30
low = jnp.bfloat16
full = jnp.float32
vmem_grant = 56 * 1024 * 1024


def dot_plain(left_side, right_side):
    return jnp.dot(left_side, right_side, preferred_element_type=full)


def dot_right_t(left_side, right_side):
    return lax.dot_general(
        left_side, right_side, (((1,), (1,)), ((), ())), preferred_element_type=full
    )


def dot_left_t(left_side, right_side):
    return lax.dot_general(
        left_side, right_side, (((0,), (0,)), ((), ())), preferred_element_type=full
    )


def rms_scale(values):
    return lax.rsqrt(jnp.mean(values * values, axis=-1, keepdims=True) + epsilon)


def xor_pairs(size, mask):
    return [(i, i ^ mask) for i in range(size)]


def gather_slots(values, axis):
    size = lax.axis_size(axis)
    return [values] + [lax.ppermute(values, axis, xor_pairs(size, s)) for s in range(1, size)]


def exchange_slots(slots, axis):
    size = lax.axis_size(axis)
    return [slots[0]] + [
        lax.ppermute(slots[s], axis, xor_pairs(size, s)) for s in range(1, size)
    ]


def gather_doubling(values, axis):
    held = values[None]
    step = 1
    while step < lax.axis_size(axis):
        arrived = lax.ppermute(held, axis, xor_pairs(lax.axis_size(axis), step))
        held = jnp.concatenate([held, arrived], axis=0)
        step *= 2
    return held


def sum_doubling(values, axis):
    step = 1
    while step < lax.axis_size(axis):
        values = values + lax.ppermute(values, axis, xor_pairs(lax.axis_size(axis), step))
        step *= 2
    return values


def after(values, *others):
    return lax.optimization_barrier((values, others))[0]


inward = [(0, 1), (3, 2)]
outward = [(1, 0), (2, 3)]
middle = [(1, 2), (2, 1)]


def send_rows(values, pairs):
    return lax.ppermute(values, "head", pairs)


def gather_parts(values):
    if lax.axis_size("head") != 4:
        return gather_slots(values, "head")
    second = send_rows(values, xor_pairs(4, 2))
    first = send_rows(values, xor_pairs(4, 1))
    across = send_rows(values, middle)
    return [values, first, second, across, send_rows(second, outward)]


def layout_of(count):
    return [(0,), (1,), (2,), (3, 4)] if count == 5 else [(s,) for s in range(count)]


def reduce_parts(slots):
    if lax.axis_size("head") != 4:
        return exchange_slots(slots, "head")
    arrived = send_rows(slots[3], inward)
    first = send_rows(slots[1], xor_pairs(4, 1))
    across = send_rows(slots[3], middle)
    passed = (slots[2].astype(full) + arrived.astype(full)).astype(low)
    return [slots[0], first, across, send_rows(passed, xor_pairs(4, 2))]


def exchange_chips(slots):
    size = lax.axis_size("blk")
    return [slots[0]] + [
        lax.ppermute(slots[m], "blk", xor_pairs(size, 2 * m)) for m in range(1, size // 2)
    ]


def exchange_blocks(slots):
    size = len(slots)
    if size != 8:
        return exchange_slots(slots, "blk")
    arrived = {s: lax.ppermute(slots[s], "blk", xor_pairs(size, s)) for s in range(2, size - 1)}
    for s in (size - 1, 1):
        arrived[s] = lax.ppermute(after(slots[s], arrived[2]), "blk", xor_pairs(size, s))
    return [slots[0]] + [arrived[s] for s in range(1, size)]


def swap_cores(values):
    return lax.ppermute(values, "blk", xor_pairs(lax.axis_size("blk"), 1))


def sum_full(arrays):
    return sum(array.astype(full) for array in arrays)


def sum_heads(values, others=None):
    size = lax.axis_size("head")
    count = values.size
    sent = values.reshape(-1)
    if others is not None:
        sent = jnp.concatenate([sent, others])
    total = 0.0
    for s, arrived in enumerate(gather_slots(sent, "head")):
        slots = jnp.split(arrived[:count].reshape(values.shape), size, axis=1)
        ordered = jnp.concatenate([slots[t ^ s] for t in range(size)], axis=1)
        total = total + jnp.concatenate([ordered.reshape(-1), arrived[count:]])
    return total[:count].reshape(values.shape), total[count:]


def rotary_tables(positions):
    half_size = HD // 2
    inverse = theta ** (-2.0 * jnp.arange(half_size, dtype=jnp.int32).astype(full) / HD)
    angles = positions.astype(full)[:, None] * inverse[None, :]
    cosine, sine = jnp.cos(angles), jnp.sin(angles)
    return (
        jnp.concatenate([cosine, cosine], axis=1),
        jnp.concatenate([-sine, sine], axis=1),
    )


def shape_of(shape, dtype):
    return jax.ShapeDtypeStruct(shape, dtype)


def sizes_of(arrays):
    return sum(a.size * a.dtype.itemsize for a in arrays)


def call_whole(body, outs, *args, scalars=1, scratch=(), flops=0):
    return pl.pallas_call(
        body,
        out_shape=outs,
        in_specs=[pl.BlockSpec(memory_space=pltpu.SMEM)] * scalars
        + [pl.BlockSpec(memory_space=pltpu.VMEM)] * (len(args) - scalars),
        out_specs=[pl.BlockSpec(memory_space=pltpu.VMEM)] * len(outs),
        scratch_shapes=list(scratch),
        compiler_params=pltpu.CompilerParams(vmem_limit_bytes=vmem_grant),
        cost_estimate=pl.CostEstimate(
            flops=flops,
            bytes_accessed=sizes_of(args) + sizes_of(outs),
            transcendentals=0,
        ),
    )(*args)


def call_grid(body, steps, outs, in_specs, out_specs, *args, scratch=(), flops=0):
    return pl.pallas_call(
        body,
        grid=(steps,),
        out_shape=outs,
        in_specs=in_specs,
        out_specs=out_specs,
        scratch_shapes=list(scratch),
        compiler_params=pltpu.CompilerParams(vmem_limit_bytes=vmem_grant),
        cost_estimate=pl.CostEstimate(
            flops=flops, bytes_accessed=sizes_of(args) + sizes_of(outs), transcendentals=0
        ),
    )(*args)


def fixed(shape):
    return pl.BlockSpec(shape, lambda i: (0,) * len(shape))


scalar_spec = pl.BlockSpec(memory_space=pltpu.SMEM)


def tile_of(size):
    return math.gcd(size, widest)


def column_tile(rows, tile, first=0):
    return pl.BlockSpec((rows, tile), lambda i: (0, first + i))


def slot_cuts(micro_count, count, rows):
    for s in range(count):
        for m in range(micro_count):
            first = (m * count + s) * rows
            yield s, slice(m * rows, (m + 1) * rows), slice(first, first + rows)


def put_slots(out_refs, values, micro_count):
    rows = out_refs[0].shape[0] // micro_count
    for s, inner, outer in slot_cuts(micro_count, len(out_refs), rows):
        out_refs[s][inner, :] = values[outer].astype(out_refs[s].dtype)


def fill_rows(rows_ref, part_refs, micro_count):
    layout = layout_of(len(part_refs))
    rows = part_refs[0].shape[0] // micro_count
    for s, inner, outer in slot_cuts(micro_count, len(layout), rows):
        rows_ref[outer, :] = functools.reduce(
            jnp.add, [part_refs[part][inner, :] for part in layout[s]]
        )


def sum_slots(refs):
    return sum(ref[...].astype(full) for ref in refs)


def ffn_forward(slots, weights, micro_count):
    n = len(slots)
    local_rows, width = slots[0].shape
    count = len(layout_of(n))
    rows, hidden = count * local_rows, weights.shape[1] // 3
    tile = tile_of(hidden)
    steps = hidden // tile

    def body(*refs):
        wg_ref, wu_ref, wd_ref = refs[n : n + 3]
        rows_ref, gate_ref, up_ref, middle_ref = refs[n + 3 : n + 7]
        out_refs, total = refs[n + 7 : -1], refs[-1]
        step = pl.program_id(0)

        @pl.when(step == 0)
        def _():
            fill_rows(rows_ref, refs[:n], micro_count)

        values = rows_ref[...]
        gate = dot_plain(values, wg_ref[...])
        up = dot_plain(values, wu_ref[...])
        gate_ref[...] = gate.astype(low)
        up_ref[...] = up.astype(low)
        middle = (gate * jax.nn.sigmoid(gate) * up).astype(low)
        middle_ref[...] = middle
        term = dot_right_t(middle, wd_ref[...])

        @pl.when(step == 0)
        def _():
            total[...] = term

        @pl.when(step > 0)
        def _():
            total[...] += term

        @pl.when(step == steps - 1)
        def _():
            put_slots(out_refs, total[...], micro_count)

    results = call_grid(
        body,
        steps,
        [shape_of((rows, width), low)]
        + [shape_of((rows, hidden), low)] * 3
        + [shape_of((local_rows, width), low)] * count,
        [fixed((local_rows, width))] * n + [column_tile(width, tile, k * steps) for k in range(3)],
        [fixed((rows, width))] + [column_tile(rows, tile)] * 3 + [fixed((local_rows, width))] * count,
        *slots,
        weights,
        weights,
        weights,
        scratch=[pltpu.VMEM((rows, width), full)],
        flops=6 * rows * width * hidden,
    )
    return results[:4], results[4:]


def ffn_backward(slots, gate, up, weights, micro_count):
    n = len(slots)
    local_rows, width = slots[0].shape
    rows, hidden = gate.shape
    count = rows // local_rows
    tile = tile_of(hidden)
    steps = hidden // tile

    def body(*refs):
        gate_ref, up_ref, wg_ref, wu_ref, wd_ref = refs[n : n + 5]
        rows_ref, gg_ref, gu_ref = refs[n + 5 : n + 8]
        out_refs, total = refs[n + 8 : -1], refs[-1]
        step = pl.program_id(0)

        @pl.when(step == 0)
        def _():
            fill_rows(rows_ref, refs[:n], micro_count)

        grad_middle = dot_plain(rows_ref[...], wd_ref[...])
        gate_values = gate_ref[...].astype(full)
        sigmoid = jax.nn.sigmoid(gate_values)
        silu = gate_values * sigmoid
        grad_up = (grad_middle * silu).astype(low)
        grad_gate = (
            grad_middle * up_ref[...].astype(full) * (sigmoid + silu * (1.0 - sigmoid))
        ).astype(low)
        gg_ref[...] = grad_gate
        gu_ref[...] = grad_up
        term = dot_right_t(grad_gate, wg_ref[...]) + dot_right_t(grad_up, wu_ref[...])

        @pl.when(step == 0)
        def _():
            total[...] = term

        @pl.when(step > 0)
        def _():
            total[...] += term

        @pl.when(step == steps - 1)
        def _():
            put_slots(out_refs, total[...], micro_count)

    results = call_grid(
        body,
        steps,
        [shape_of((rows, width), low)]
        + [shape_of((rows, hidden), low)] * 2
        + [shape_of((local_rows, width), low)] * count,
        [fixed((local_rows, width))] * n
        + [column_tile(rows, tile)] * 2
        + [column_tile(width, tile, k * steps) for k in range(3)],
        [fixed((rows, width))] + [column_tile(rows, tile)] * 2 + [fixed((local_rows, width))] * count,
        *slots,
        gate,
        up,
        weights,
        weights,
        weights,
        scratch=[pltpu.VMEM((rows, width), full)],
        flops=6 * rows * width * hidden,
    )
    return results[:3], results[3:]


def ffn_weight_term(held, part, parts, lefts, rights):
    n = len(lefts)
    rows, width = lefts[0].shape
    hidden = rights[0].shape[1]
    tile = tile_of(hidden)
    steps = hidden // tile

    def body(*refs):
        out_ref, left_t = refs[-2:]

        @pl.when(pl.program_id(0) == 0)
        def _():
            for m in range(n):
                left_t[:, m * rows : (m + 1) * rows] = jnp.transpose(refs[m][...])

        right = jnp.concatenate([ref[...] for ref in refs[n : 2 * n]], axis=0)
        out_ref[...] = dot_plain(left_t[...], right).astype(low)

    shape = shape_of((width, parts * hidden), low)
    return pl.pallas_call(
        body,
        grid=(steps,),
        out_shape=shape,
        in_specs=[fixed((rows, width))] * n
        + [column_tile(rows, tile)] * n
        + [pl.BlockSpec(memory_space=pl.ANY)] * len(held),
        out_specs=column_tile(width, tile, part * steps),
        scratch_shapes=[pltpu.VMEM((width, n * rows), low)],
        input_output_aliases={2 * n: 0} if held else {},
        compiler_params=pltpu.CompilerParams(vmem_limit_bytes=vmem_grant),
        cost_estimate=pl.CostEstimate(
            flops=2 * n * rows * width * hidden,
            bytes_accessed=sizes_of(lefts) + width * hidden * 2,
            transcendentals=0,
        ),
    )(*lefts, *rights, *held)


def down_weight_term(parts, right, micro_count):
    n = len(parts)
    width = parts[0].shape[1]
    rows, hidden = right.shape
    tile = tile_of(hidden)

    def body(*refs):
        right_ref, out_ref, left, left_t = refs[n:]

        @pl.when(pl.program_id(0) == 0)
        def _():
            fill_rows(left, refs[:n], micro_count)
            left_t[...] = jnp.transpose(left[...])

        out_ref[...] = dot_plain(left_t[...], right_ref[...]).astype(low)

    return call_grid(
        body,
        hidden // tile,
        [shape_of((width, hidden), low)],
        [fixed(part.shape) for part in parts] + [column_tile(rows, tile)],
        [column_tile(width, tile)],
        *parts,
        right,
        scratch=[pltpu.VMEM((rows, width), low), pltpu.VMEM((width, rows), low)],
        flops=2 * rows * width * hidden,
    )[0]


def widen_ffn(grads, down_grads):
    rows, hidden = down_grads.shape

    def body(grad_ref, turned_ref, gate_ref, up_ref, down_ref):
        gate_ref[...] = grad_ref[:, :hidden].astype(full)
        up_ref[...] = grad_ref[:, hidden:].astype(full)
        down_ref[...] = jnp.transpose(turned_ref[...]).astype(full)

    return call_whole(
        body,
        [shape_of((rows, hidden), full)] * 2 + [shape_of((hidden, rows), full)],
        grads,
        down_grads,
        scalars=0,
    )


def after_attention(arrived, tokens, gain):
    n = len(arrived)

    def body(*refs):
        token_ref, gain_ref, hidden_ref, low_ref, hat_ref, scale_ref = refs[n:]
        attn = sum_slots(refs[:n])
        scale = rms_scale(attn)
        hat = attn * scale
        hidden = token_ref[...].astype(full) + hat * gain_ref[...]
        hidden_ref[...] = hidden
        low_ref[...] = hidden.astype(low)
        hat_ref[...] = hat
        scale_ref[...] = scale

    shape = tokens.shape
    return call_whole(
        body,
        [shape_of(shape, full), shape_of(shape, low), shape_of(shape, full), shape_of((shape[0], 1), full)],
        *arrived,
        tokens,
        gain,
        scalars=0,
    )


def after_ffn(arrived, hidden, cotangent, gain):
    n = len(arrived)

    def body(*refs):
        hidden_ref, grad_ref, gain_ref, out_ref, low_ref, gain_grad_ref = refs[n:]
        down = sum_slots(refs[:n])
        scale = rms_scale(down)
        hat = down * scale
        out_ref[...] = (hidden_ref[...] + hat * gain_ref[...]).astype(low)
        grad_out = grad_ref[...].astype(full)
        gain_grad_ref[...] = jnp.sum(grad_out * hat, axis=0, keepdims=True)
        grad = grad_out * gain_ref[...]
        low_ref[...] = (scale * (grad - hat * jnp.mean(grad * hat, axis=1, keepdims=True))).astype(low)

    shape = hidden.shape
    return call_whole(
        body,
        [shape_of(shape, low), shape_of(shape, low), shape_of((1, shape[1]), full)],
        *arrived,
        hidden,
        cotangent,
        gain,
        scalars=0,
    )


def before_attention(arrived, cotangent, hat, scale, gain):
    n = len(arrived)

    def body(*refs):
        grad_ref, hat_ref, scale_ref, gain_ref, hidden_ref, low_ref, gain_grad_ref = refs[n:]
        grad_hidden = sum_slots(refs[:n]) + grad_ref[...].astype(full)
        hidden_ref[...] = grad_hidden
        hat = hat_ref[...]
        gain_grad_ref[...] = jnp.sum(grad_hidden * hat, axis=0, keepdims=True)
        grad = grad_hidden * gain_ref[...]
        low_ref[...] = (
            scale_ref[...] * (grad - hat * jnp.mean(grad * hat, axis=1, keepdims=True))
        ).astype(low)

    shape = hat.shape
    return call_whole(
        body,
        [shape_of(shape, full), shape_of(shape, low), shape_of((1, shape[1]), full)],
        *arrived,
        cotangent,
        hat,
        scale,
        gain,
        scalars=0,
    )


def project_qkv(token_slots, weights, micro_count):
    count = len(token_slots)
    local_rows, width = token_slots[0].shape
    rows, features = len(layout_of(count)) * local_rows, weights.shape[1]
    part = features // 3
    tile = tile_of(part)
    steps = features // tile
    part_steps = part // tile

    def body(*refs):
        weight_ref, rows_ref, raw_ref, square_ref, totals = refs[count:]
        step = pl.program_id(0)

        @pl.when(step == 0)
        def _():
            fill_rows(rows_ref, refs[:count], micro_count)
            totals[...] = jnp.zeros_like(totals)

        raw = dot_plain(rows_ref[...], weight_ref[...])
        raw_ref[...] = raw
        sums = jnp.sum(raw * raw, axis=1, keepdims=True)
        for k in range(2):

            @pl.when(step // part_steps == k)
            def _():
                totals[:, k : k + 1] += sums

        @pl.when(step == steps - 1)
        def _():
            square_ref[...] = jnp.transpose(totals[...])[:2, :]

    return call_grid(
        body,
        steps,
        [shape_of((rows, width), low), shape_of((rows, features), full), shape_of((2, rows), full)],
        [fixed((local_rows, width))] * count + [column_tile(width, tile)],
        [fixed((rows, width)), column_tile(rows, tile), fixed((2, rows))],
        *token_slots,
        weights,
        scratch=[pltpu.VMEM((rows, 128), full)],
        flops=2 * rows * width * features,
    )


def project_output(mixed, weights_t, head_size):
    micro_count, rows, features = mixed.shape
    width = weights_t.shape[0]
    local_rows = micro_count * rows // head_size

    def body(mixed_ref, weight_ref, *out_refs):
        values = dot_right_t(mixed_ref[...].reshape(micro_count * rows, features), weight_ref[...])
        put_slots(out_refs, values, micro_count)

    return call_whole(
        body,
        [shape_of((local_rows, width), low)] * head_size,
        mixed,
        weights_t,
        scalars=0,
        flops=2 * micro_count * rows * width * features,
    )


def project_mixed_grad(grad_rows, weights_t, head_size):
    rows, width = grad_rows.shape
    features = weights_t.shape[1] // head_size

    def body(grad_ref, weight_ref, *out_refs):
        term = dot_plain(grad_ref[...], weight_ref[...]).astype(low)
        for s in range(head_size):

            @pl.when(pl.program_id(0) == s)
            def _():
                out_refs[s][...] = term

    return call_grid(
        body,
        head_size,
        [shape_of((rows, features), low)] * head_size,
        [fixed((rows, width)), column_tile(width, features)],
        [fixed((rows, features))] * head_size,
        grad_rows,
        weights_t,
        flops=2 * rows * width * weights_t.shape[1],
    )


def join_rows(parts, micro_count):
    rows, width = parts[0].shape
    count = len(parts)

    def body(*refs):
        fill_rows(refs[count], refs[:count], micro_count)

    return call_whole(
        body, [shape_of((len(layout_of(count)) * rows, width), low)], *parts, scalars=0
    )[0]


def norm_gradients(raw, scales, gains, grads):
    rows, features = grads.shape
    width = features // 2

    def body(raw_ref, scale_ref, gain_ref, grad_ref, dot_ref, gain_grad_ref, totals):
        totals[...] = jnp.zeros_like(totals)
        for k in range(2):
            cut = slice(k * width, (k + 1) * width)
            terms = grad_ref[:, cut] * (raw_ref[:, cut] * scale_ref[:, k : k + 1])
            gain_grad_ref[:, cut] = jnp.sum(terms, axis=0, keepdims=True)
            totals[:, k : k + 1] = jnp.sum(terms * gain_ref[:, cut], axis=1, keepdims=True)
        dot_ref[...] = jnp.transpose(totals[...])[:2, :]

    return call_whole(
        body,
        [shape_of((2, rows), full), shape_of((1, features), full)],
        raw,
        scales,
        gains,
        grads,
        scalars=0,
        scratch=[pltpu.VMEM((rows, 128), full)],
    )


def norm_backward(raw, scales, dots, gains, grads):
    rows, features = grads.shape
    width = features // 2

    def body(raw_ref, scale_ref, dot_ref, gain_ref, grad_ref, low_ref):
        for k in range(2):
            cut = slice(k * width, (k + 1) * width)
            scale = scale_ref[:, k : k + 1]
            hat = raw_ref[:, cut] * scale
            grad_hat = grad_ref[:, cut] * gain_ref[:, cut]
            low_ref[:, cut] = (scale * (grad_hat - hat * dot_ref[:, k : k + 1])).astype(low)

    return call_whole(
        body, [shape_of((rows, features), low)], raw, scales, dots, gains, grads, scalars=0
    )[0]


def project_input_grad(grad_qk, grad_value, weights, slot_count, micro_count):
    rows, features = grad_value.shape[0], weights.shape[1]
    width = features // 3
    out_width = weights.shape[0]
    local_rows = rows // slot_count
    tile = tile_of(out_width)
    steps = out_width // tile

    def body(qk_ref, value_ref, weight_ref, *out_refs):
        terms = dot_right_t(qk_ref[...], weight_ref[:, : 2 * width])
        terms += dot_right_t(value_ref[...], weight_ref[:, 2 * width :])
        put_slots(out_refs, terms, micro_count)

    return call_grid(
        body,
        steps,
        [shape_of((local_rows, out_width), low)] * slot_count,
        [
            fixed((rows, 2 * width)),
            fixed((rows, width)),
            pl.BlockSpec((tile, features), lambda i: (i, 0)),
        ],
        [column_tile(local_rows, tile)] * slot_count,
        grad_qk,
        grad_value,
        weights,
        flops=2 * rows * features * out_width,
    )


def weight_term_slots(me, pairs, blocks, place, places, held=()):
    n = len(pairs)
    rows, width = pairs[0][0].shape
    sizes = [right.shape[1] for _, right in pairs]
    features = sum(sizes)
    part = width // blocks
    half = blocks // 2

    def body(me_ref, *refs):
        odd_ref, even_ref = refs[-2 - n : -n]
        lefts = refs[-n:]
        step = pl.program_id(0)

        @pl.when(step == 0)
        def _():
            for left_t, left in zip(lefts, refs[:n]):
                left_t[...] = jnp.transpose(left[...])

        slot = jnp.where(step < half, 2 * step + 1, 2 * step - blocks)
        rows_at = pl.multiple_of((me_ref[0] ^ slot) * part, part)
        first = 0
        for left_t, right, size in zip(lefts, refs[n : 2 * n], sizes):
            term = dot_plain(left_t[pl.ds(rows_at, part), :], right[...]).astype(low)
            cut = slice(first, first + size)
            first += size

            @pl.when(step < half)
            def _():
                odd_ref[0, :, cut] = term

            @pl.when(step >= half)
            def _():
                even_ref[0, :, cut] = term

    outs = [shape_of((half, part, places * features), low)] * 2
    return pl.pallas_call(
        body,
        grid=(blocks,),
        out_shape=outs,
        in_specs=[scalar_spec]
        + [fixed((rows, width))] * n
        + [fixed((rows, size)) for size in sizes]
        + [pl.BlockSpec(memory_space=pl.ANY)] * len(held),
        out_specs=[
            pl.BlockSpec((1, part, features), lambda i: (jnp.minimum(i, half - 1), 0, place)),
            pl.BlockSpec((1, part, features), lambda i: (jnp.maximum(i - half, 0), 0, place)),
        ],
        scratch_shapes=[pltpu.VMEM((width, rows), low)] * n,
        input_output_aliases={1 + 2 * n + k: k for k in range(len(held))},
        compiler_params=pltpu.CompilerParams(vmem_limit_bytes=vmem_grant),
        cost_estimate=pl.CostEstimate(
            flops=2 * rows * width * features,
            bytes_accessed=n * rows * width * 2 + rows * features * 2 + width * features * 2,
            transcendentals=0,
        ),
    )(me, *[left for left, _ in pairs], *[right for _, right in pairs], *held)


def add_cores(terms, *others):
    odd, even = terms
    arrived = swap_cores(odd)
    even = after(even, *others) if others else even
    return [even[k].astype(full) + arrived[k].astype(full) for k in range(even.shape[0])]


def add_chips(pairs, *others):
    half = pairs[0].shape[1] // 2
    one, other = slice(0, half), slice(half, 2 * half)
    if len(pairs) != 4:
        slots = exchange_chips([pairs[0]] + [pair.astype(low) for pair in pairs[1:]])
        total = sum_full(slots)
        return total[:, one], total[:, other]
    along = [xor_pairs(8, 2), xor_pairs(8, 4)]
    sent = [
        jnp.stack([pairs[1][:, one], pairs[3][:, one]]).astype(low),
        jnp.stack([pairs[2][:, other], pairs[3][:, other]]).astype(low),
    ]
    arrived = [lax.ppermute(sent[k], "blk", along[k]).astype(full) for k in range(2)]
    sent = [
        (pairs[2][:, one] + arrived[0][1]).astype(low),
        (pairs[1][:, other] + arrived[1][1]).astype(low),
    ]
    sent = after(sent, *others)
    final = [lax.ppermute(sent[k], "blk", along[1 - k]).astype(full) for k in range(2)]
    return (
        pairs[0][:, one] + arrived[0][0] + final[0],
        pairs[0][:, other] + arrived[1][0] + final[1],
    )


def send_views(me, raw, scales, gains, tables, heads_local):
    micro_count, rows = raw.shape[:2]
    blocks = micro_count * heads_local
    width = heads_local * HD

    def body(me_ref, *refs):
        raw_ref, scale_ref, gain_ref, cos_ref, sin_ref = refs[:5]
        out_refs = refs[5:]
        cosine, sine = cos_ref[...], sin_ref[...]
        for s in range(blocks):
            target = me_ref[0] ^ s
            column = pl.multiple_of((target % heads_local) * HD, HD)

            micro = target // heads_local
            for part in range(2):
                feature = pl.multiple_of(part * width + column, HD)
                values = raw_ref[micro, :, pl.ds(feature, HD)]
                values = values * scale_ref[micro, :, part : part + 1]
                values = values * gain_ref[:, pl.ds(feature, HD)]
                turned = values * cosine + pltpu.roll(values, HD // 2, 1) * sine
                out_refs[s][:, part * HD : (part + 1) * HD] = turned.astype(low)
            feature = pl.multiple_of(2 * width + column, HD)
            out_refs[s][:, 2 * HD :] = raw_ref[micro, :, pl.ds(feature, HD)].astype(low)

    return call_whole(
        body,
        [shape_of((rows, 3 * HD), low)] * blocks,
        me,
        raw,
        scales,
        gains,
        *tables,
    )


def masked_scores(k_rows, q_rows, key_seg, query_seg, key_pos=None, query_pos=None):
    scores = dot_right_t(k_rows, q_rows) * score_scale
    allowed = key_seg == query_seg
    if key_pos is not None:
        allowed = (allowed & (key_pos <= query_pos)) | (key_pos == query_pos)
    return jnp.where(allowed, scores, hidden_score)


def attention_forward(me, slots, key_seg, key_pos, query_seg, query_pos):
    blocks = len(slots)
    rows = slots[0].shape[0]
    length = blocks * rows

    def body(me_ref, *refs):
        slot_refs = refs[:blocks]
        ks_ref, kp_ref, qs_ref, qp_ref = refs[blocks : blocks + 4]
        out_refs = refs[blocks + 4 : 2 * blocks + 4]
        mixed_ref, norm_ref, q_all, k_all, v_all = refs[2 * blocks + 4 :]
        for s in range(blocks):
            place = pl.ds(pl.multiple_of((me_ref[0] ^ s) * rows, rows), rows)
            q_all[place, :] = slot_refs[s][:, :HD]
            k_all[place, :] = slot_refs[s][:, HD : 2 * HD]
            v_all[place, :] = slot_refs[s][:, 2 * HD :]
        for i in range(blocks):
            here = slice(i * rows, (i + 1) * rows)
            q_rows = q_all[here, :]
            query_seg_row = qs_ref[:, here]
            parts = [
                masked_scores(
                    k_all[here, :], q_rows, ks_ref[here, :], query_seg_row, kp_ref[here, :], qp_ref[:, here]
                )
            ]
            spans = [here]
            if i > 0:
                past = slice(0, i * rows)
                parts.append(masked_scores(k_all[past, :], q_rows, ks_ref[past, :], query_seg_row))
                spans.append(past)
            top = functools.reduce(
                jnp.maximum, [jnp.max(part, axis=0, keepdims=True) for part in parts]
            )
            total = jnp.zeros((1, rows), full)
            summed = jnp.zeros((HD, rows), full)
            for part, span in zip(parts, spans):
                expanded = jnp.exp(part - top)
                total = total + jnp.sum(expanded, axis=0, keepdims=True)
                summed = summed + dot_left_t(v_all[span, :], expanded.astype(low))
            mixed_ref[here, :] = jnp.transpose(summed / total)
            norm_ref[:, here] = top + jnp.log(total)
        for s in range(blocks):
            place = pl.ds(pl.multiple_of((me_ref[0] ^ s) * rows, rows), rows)
            out_refs[s][...] = mixed_ref[place, :].astype(low)

    return call_whole(
        body,
        [shape_of((rows, HD), low)] * blocks
        + [shape_of((length, HD), full), shape_of((1, length), full)],
        me,
        *slots,
        key_seg,
        key_pos,
        query_seg,
        query_pos,
        scratch=[pltpu.VMEM((length, HD), low)] * 3,
        flops=2 * length * length * HD,
    )


def attention_backward(me, slots, grad_slots, mixed, norm, key_seg, key_pos, query_seg, query_pos):
    blocks = len(slots)
    rows = slots[0].shape[0]
    length = blocks * rows

    def body(me_ref, *refs):
        slot_refs = refs[:blocks]
        grad_refs = refs[blocks : 2 * blocks]
        mixed_ref, norm_ref, ks_ref, kp_ref, qs_ref, qp_ref = refs[2 * blocks : 2 * blocks + 6]
        out_refs = refs[2 * blocks + 6 : 3 * blocks + 6]
        q_all, k_all, v_all, g_all, dq_all, dk_all, dv_all = refs[3 * blocks + 6 :]
        for s in range(blocks):
            place = pl.ds(pl.multiple_of((me_ref[0] ^ s) * rows, rows), rows)
            q_all[place, :] = slot_refs[s][:, :HD]
            k_all[place, :] = slot_refs[s][:, HD : 2 * HD]
            v_all[place, :] = slot_refs[s][:, 2 * HD :]
            g_all[place, :] = grad_refs[s][...]
        for i in range(blocks):
            here = slice(i * rows, (i + 1) * rows)
            q_rows = q_all[here, :]
            g_rows = g_all[here, :]
            query_seg_row = qs_ref[:, here]
            norm_row = norm_ref[:, here]
            delta = jnp.sum(
                jnp.transpose(g_rows.astype(full) * mixed_ref[here, :]), axis=0, keepdims=True
            )
            spans = [here] + ([slice(0, i * rows)] if i > 0 else [])
            grad_query = jnp.zeros((HD, rows), full)
            for n, span in enumerate(spans):
                k_rows = k_all[span, :]
                if n == 0:
                    scores = masked_scores(
                        k_rows, q_rows, ks_ref[span, :], query_seg_row, kp_ref[span, :], qp_ref[:, here]
                    )
                else:
                    scores = masked_scores(k_rows, q_rows, ks_ref[span, :], query_seg_row)
                weights = jnp.exp(scores - norm_row)
                grad_probs = dot_right_t(v_all[span, :], g_rows)
                grad_scores = (weights * (grad_probs - delta)).astype(low)
                key_term = dot_plain(grad_scores, q_rows)
                value_term = dot_plain(weights.astype(low), g_rows)
                if n == 0:
                    dk_all[span, :] = key_term
                    dv_all[span, :] = value_term
                else:
                    dk_all[span, :] += key_term
                    dv_all[span, :] += value_term
                grad_query = grad_query + dot_left_t(k_rows, grad_scores)
            dq_all[here, :] = jnp.transpose(grad_query)
        for s in range(blocks):
            place = pl.ds(pl.multiple_of((me_ref[0] ^ s) * rows, rows), rows)
            out_refs[s][:, :HD] = (dq_all[place, :] * score_scale).astype(low)
            out_refs[s][:, HD : 2 * HD] = (dk_all[place, :] * score_scale).astype(low)
            out_refs[s][:, 2 * HD :] = dv_all[place, :].astype(low)

    return call_whole(
        body,
        [shape_of((rows, 3 * HD), low)] * blocks,
        me,
        *slots,
        *grad_slots,
        mixed,
        norm,
        key_seg,
        key_pos,
        query_seg,
        query_pos,
        scratch=[pltpu.VMEM((length, HD), low)] * 4 + [pltpu.VMEM((length, HD), full)] * 3,
        flops=5 * length * length * HD,
    )


def assemble_mixed(me, slots, micro_count, heads_local):
    rows = slots[0].shape[0]
    blocks = len(slots)

    def body(me_ref, *refs):
        out_ref = refs[blocks]
        for s in range(blocks):
            source = me_ref[0] ^ s
            column = pl.multiple_of((source % heads_local) * HD, HD)
            out_ref[source // heads_local, :, pl.ds(column, HD)] = refs[s][...]

    return call_whole(
        body, [shape_of((micro_count, rows, heads_local * HD), low)], me, *slots
    )[0]


def split_mixed(me, slots, micro_count, heads_local):
    count = len(slots)
    rows = slots[0].shape[0] // micro_count
    blocks = micro_count * heads_local

    def body(me_ref, *refs):
        for t in range(blocks):
            target = me_ref[0] ^ t
            column = pl.multiple_of((target % heads_local) * HD, HD)
            first = pl.multiple_of((target // heads_local) * rows, rows)
            for s in range(count):
                refs[count + t][s * rows : (s + 1) * rows, :] = refs[s][
                    pl.ds(first, rows), pl.ds(column, HD)
                ]

    return call_whole(body, [shape_of((count * rows, HD), low)] * blocks, me, *slots)


def receive_grads(me, slots, tables, micro_count, heads_local):
    rows = slots[0].shape[0]
    blocks = len(slots)
    width = heads_local * HD

    def body(me_ref, *refs):
        cos_ref, sin_ref, norm_ref, value_ref = refs[blocks:]
        cosine, sine = cos_ref[...], sin_ref[...]
        for s in range(blocks):
            source = me_ref[0] ^ s
            micro = source // heads_local
            column = pl.multiple_of((source % heads_local) * HD, HD)
            for part in range(2):
                grads = refs[s][:, part * HD : (part + 1) * HD].astype(full)
                turned = grads * cosine - pltpu.roll(grads, HD // 2, 1) * sine
                norm_ref[micro, :, pl.ds(part * width + column, HD)] = turned
            value_ref[micro, :, pl.ds(column, HD)] = refs[s][:, 2 * HD :]

    return call_whole(
        body,
        [
            shape_of((micro_count, rows, 2 * width), full),
            shape_of((micro_count, rows, width), low),
        ],
        me,
        *slots,
        *tables,
    )


def turn(values, tables):
    return values * tables[0][:, None, :] + jnp.roll(values, HD // 2, axis=-1) * tables[1][:, None, :]


def turn_back(grads, tables):
    return grads * tables[0][:, None, :] - jnp.roll(grads, HD // 2, axis=-1) * tables[1][:, None, :]


def block_scores(query_view, key_rows, query_mark, key_mark):
    scores = score_scale * jnp.einsum(
        "qhd,khd->hqk", query_view, key_rows, preferred_element_type=full
    )
    query_seg, query_pos = query_mark
    key_seg, key_pos = key_mark
    allowed = (query_seg[:, None] == key_seg[None, :]) & (key_pos[None, :] <= query_pos[:, None])
    allowed = allowed | (key_pos[None, :] == query_pos[:, None])
    return jnp.where(allowed[None], scores, hidden_score)


def gathered_forward(query_view, query_mark, stacked):
    rows, heads = query_view.shape[:2]

    def step(running, block):
        key_rows, value_rows, key_seg, key_pos = block
        top, total, summed = running
        scores = block_scores(query_view, key_rows, query_mark, (key_seg, key_pos))
        new_top = jnp.maximum(top, jnp.max(scores, axis=-1))
        shrink = jnp.exp(top - new_top)
        expanded = jnp.where(scores > hidden_score, jnp.exp(scores - new_top[..., None]), 0.0)
        new_total = total * shrink + jnp.sum(expanded, axis=-1)
        new_summed = summed * shrink[..., None] + jnp.einsum(
            "hqk,khd->hqd", expanded.astype(low), value_rows, preferred_element_type=full
        )
        return ((new_top, new_total, new_summed), None)

    start = (
        jnp.full((heads, rows), hidden_score, full),
        jnp.zeros((heads, rows), full),
        jnp.zeros((heads, rows, HD), full),
    )
    top, total, summed = lax.scan(step, start, stacked)[0]
    return jnp.swapaxes(summed / total[..., None], 0, 1), top + jnp.log(total)


def gathered_backward(query_view, grad_view, mixed, norm, query_mark, stacked):
    delta = jnp.sum(grad_view.astype(full) * mixed, axis=2).T

    def step(running, block):
        key_rows, value_rows, key_seg, key_pos = block
        scores = block_scores(query_view, key_rows, query_mark, (key_seg, key_pos))
        weights = jnp.exp(scores - norm[..., None])
        grad_probs = jnp.einsum("qhd,khd->hqk", grad_view, value_rows, preferred_element_type=full)
        grad_scores = (weights * (grad_probs - delta[..., None])).astype(low)
        grad_query = running + jnp.einsum(
            "hqk,khd->qhd", grad_scores, key_rows, preferred_element_type=full
        )
        grad_keys = jnp.einsum("hqk,qhd->khd", grad_scores, query_view, preferred_element_type=full)
        grad_values = jnp.einsum(
            "hqk,qhd->khd", weights.astype(low), grad_view, preferred_element_type=full
        )
        return (
            grad_query,
            jnp.concatenate([grad_keys * score_scale, grad_values], axis=1).astype(low),
        )

    grad_query, key_terms = lax.scan(step, jnp.zeros(query_view.shape, full), stacked)
    return grad_query * score_scale, key_terms


class GatheredAttention:
    def __init__(self, raw, scales, gains, tables, codes, positions):
        blocks, rows = positions.shape
        self.tables, self.rows = tables, rows
        width = gains.shape[1] // 2
        shape = (rows, width // HD, HD)
        self.sets = []
        for m in range(raw.shape[0]):
            values = raw[m]
            views = []
            for part in range(2):
                cut = values[:, part * width : (part + 1) * width]
                normed = cut * scales[m, :, part : part + 1] * gains[:, part * width : (part + 1) * width]
                views.append(turn(normed.reshape(shape), tables).astype(low))
            value_view = values[:, 2 * width :].astype(low).reshape(shape)
            seg_all = (codes[m] // 2).reshape(blocks, rows)
            key_seg = jnp.where(codes[m] % 2 == 1, codes[m] // 2, -1).reshape(blocks, rows)
            place = lax.axis_index("blk")
            mark = tuple(
                lax.dynamic_index_in_dim(mark, place, 0, keepdims=False)
                for mark in (seg_all, positions)
            )
            stacked = (
                lax.all_gather(views[1], "blk"),
                lax.all_gather(value_view, "blk"),
                key_seg,
                positions,
            )
            self.sets.append((views[0], mark, stacked))
        self.slots = [one[2][0] for one in self.sets]

    def forward(self):
        results = [gathered_forward(*one) for one in self.sets]
        self.kept = results
        return jnp.stack(
            [mixed.reshape(self.rows, -1).astype(low) for mixed, norm in results]
        )

    def backward(self, grad_parts, *others):
        grad_mixed = jnp.stack(grad_parts).reshape(len(grad_parts), len(self.sets), -1, grad_parts[0].shape[1])
        grad_mixed = grad_mixed.swapaxes(0, 1).reshape(len(self.sets), self.rows, -1)
        norms, values = [], []
        for m, (view, mark, stacked) in enumerate(self.sets):
            grad_query, terms = gathered_backward(
                view, grad_mixed[m].reshape(view.shape), *self.kept[m], mark, stacked
            )
            own = lax.psum_scatter(terms, "blk", scatter_dimension=0, tiled=False)
            heads = view.shape[1]
            both = [turn_back(grad_query, self.tables)]
            both.append(turn_back(own[:, :heads].astype(full), self.tables))
            norms.append(jnp.concatenate([g.reshape(self.rows, -1) for g in both], axis=1))
            values.append(own[:, heads:].reshape(self.rows, -1))
        return jnp.stack(norms), jnp.stack(values)


class ExchangedAttention:
    def __init__(self, raw, scales, gains, tables, codes, positions):
        self.blocks, self.tables = positions.shape[0], tables
        self.heads = gains.shape[1] // (2 * HD)
        self.micro_count = raw.shape[0]
        place = lax.axis_index("blk")
        self.me = place.astype(jnp.int32).reshape(1)
        self.slots = exchange_blocks(
            send_views(self.me, raw, scales, gains, tables, self.heads)
        )
        codes = lax.dynamic_index_in_dim(codes, place // self.heads, 0, keepdims=False)
        seg_all = codes // 2
        seg_key = jnp.where(codes % 2 == 1, seg_all, -1)
        pos_all = positions.reshape(-1)
        self.marks = (seg_key[:, None], pos_all[:, None], seg_all[None, :], pos_all[None, :])

    def forward(self):
        results = attention_forward(self.me, self.slots, *self.marks)
        self.kept = results[self.blocks :]
        return assemble_mixed(
            self.me,
            exchange_slots(results[: self.blocks], "blk"),
            self.micro_count,
            self.heads,
        )

    def backward(self, grad_parts, *others):
        grad_slots = exchange_blocks(
            split_mixed(self.me, grad_parts, self.micro_count, self.heads)
        )
        self.arrived = grad_slots[1:]
        back_slots = exchange_blocks(
            attention_backward(self.me, self.slots, grad_slots, *self.kept, *self.marks)
        )
        back_slots = after(back_slots, *others)
        return receive_grads(self.me, back_slots, self.tables, self.micro_count, self.heads)


def on_device(
    tokens,
    cotangent,
    segments,
    padding,
    query_weight,
    key_weight,
    value_weight,
    output_weight,
    query_gain,
    key_gain,
    attn_gain,
    gate_weight,
    up_weight,
    down_weight,
    ffn_gain,
):
    micro_count, local_rows, model_width = tokens.shape
    blocks = lax.axis_size("blk")
    head_size = lax.axis_size("head")
    group_rows = local_rows * head_size
    width = query_weight.shape[1]
    heads_local = width // HD
    block_index = lax.axis_index("blk")
    head_index = lax.axis_index("head")
    me = block_index.astype(jnp.int32).reshape(1)
    slot_owner = head_index ^ jnp.arange(head_size, dtype=jnp.int32)
    group_order = (
        slot_owner[:, None] * local_rows + jnp.arange(local_rows, dtype=jnp.int32)[None, :]
    ).reshape(group_rows)
    tables = rotary_tables(block_index * group_rows + group_order)

    def gather_weights(*parts):
        return lax.all_gather(jnp.concatenate(parts, axis=1), "blk", axis=0, tiled=True)

    qkv_full = gather_weights(query_weight, key_weight, value_weight)
    output_full_t = gather_weights(output_weight.T)
    ffn_full = gather_weights(gate_weight, up_weight, down_weight.T)

    def by_micro(values):
        return values.reshape(micro_count, -1, values.shape[-1])

    def all_rows(values):
        return values.reshape(-1, values.shape[-1])

    def sum_token_heads(values, others=None):
        sums, others = sum_heads(values.reshape(2 * micro_count, group_rows), others)
        return sums.reshape(2, micro_count * group_rows).T, others

    token_rows, raw, squares = project_qkv(gather_parts(all_rows(tokens)), qkv_full, micro_count)
    codes = jnp.concatenate(gather_slots(segments * 2 + padding, "head"), axis=1)
    codes = gather_doubling(codes, "blk")
    codes = codes[block_index ^ jnp.arange(blocks, dtype=jnp.int32)].swapaxes(0, 1)

    scales = lax.rsqrt(sum_token_heads(squares)[0] / model_width + epsilon)
    gain_row = jnp.concatenate([query_gain, key_gain])[None, :]
    positions = jnp.arange(blocks, dtype=jnp.int32)[:, None] * group_rows + group_order[None, :]
    exchanged = blocks == micro_count * heads_local and blocks & (blocks - 1) == 0
    attention = (ExchangedAttention if exchanged else GatheredAttention)(
        by_micro(raw), by_micro(scales), gain_row, tables, codes.reshape(micro_count, -1), positions
    )
    output_parts = gather_slots(after(output_weight.T, attention.slots[1]), "head")
    mixed = attention.forward()

    attn_gain, ffn_gain = attn_gain[None, :], ffn_gain[None, :]
    token_own, grad_own = all_rows(tokens), all_rows(cotangent)
    arrived = reduce_parts(project_output(mixed, output_full_t, head_size))
    hidden, hidden_low, attn_hat, attn_scale = after_attention(arrived, token_own, attn_gain)
    (hidden_rows, gate, up, middle_rows), slots = ffn_forward(
        gather_parts(hidden_low), ffn_full, micro_count
    )
    output_all_t = gather_weights(*after(output_parts, gate))
    output, grad_down, ffn_gain_grad = after_ffn(reduce_parts(slots), hidden, grad_own, ffn_gain)
    grad_parts = gather_parts(grad_down)
    down_terms = down_weight_term(grad_parts, middle_rows, micro_count)
    (_, grad_gate, grad_up), slots = ffn_backward(
        grad_parts, after(gate, down_terms), up, ffn_full, micro_count
    )
    arrived = reduce_parts(slots)
    grad_hidden, grad_attn, attn_gain_grad = before_attention(
        arrived, grad_own, attn_hat, attn_scale, attn_gain
    )
    ffn_terms = ffn_weight_term([], 0, 2, [hidden_rows], [grad_gate])
    ffn_terms = ffn_weight_term([ffn_terms], 1, 2, [hidden_rows], [grad_up])
    ffn_terms = after(ffn_terms, *arrived)
    down_grads = lax.psum_scatter(down_terms, "blk", scatter_dimension=0, tiled=True)
    ffn_grads = widen_ffn(
        lax.psum_scatter(ffn_terms, "blk", scatter_dimension=0, tiled=True), down_grads
    )

    grad_parts = exchange_slots(project_mixed_grad(grad_attn, output_all_t, head_size), "head")
    grad_attn_parts = gather_parts(after(grad_attn, *grad_parts[1:]))
    grad_norm, grad_value = attention.backward(grad_parts, *grad_attn_parts[1:])
    grad_attn_rows = join_rows(grad_attn_parts, micro_count)
    grad_norm, grad_value = all_rows(grad_norm), all_rows(grad_value)
    dots, qk_gain_grad = norm_gradients(raw, scales, gain_row, grad_norm)
    dots, gain_grads = sum_token_heads(
        dots, jnp.concatenate([attn_gain_grad, ffn_gain_grad], axis=1)[0]
    )
    mean_dots = dots / model_width
    gain_grads = jnp.concatenate([gain_grads, qk_gain_grad[0]])
    grad_qk = norm_backward(raw, scales, mean_dots, gain_row, grad_norm)
    early_terms = weight_term_slots(
        me, [(grad_attn_rows, all_rows(mixed)), (token_rows, grad_value)], blocks, 0, 2
    )
    hops = [gain_grads]
    for k in range(blocks.bit_length() - 1):
        hops.append(hops[-1] + lax.ppermute(hops[-1], "blk", xor_pairs(blocks, 1 << k)))
    norm_gain_grads = hops[-1][: 2 * model_width]
    qk_gain_grad = hops[-1][2 * model_width :]
    terms = weight_term_slots(
        me, [(token_rows, after(grad_qk, hops[1]))], blocks, 1, 2, early_terms
    )
    slots = project_input_grad(
        after(grad_qk, *terms), grad_value, qkv_full, head_size, micro_count
    )
    pairs = add_cores(terms, hops[-1], *slots)
    input_parts = reduce_parts(slots)
    early_grads, qk_grad = add_chips(pairs, *ffn_grads, input_parts[1])
    output_grad = early_grads[:, :width].T
    input_grad = sum_full(input_parts) + grad_hidden
    return (
        by_micro(output),
        by_micro(input_grad),
        qk_grad[:, :width],
        qk_grad[:, width:],
        early_grads[:, width:],
        output_grad,
        qk_gain_grad[:width],
        qk_gain_grad[width:],
        norm_gain_grads[:model_width],
        *ffn_grads,
        norm_gain_grads[model_width:],
    )


def solution(mesh):
    return jax.shard_map(
        on_device,
        mesh=mesh,
        in_specs=(
            P(None, ("blk", "head"), None),
            P(None, ("blk", "head"), None),
            P(None, ("blk", "head")),
            P(None, ("blk", "head")),
            P("blk", "head"),
            P("blk", "head"),
            P("blk", "head"),
            P("head", "blk"),
            P("head"),
            P("head"),
            P(),
            P("blk", "head"),
            P("blk", "head"),
            P("head", "blk"),
            P(),
        ),
        out_specs=(
            P(None, ("blk", "head"), None),
            P(None, ("blk", "head"), None),
            P("blk", "head"),
            P("blk", "head"),
            P("blk", "head"),
            P("head", "blk"),
            P("head"),
            P("head"),
            P(),
            P("blk", "head"),
            P("blk", "head"),
            P("head", "blk"),
            P(),
        ),
        check_vma=False,
    )
```
